32 devices in a mesh: segment: 2 (over core), dp: 8 (over z, y), tensor: 2 (over x).
Axes of the slice: x: 2, y: 2, z: 4, core: 2. Of those that a mesh axis runs over, the one named last changes fastest.
Arguments:
- layer_input: bfloat16 [2, 8, 128, 768], P(None, 'dp'), may hold values from -8 to 8
- doc_lengths: int32 [2, 8, 3], P(None, 'dp'), may hold values from 1 to 4, 8 in all within a row
- norm_gains: float32 [2, 2, 768], P('segment'), may hold values from 0.5 to 1.5
- mixing: bfloat16 [2, 768, 4, 768], P('segment', None, None, 'tensor'), may hold values from -0.21875 to 0.21875
- rate_weight: bfloat16 [2, 768, 12], P('segment', None, 'tensor'), may hold values from -0.21875 to 0.21875
- rate_offset: float32 [2, 12], P('segment', 'tensor'), may hold values from -1 to 1
- expand: float32 [2, 12, 64, 256], P('segment', 'tensor'), may hold values from -0.75 to 0.75
- hidden_bias: float32 [2, 12, 256], P('segment', 'tensor'), may hold values from -3 to 3
- contract: float32 [2, 12, 256, 64], P('segment', 'tensor'), may hold values from -0.375 to 0.375
- result_bias: float32 [2, 12, 64], P('segment', 'tensor'), may hold values from -3 to 3
- head_gains: float32 [2, 2, 12, 64], P('segment', None, 'tensor'), may hold values from 0.5 to 1.5
- head_shift: float32 [2, 12, 64], P('segment', 'tensor'), may hold values from -2 to 2
- output_proj: bfloat16 [2, 768, 768], P('segment', 'tensor'), may hold values from -0.4375 to 0.4375
- swiglu: bfloat16 [2, 768, 2, 2048], P('segment', None, None, 'tensor'), may hold values from -0.21875 to 0.21875
- down_proj: bfloat16 [2, 2048, 768], P('segment', 'tensor'), may hold values from -0.25 to 0.25
- cotangent: bfloat16 [2, 8, 128, 768], P(None, 'dp'), may hold values from -6 to 6
Outputs:
- layer_output: bfloat16 [2, 2, 8, 128, 768], P('segment', None, 'dp')
- input_grads: float32 [2, 2, 8, 128, 768], P('segment', None, 'dp')
- grad_gains: float32 [2, 2, 768], P('segment')
- grad_mixing: float32 [2, 768, 4, 768], P('segment', None, None, 'tensor')
- grad_rate: float32 [2, 768, 12], P('segment', None, 'tensor')
- grad_offset: float32 [2, 12], P('segment', 'tensor')
- grad_expand: float32 [2, 12, 64, 256], P('segment', 'tensor')
- grad_hidden: float32 [2, 12, 256], P('segment', 'tensor')
- grad_contract: float32 [2, 12, 256, 64], P('segment', 'tensor')
- grad_result: float32 [2, 12, 64], P('segment', 'tensor')
- grad_heads: float32 [2, 2, 12, 64], P('segment', None, 'tensor')
- grad_shift: float32 [2, 12, 64], P('segment', 'tensor')
- grad_output: float32 [2, 768, 768], P('segment', 'tensor')
- grad_swiglu: float32 [2, 768, 2, 2048], P('segment', None, None, 'tensor')
- grad_down: float32 [2, 2048, 768], P('segment', 'tensor')
- rate_stats: float32 [2, 2, 8, 2, 12], P('segment')
The draws below stay inside these ranges and needn't reach their ends.
Inputs may be any that keep to these rules, and one draw needn't show every extreme that they name: `doc_lengths`: lengths are counted in inner blocks of 16 tokens; the 3 lengths of a row sum to 8, and in every row the longest is exactly 4.
All inputs are finite; a program needn't handle non-finite values.
Results may differ from the reference program's by a relative error of at most 0.023.
Values may be sent and summed in bfloat16 or wider, within the bound.
No kernel may reach another device: no remote copies, remote signals or barrier semaphores. Data moves between devices by JAX's collectives and lax.ppermute only.
A program may use at most 192 MiB of HBM per device.

```python
import math
from functools import partial
import jax
import jax.numpy as jnp
import numpy as np
from jax import lax

D = 768
HEADS = 12
HD = 64
INNER = 256
FF = 2048
MBT = 16
LEN = 128
MB = 2
DOCS = 3
LAYERS = 2
BATCH = 8


def draw_layer_input(key, part):
    key = jax.random.fold_in(key, 11)
    noise_key, row_key = jax.random.split(key)
    noise = jax.random.normal(noise_key, (MB, BATCH, LEN, D), jnp.float32)
    row_part = 1.5 * jax.random.normal(row_key, (MB, BATCH, 1, D), jnp.float32)
    return jnp.clip(noise + row_part, -8.0, 8.0).astype(jnp.bfloat16)


def block_levels(rng, dims, cuts, low, largest):
    def one(dim, blocks):
        draws = jax.random.uniform(jax.random.fold_in(jax.random.fold_in(rng, 6), dim), (blocks,), jnp.float32, low / len(cuts), largest / len(cuts))
        return jnp.repeat(jnp.exp(draws), dims[dim] // blocks).reshape((-1,) + (1,) * (len(dims) - dim - 1))

    level = one(*cuts[0])
    for cut in cuts[1:]:
        level = level * one(*cut)
    return level


def split_up(amount, total, bound, skew):
    portions = [(1 << 20) // math.isqrt(rank ** skew) + 1 for rank in range(2, amount + 1)]
    rest, counts = total - bound - (amount - 1), [1] * (amount - 1)
    while rest > 0:
        movable = [i for i in range(amount - 1) if counts[i] < bound]
        whole, budget = sum([portions[i] for i in movable]), rest
        for i in movable:
            more = min(bound - counts[i], max(1, budget * portions[i] // whole), rest)
            counts[i] = counts[i] + more
            rest = rest - more
    return np.array([bound] + counts)


def ragged(rng, amount, total, reach, lean):
    if amount == 2:
        one = jax.random.randint(rng, (), max(1, total - reach), min(reach, total - 1) + 1)
        return jnp.stack([one, total - one])
    sizes = jnp.asarray(split_up(amount, total, reach, lean), jnp.int32)
    twos = (amount - 1) // 2
    giver, sink = sizes[1:1 + 2 * twos:2], sizes[2:2 + 2 * twos:2]
    room = jnp.minimum(giver - 1, reach - sink)
    passed = jax.random.randint(jax.random.fold_in(rng, 1), (twos,), 0, 1 << 20) % (room + 1)
    sizes = sizes.at[1:1 + 2 * twos:2].set(giver - passed).at[2:2 + 2 * twos:2].set(sink + passed)
    return sizes[jax.random.permutation(jax.random.fold_in(rng, 2), amount)]


def scatter_about(stream_key, shape, scale, reach, shards=(), kind=jnp.bfloat16):
    drawn = scale * jax.random.normal(stream_key, shape, jnp.float32)
    if shards:
        drawn = drawn * block_levels(stream_key, shape, shards, -0.22, 0.18)
    return jnp.clip(drawn, -reach, reach).astype(kind)


def setup_inputs(seed: int = 0) -> dict:
    keys = jax.random.split(jax.random.key(seed), 17)
    layer_input = draw_layer_input(jax.random.fold_in(keys[16], 71), 0)
    doc_lengths = jax.vmap(lambda own: ragged(own, DOCS, LEN // MBT, LEN // (2 * MBT), 0))(jax.random.split(keys[1], MB * BATCH)).reshape((MB, BATCH, DOCS)).astype(jnp.int32)
    norm_gains = jnp.clip(1.0 + 0.1 * jax.random.normal(keys[2], (LAYERS, 2, D), jnp.float32), 0.5, 1.5)
    mixing = scatter_about(keys[3], (LAYERS, D, 4, HEADS * HD), D ** -0.5, 0.21875, ((0, 2), (3, 2)))
    rate_weight = scatter_about(keys[4], (LAYERS, D, HEADS), D ** -0.5, 0.21875, ((0, 2), (2, 2)))
    rate_offset = jnp.clip(jax.random.uniform(keys[5], (LAYERS, HEADS), jnp.float32, -1.0, 1.0) * block_levels(keys[5], (LAYERS, HEADS), ((0, 2), (1, 2)), -0.4, 0.0), -1.0, 1.0)
    expand = scatter_about(keys[6], (LAYERS, HEADS, HD, INNER), HD ** -0.5, 0.75, ((0, 2), (1, 2)), jnp.float32)
    hidden_bias = scatter_about(keys[7], (LAYERS, HEADS, INNER), 0.5, 3.0, ((0, 2), (1, 2)), jnp.float32)
    contract = scatter_about(keys[8], (LAYERS, HEADS, INNER, HD), INNER ** -0.5, 0.375, ((0, 2), (1, 2)), jnp.float32)
    result_bias = scatter_about(keys[9], (LAYERS, HEADS, HD), 0.5, 3.0, ((0, 2), (1, 2)), jnp.float32)
    head_gains = jnp.clip(1.0 + 0.1 * jax.random.normal(keys[10], (LAYERS, 2, HEADS, HD), jnp.float32), 0.5, 1.5)
    head_shift = scatter_about(keys[11], (LAYERS, HEADS, HD), 0.3, 2.0, ((0, 2), (1, 2)), jnp.float32)
    output_proj = scatter_about(keys[12], (LAYERS, HEADS * HD, D), (HEADS * HD // 4) ** -0.5, 0.4375, ((0, 2), (1, 2)))
    swiglu = scatter_about(keys[13], (LAYERS, D, 2, FF), D ** -0.5, 0.21875, ((0, 2), (3, 2)))
    down_proj = scatter_about(keys[14], (LAYERS, FF, D), (FF // 4) ** -0.5, 0.25, ((0, 2), (1, 2)))
    cotangent = scatter_about(keys[15], (MB, BATCH, LEN, D), 1.0, 6.0, ((1, 8),))
    return {"layer_input": layer_input, "doc_lengths": doc_lengths, "norm_gains": norm_gains, "mixing": mixing, "rate_weight": rate_weight, "rate_offset": rate_offset, "expand": expand, "hidden_bias": hidden_bias, "contract": contract, "result_bias": result_bias, "head_gains": head_gains, "head_shift": head_shift, "output_proj": output_proj, "swiglu": swiglu, "down_proj": down_proj, "cotangent": cotangent}


@jax.custom_vjp
def low(v):
    return lax.optimization_barrier(v.astype(jnp.bfloat16)).astype(jnp.float32)

@jax.custom_vjp
def low_back(v):
    return v

def low_keep(v):
    return (low(v), None)

def low_pass(kept, grad):
    return (grad,)

def back_keep(v):
    return (v, None)

def back_low(kept, grad):
    return (low(grad),)
low.defvjp(low_keep, low_pass)
low_back.defvjp(back_keep, back_low)
epsilon = 1e-06
rate_scale = 0.125
highest = lax.Precision.HIGHEST
slope_const = 0.7978845608028654

def exact_dot(left, right):
    return jnp.dot(left, right, precision=highest)

def rms_scale(values, gain):
    return values * lax.rsqrt(lax.optimization_barrier(jnp.mean(values * values, axis=-1, keepdims=True)) + epsilon) * gain

def center_scale(values, gain, shift_in):
    centered = values - lax.optimization_barrier(jnp.mean(values, axis=-1, keepdims=True))
    return centered * lax.rsqrt(lax.optimization_barrier(jnp.mean(centered * centered, axis=-1, keepdims=True)) + epsilon) * gain + shift_in

def gelu_tanh(point):
    return jax.nn.gelu(point, approximate=True)

def gelu_slope(point):
    tangent = jnp.tanh(slope_const * (point + 0.044715 * point * point * point))
    return 0.5 * (1.0 + tangent) + 0.5 * point * (1.0 - tangent * tangent) * slope_const * (1.0 + 0.134145 * point * point)

def ttt_head(queries, keys_in, values_in, rates, resets, first_w, first_b, second_w, second_b, gain, shift_in):
    blocks = resets.shape[0]
    block_len = queries.shape[0] // blocks
    positions = jnp.arange(block_len)
    causal = (positions[:, None] >= positions[None, :]).astype(jnp.float32)
    weighting = causal / (positions[:, None] + 1).astype(jnp.float32)
    initial = (first_w, first_b, second_w, second_b)

    def block_update(state, inputs):
        query_blk, key_blk, value_blk, rate_blk, flag = inputs
        state = jax.tree.map(lambda now, start: flag * start + (1.0 - flag) * now, state, initial)
        up_w, up_b, down_w, down_b = state
        pre_one = exact_dot(key_blk, up_w) + up_b
        act_one = gelu_tanh(pre_one)
        pre_two = exact_dot(act_one, down_w) + down_b
        centered = pre_two - lax.optimization_barrier(jnp.mean(pre_two, axis=-1, keepdims=True))
        inv_std = lax.rsqrt(lax.optimization_barrier(jnp.mean(centered * centered, axis=-1, keepdims=True)) + epsilon)
        normed = centered * inv_std
        misfit = (normed * gain + shift_in - (value_blk - key_blk)) * gain
        grad_two = (misfit - lax.optimization_barrier(jnp.mean(misfit, axis=-1, keepdims=True)) - normed * lax.optimization_barrier(jnp.mean(misfit * normed, axis=-1, keepdims=True))) * inv_std
        grad_one = exact_dot(grad_two, down_w.T) * gelu_slope(pre_one)
        coeff = weighting * rate_blk[None, :]
        new_one = exact_dot(query_blk, up_w) + up_b - exact_dot(coeff * (exact_dot(query_blk, key_blk.T) + 1.0), grad_one)
        new_act = gelu_tanh(new_one)
        new_two = exact_dot(new_act, down_w) + down_b - exact_dot(coeff * (exact_dot(new_act, act_one.T) + 1.0), grad_two)
        out_blk = query_blk + center_scale(new_two, gain, shift_in)
        last_rate = (rate_blk / block_len)[:, None]
        step_one = last_rate * grad_one
        step_two = last_rate * grad_two
        state = (up_w - exact_dot(key_blk.T, step_one), up_b - lax.optimization_barrier(jnp.sum(step_one, axis=0)), down_w - exact_dot(act_one.T, step_two), down_b - lax.optimization_barrier(jnp.sum(step_two, axis=0)))
        return (state, out_blk)

    def to_blocks(array):
        return array.reshape((blocks, block_len) + array.shape[1:])
    _, outputs = lax.scan(jax.checkpoint(block_update), initial, (to_blocks(queries), to_blocks(keys_in), to_blocks(values_in), to_blocks(rates), resets))
    return outputs.reshape(queries.shape)

def mixer(projected, logits, resets, first_w, first_b, second_w, second_b, gains_in, shift_in):
    row_count, length, _, width_all = projected.shape
    head_count = logits.shape[-1]
    sections = projected.reshape(row_count, length, 4, head_count, width_all // head_count)
    rates = jax.nn.sigmoid(logits) * rate_scale
    per_head = jax.vmap(ttt_head, in_axes=(1, 1, 1, 1, None, 0, 0, 0, 0, 0, 0), out_axes=1)
    per_row = jax.vmap(per_head, in_axes=(0, 0, 0, 0, 0, None, None, None, None, None, None))
    inner_out = per_row(sections[:, :, 0], sections[:, :, 1], sections[:, :, 2], rates, resets, first_w, first_b, second_w, second_b, gains_in[0], shift_in)
    mixed = gelu_tanh(sections[:, :, 3]) * rms_scale(inner_out, gains_in[1])
    return mixed.reshape(row_count, length, width_all)

def rate_summary(logits):
    probs = jax.nn.sigmoid(logits)
    return jnp.stack([lax.optimization_barrier(jnp.mean(probs, axis=1)), lax.optimization_barrier(jnp.max(probs, axis=1))], axis=1)

def reset_flags(lengths, blocks):
    starts = jnp.cumsum(lengths, axis=-1) - lengths
    marks = jnp.arange(blocks, dtype=jnp.int32)
    hits = (starts[..., :, None] == marks).astype(jnp.float32)
    return lax.optimization_barrier(jnp.sum(hits, axis=-2))

def layer(source, resets, params):
    gain_pair, mix_w, rate_w, offset_row, first_w, first_b, second_w, second_b, gains_in, shift_in, out_w, wide_w, down_w = params
    x_one = low(rms_scale(source, gain_pair[0]))
    projected = low_back(jnp.einsum('rld,dcn->rlcn', x_one, mix_w, precision=highest))
    logits = low_back(jnp.einsum('rld,dh->rlh', x_one, rate_w, precision=highest)) + offset_row
    mixed = low(mixer(projected, logits, resets, first_w, first_b, second_w, second_b, gains_in, shift_in))
    attention = low_back(jnp.einsum('rlc,cd->rld', mixed, out_w, precision=highest))
    h_one = source + attention
    x_two = low(rms_scale(h_one, gain_pair[1]))
    gate_up = low_back(jnp.einsum('rld,dcf->rlcf', x_two, wide_w, precision=highest))
    hidden = low(jax.nn.silu(gate_up[:, :, 0]) * gate_up[:, :, 1])
    feed = low_back(jnp.einsum('rlf,fd->rld', hidden, down_w, precision=highest))
    return (h_one + feed, rate_summary(logits))

def reference(layer_input, doc_lengths, norm_gains, mixing, rate_weight, rate_offset, expand, hidden_bias, contract, result_bias, head_gains, head_shift, output_proj, swiglu, down_proj, cotangent):
    weights = tuple((array.astype(jnp.float32) for array in (norm_gains, mixing, rate_weight, rate_offset, expand, hidden_bias, contract, result_bias, head_gains, head_shift, output_proj, swiglu, down_proj)))
    flags = reset_flags(doc_lengths, LEN // MBT)

    def model(source, shift_in, params, resets):
        first_out, first_stats = layer(source, resets, tuple((param[0] for param in params)))
        middle = low_back(low(first_out)) + shift_in
        second_out, second_stats = layer(middle, resets, tuple((param[1] for param in params)))
        return (second_out, (first_out, second_out, first_stats, second_stats))

    def one_batch(totals, inputs):
        source, resets, grad_given = inputs
        source = source.astype(jnp.float32)
        _, back, extra = jax.vjp(partial(model, resets=resets), source, jnp.zeros_like(source), weights, has_aux=True)
        source_grad, middle_grad, weight_grad = back(grad_given.astype(jnp.float32))
        totals = jax.tree.map(jnp.add, totals, weight_grad)
        first_out, second_out, first_stats, second_stats = extra
        return (totals, (jnp.stack([first_out, second_out]).astype(jnp.bfloat16), jnp.stack([source_grad, middle_grad]), jnp.stack([first_stats, second_stats])))
    start = jax.tree.map(jnp.zeros_like, weights)
    totals, (outputs, grads_all, stats_all) = lax.scan(one_batch, start, (layer_input, flags, cotangent))
    layer_output = jnp.swapaxes(outputs, 0, 1)
    input_grads = jnp.swapaxes(grads_all, 0, 1)
    rate_stats = jnp.swapaxes(stats_all, 0, 1)
    return (layer_output, input_grads, totals[0], totals[1], totals[2], totals[3], totals[4], totals[5], totals[6], totals[7], totals[8], totals[9], totals[10], totals[11], totals[12], rate_stats)
```

```python
import functools
import jax
import jax.numpy as jnp
from jax import lax
from jax.experimental import pallas as pl
from jax.experimental.pallas import tpu as pltpu
from jax.sharding import PartitionSpec as P

MBT = 16
EPS = 1e-06
RATE = 0.125
C0 = 0.7978845608028654
BF = jnp.bfloat16
F32 = jnp.float32
VMEM = pl.BlockSpec(memory_space=pltpu.VMEM)
SMEM = pl.BlockSpec(memory_space=pltpu.SMEM)
ANY = pl.BlockSpec(memory_space=pl.ANY)
NRM, INV, MIS, MEANN, GZ2, NA, INVA, NO, INVO, GATE = range(10)
INNER_ROWS = 832


def dot(a, b):
    return jnp.dot(a, b, preferred_element_type=F32)


def dot_t(a, b):
    return lax.dot_general(a, b, (((1,), (1,)), ((), ())), preferred_element_type=F32)


def tdot(a, b):
    return lax.dot_general(a, b, (((0,), (0,)), ((), ())), preferred_element_type=F32)


def cat(parts, axis):
    return jnp.concatenate(parts, axis=axis)


def gelu_parts(z):
    z2 = z * z
    t = jnp.tanh(C0 * z * (1.0 + 0.044715 * z2))
    h = 0.5 * (1.0 + t)
    du = C0 * (1.0 + 0.134145 * z2)
    sech = 1.0 - t * t
    value = z * h
    slope = h + 0.5 * z * sech * du
    return value, slope, t, z2, du, sech


def gelu_two(z):
    value, slope, _, _, _, _ = gelu_parts(z)
    return value, slope


def gelu_curve(z):
    _, _, t, z2, du, sech = gelu_parts(z)
    return sech * (C0 * (1.0 + 0.26829 * z2) - z * t * du * du)


def rms_inv(values):
    return lax.rsqrt(jnp.mean(values * values, axis=-1, keepdims=True) + EPS)


class Pick:
    def __init__(self, layer, sems):
        self.own = lax.axis_index("segment") == layer
        self.sems = sems
        self.count = 0

    def start(self, own_ref, other_ref, dst):
        sem = self.sems.at[self.count]
        self.count += 1

        @pl.when(self.own)
        def _():
            pltpu.make_async_copy(own_ref, dst, sem).start()

        @pl.when(jnp.logical_not(self.own))
        def _():
            pltpu.make_async_copy(other_ref, dst, sem).start()

        return pltpu.make_async_copy(own_ref, dst, sem)


def doc_places(dl_ref, steps):
    core = lax.axis_index("segment")
    one, two = dl_ref[core, 0], dl_ref[core, 1]
    begin = jnp.where(one == steps, 0, jnp.where(two == steps, one, one + two))
    cut = jnp.where(one == steps, two, one)
    return begin, cut


def block_starts(begin, steps):
    places = []
    for s in range(steps):
        places.append(pl.multiple_of((begin + s) * MBT, MBT))
        places.append(pl.multiple_of(jnp.where(s < begin, s, s + steps) * MBT, MBT))
    return places


def gather_rows(ref, lead, places):
    return cat([ref[lead, pl.ds(p, MBT), :] for p in places], 0)


def scatter_rows(ref, places, value):
    for i, p in enumerate(places):
        ref[pl.ds(p, MBT), :] = value[i * MBT : (i + 1) * MBT, :]


def masks(cut, length):
    def parts(axis):
        i = lax.broadcasted_iota(jnp.int32, (length, length), axis)
        step, lane, t = i >> 5, (i >> 4) & 1, i & 15
        doc = jnp.where(lane == 0, 0, jnp.where(step < cut, 1, 2))
        return step, lane, t, doc

    s0, l0, t0, d0 = parts(0)
    s1, l1, t1, d1 = parts(1)
    same = d0 == d1
    block = (s0 == s1) & (l0 == l1)
    past = jnp.where(same & (s1 < s0), 1.0 / MBT, 0.0)
    past_t = jnp.where(same & (s0 < s1), 1.0 / MBT, 0.0)
    inside = jnp.where(block & (t1 <= t0), 1.0 / (t0 + 1).astype(F32), 0.0)
    inside_t = jnp.where(block & (t0 <= t1), 1.0 / (t1 + 1).astype(F32), 0.0)
    return past, past + inside, past_t, past_t + inside_t


class Halves:
    def __init__(self):
        lane = lax.broadcasted_iota(jnp.int32, (1, 128), 1)
        self.left = lane < 64
        r = lax.broadcasted_iota(jnp.int32, (256, 128), 0) & 127
        c = lax.broadcasted_iota(jnp.int32, (256, 128), 1)
        self.mean_mat = jnp.where((r < 64) == (c < 64), 1.0 / 64.0, 0.0).astype(BF)

    def mean(self, x):
        high = x.astype(BF)
        low = (x - high.astype(F32)).astype(BF)
        return dot(cat([high, low], 1), self.mean_mat)

    def split(self, x):
        zero = jnp.zeros_like(x)
        return cat([jnp.where(self.left, x, zero), jnp.where(self.left, zero, x)], 0)

    def pack(self, a, b):
        return jnp.where(self.left, a, b)


def pair_weights(inner_ref, small_ref, heads, p, halves):
    width = inner_ref.shape[2]
    zero = jnp.zeros((64, width), BF)

    def blocks(a, b):
        return cat([cat([a, zero], 1), cat([zero, b], 1)], 0)

    def centred(index):
        w = inner_ref[heads + index].astype(F32)
        return (w - jnp.mean(w, axis=0, keepdims=True)).astype(BF)

    w1 = blocks(inner_ref[2 * p], inner_ref[2 * p + 1])
    w2 = blocks(centred(2 * p), centred(2 * p + 1))
    return w1, w2


def pad_rows(parts, rows):
    have = sum(x.shape[0] for x in parts)
    if have < rows:
        parts = parts + [jnp.zeros((rows - have, parts[0].shape[1]), parts[0].dtype)]
    return cat(parts, 0) if len(parts) > 1 else parts[0]


def mixer_forward(refs, x_one, mix_ref, rate_ref, inner_ref, small_ref, begin_cut, x1_ready):
    (mixed_ref, stats_ref, kq_ref, x2_ref, g1_ref, y2_ref, d1_ref, ud2_ref, e1_ref, sm_ref, sg_ref) = refs
    _, cut = begin_cut
    length = x_one.shape[0]
    heads = inner_ref.shape[0] // 2
    pairs = heads // 2
    hid = inner_ref.shape[2]
    wide = heads * 64
    steps = length // (2 * MBT)
    rows = 2 * MBT
    past, near, _, _ = masks(cut, length)
    hv = Halves()
    proj = dot(x_one, mix_ref[...])
    logits = dot_t(x_one, rate_ref[...]) + small_ref[3:4, 0:16]
    sg = jax.nn.sigmoid(logits)
    sg_ref[...] = sg
    stats_ref[...] = cat(
        [jnp.mean(sg, axis=0, keepdims=True), jnp.max(sg, axis=0, keepdims=True)], 0
    )
    rates = RATE * sg
    st = []
    for p in range(pairs):
        c = slice(128 * p, 128 * p + 128)
        h = slice(2 * hid * p, 2 * hid * (p + 1))
        q, k, v, gate = [proj[:, wide * i + 128 * p : wide * i + 128 * p + 128] for i in range(4)]
        d = dict(q=q, gate=gate, diff=v - k, c=c, h=h)
        d["w1"], d["w2"] = pair_weights(inner_ref, small_ref, heads, p, hv)
        d["b1"] = small_ref[0:1, h]
        b2 = small_ref[2:3, 128 * p : 128 * p + 128]
        d["b2"] = b2 - hv.mean(jnp.broadcast_to(b2, (8, 128)))[0:1]
        d["g"] = small_ref[2:3, wide + 128 * p : wide + 128 * p + 128]
        d["gp"] = small_ref[2:3, 2 * wide + 128 * p : 2 * wide + 128 * p + 128]
        d["be"] = small_ref[2:3, 3 * wide + 128 * p : 3 * wide + 128 * p + 128]
        d["r"] = [rates[:, 2 * p + i : 2 * p + i + 1] for i in range(2)]
        d["rp"] = hv.pack(d["r"][0], d["r"][1])
        d["kb"], d["qb"] = k.astype(BF), q.astype(BF)
        kq_ref[:, c] = d["kb"]
        kq_ref[:, wide + 128 * p : wide + 128 * p + 128] = d["qb"]
        d["base"] = dot(d["kb"], d["w1"]) + d["b1"]
        kk = dot_t(hv.split(d["kb"]), d["kb"])
        d["m1"] = [(past * (kk[i * length : (i + 1) * length] + 1.0)).astype(BF) for i in range(2)]
        for name in ("x2", "g1", "g2", "z1", "u"):
            d[name] = []
        st.append(d)
    for s in range(steps):
        sl = slice(rows * s, rows * s + rows)
        for p in range(pairs):
            d = st[p]
            c, h = d["c"], d["h"]
            z1 = d["base"][sl]
            if s:
                g1 = pad_rows(d["g1"], length)
                x2 = pad_rows(d["x2"], length)
                g2 = pad_rows(d["g2"], length)
                z1 = z1 - cat([dot(d["m1"][i][sl], g1[:, hid * i : hid * (i + 1)]) for i in range(2)], 1)
            act, slope = gelu_two(z1)
            actb = act.astype(BF)
            z2 = dot_t(actb, d["w2"]) + d["b2"]
            if s:
                far = [
                    (past[sl] * (dot_t(actb[:, hid * i : hid * (i + 1)], x2[:, hid * i : hid * (i + 1)]) + 1.0)).astype(BF)
                    for i in range(2)
                ]
                z2 = z2 - dot(cat(far, 1), hv.split(g2))
            inv = lax.rsqrt(hv.mean(z2 * z2) + EPS)
            n = z2 * inv
            mis = n * d["g"] + d["be"] - d["diff"][sl]
            misg = mis * d["g"]
            both = hv.mean(cat([misg, misg * n], 0))
            gz2 = (misg - both[:rows] - n * both[rows:]) * inv
            gz2b = gz2.astype(BF)
            u = dot(gz2b, d["w2"])
            if s:
                f = dot_t(hv.split(gz2b), g2)
                u = u - cat(
                    [
                        dot((past[sl] * f[rows * i : rows * (i + 1)]).astype(BF), x2[:, hid * i : hid * (i + 1)])
                        for i in range(2)
                    ],
                    1,
                )
            gz1 = u * slope
            r0, r1 = d["r"][0][sl], d["r"][1][sl]
            g1n = cat([gz1[:, :hid] * r0, gz1[:, hid:] * r1], 1).astype(BF)
            g2n = (gz2 * d["rp"][sl]).astype(BF)
            d["x2"].append(actb)
            d["g1"].append(g1n)
            d["g2"].append(g2n)
            d["z1"].append(z1)
            d["u"].append(u)
            x2_ref[sl, h] = actb
            g1_ref[sl, h] = g1n
            d1_ref[sl, h] = slope.astype(BF)
            sm_ref[NRM, sl, c] = n
            sm_ref[INV, sl, c] = inv
            sm_ref[MIS, sl, c] = mis
            sm_ref[MEANN, sl, c] = both[rows:]
            sm_ref[GZ2, sl, c] = gz2
    mixed = []
    for p in range(pairs):
        d = st[p]
        c, h = d["c"], d["h"]
        g1, x2, g2 = cat(d["g1"], 0), cat(d["x2"], 0), cat(d["g2"], 0)
        ud2_ref[:, h] = (cat(d["u"], 0) * gelu_curve(cat(d["z1"], 0))).astype(BF)
        qk = dot_t(hv.split(d["qb"]), d["kb"])
        corr = [
            dot((near * (qk[length * i : length * (i + 1)] + 1.0)).astype(BF), g1[:, hid * i : hid * (i + 1)])
            for i in range(2)
        ]
        act, slope = gelu_two(dot(d["qb"], d["w1"]) + d["b1"] - cat(corr, 1))
        actb = act.astype(BF)
        y2_ref[:, h] = actb
        e1_ref[:, h] = slope.astype(BF)
        far = [
            (near * (dot_t(actb[:, hid * i : hid * (i + 1)], x2[:, hid * i : hid * (i + 1)]) + 1.0)).astype(BF)
            for i in range(2)
        ]
        a2 = dot_t(actb, d["w2"]) + d["b2"] - dot(cat(far, 1), hv.split(g2))
        inv_a = lax.rsqrt(hv.mean(a2 * a2) + EPS)
        n_a = a2 * inv_a
        out = d["q"] + n_a * d["g"] + d["be"]
        inv_o = lax.rsqrt(hv.mean(out * out) + EPS)
        n_o = out * inv_o
        gated, _ = gelu_two(d["gate"])
        low = (gated * n_o * d["gp"]).astype(BF)
        mixed_ref[:, c] = low
        mixed.append(low)
        sm_ref[NA, :, c] = n_a
        sm_ref[INVA, :, c] = inv_a
        sm_ref[NO, :, c] = n_o
        sm_ref[INVO, :, c] = inv_o
        sm_ref[GATE, :, c] = d["gate"]
    return cat(mixed, 1)


def mixer_backward(dmixed, mixed_refs, inner_ref, small_ref, begin_cut, ig_ref):
    (kq_ref, x2_ref, g1_ref, y2_ref, d1_ref, ud2_ref, e1_ref, sm_ref, sg_ref) = mixed_refs
    _, cut = begin_cut
    length = dmixed.shape[0]
    heads = inner_ref.shape[0] // 2
    pairs = heads // 2
    hid = inner_ref.shape[2]
    wide = heads * 64
    steps = length // (2 * MBT)
    rows = 2 * MBT
    past, near, past_t, near_t = masks(cut, length)
    hv = Halves()
    sg = sg_ref[...]
    rates = RATE * sg

    def by_head(fn):
        return [fn(slice(hid * i, hid * (i + 1)), i) for i in range(2)]

    st = []
    for p in range(pairs):
        c = slice(128 * p, 128 * p + 128)
        h = slice(2 * hid * p, 2 * hid * (p + 1))
        d = dict(c=c, h=h)
        d["w1"], d["w2"] = pair_weights(inner_ref, small_ref, heads, p, hv)
        g = small_ref[2:3, wide + 128 * p : wide + 128 * p + 128]
        gp = small_ref[2:3, 2 * wide + 128 * p : 2 * wide + 128 * p + 128]
        d["g"] = g
        d["r"] = [rates[:, 2 * p + i : 2 * p + i + 1] for i in range(2)]
        d["rp"] = hv.pack(d["r"][0], d["r"][1])
        kb = kq_ref[:, c]
        qb = kq_ref[:, wide + 128 * p : wide + 128 * p + 128]
        x2, g1, y2 = x2_ref[:, h], g1_ref[:, h], y2_ref[:, h]
        gz2 = sm_ref[GZ2, :, c]
        gz2b = gz2.astype(BF)
        g2b = (gz2 * d["rp"]).astype(BF)
        dm = dmixed[:, c]
        gate = sm_ref[GATE, :, c]
        n_o, inv_o = sm_ref[NO, :, c], sm_ref[INVO, :, c]
        n_a, inv_a = sm_ref[NA, :, c], sm_ref[INVA, :, c]
        gated, gate_slope = gelu_two(gate)
        d["dgate"] = dm * n_o * gp * gate_slope
        drm = dm * gated
        d["dgp"] = jnp.sum(drm * n_o, axis=0, keepdims=True)
        dpg = drm * gp
        do = (dpg - n_o * hv.mean(dpg * n_o)) * inv_o
        dn = do * g
        both = hv.mean(cat([dn, dn * n_a], 0))
        da2 = (dn - both[:length] - n_a * both[length:]) * inv_a
        d["dg"] = jnp.sum(do * n_a, axis=0, keepdims=True)
        d["dbe"] = jnp.sum(do, axis=0, keepdims=True)
        d["db2"] = jnp.sum(da2, axis=0, keepdims=True)
        da2b = da2.astype(BF)
        da2m, g2m = hv.split(da2b), hv.split(g2b)
        km, qm = hv.split(kb), hv.split(qb)

        def weigh(mask, full, i):
            return (mask * full[length * i : length * (i + 1)]).astype(BF)

        p2 = dot_t(da2m, g2b)
        p2t = dot_t(g2m, da2b)
        dy2 = dot(da2b, d["w2"]) - cat(by_head(lambda e, i: dot(weigh(near, p2, i), x2[:, e])), 1)
        d["bx2"] = cat(by_head(lambda e, i: dot(weigh(near_t, p2t, i), y2[:, e])), 1)
        syt = cat(by_head(lambda e, i: (near_t * (dot_t(x2[:, e], y2[:, e]) + 1.0)).astype(BF)), 1)
        d["bg2"] = -dot(syt, da2m)
        da1 = dy2 * e1_ref[:, h].astype(F32)
        da1b = da1.astype(BF)
        d["db1"] = jnp.sum(da1, axis=0, keepdims=True)
        p1 = cat(by_head(lambda e, i: (near * dot_t(da1b[:, e], g1[:, e])).astype(BF)), 1)
        p1t = cat(by_head(lambda e, i: (near_t * dot_t(g1[:, e], da1b[:, e])).astype(BF)), 1)
        d["dq"] = do + dot_t(da1b, d["w1"]) - dot(p1, km)
        d["dk"] = -dot(p1t, qm)
        kq = dot_t(km, qb) + 1.0
        kk = dot_t(km, kb) + 1.0
        d["bg1"] = cat(by_head(lambda e, i: dot(weigh(near_t, kq, i), da1b[:, e])), 1)
        d["m1t"] = [weigh(past_t, kk, i) for i in range(2)]
        d["rx"] = by_head(lambda e, i: (past_t * (dot_t(x2[:, e], x2[:, e]) + 1.0)).astype(BF))
        ft = dot_t(g2m, gz2b)
        d["ft"] = [weigh(past_t, ft, i) for i in range(2)]
        d.update(x2=x2, y2=y2, g1=g1, g2b=g2b, g2m=g2m, gz2=gz2, gz2b=gz2b, gz2m=hv.split(gz2b))
        d.update(km=km, kb=kb, qb=qb, da1b=da1b, da2b=da2b)
        for name in ("z1", "z2", "u", "rg1", "rg2", "t"):
            d[name] = [None] * steps
        st.append(d)
    for s in reversed(range(steps)):
        sl = slice(rows * s, rows * s + rows)
        later = rows * (s + 1)
        for p in range(pairs):
            d = st[p]
            c, h = d["c"], d["h"]
            x2 = d["x2"]
            bg1, bg2, bx2 = -d["bg1"][sl], d["bg2"][sl], -d["bx2"][sl]
            if s < steps - 1:

                def full(parts):
                    done = parts[s + 1 :]
                    return cat([jnp.zeros((later, done[0].shape[1]), BF)] + done, 0)

                z1l, z2l, ul = full(d["z1"]), full(d["z2"]), full(d["u"])
                bg1 = bg1 - cat(by_head(lambda e, i: dot(d["m1t"][i][sl], z1l[:, e])), 1)
                xu = by_head(lambda e, i: (past_t[sl] * dot_t(x2[sl, e], ul[:, e])).astype(BF))
                lhs = cat([d["rx"][0][sl], d["rx"][1][sl]] + xu, 1)
                bg2 = bg2 - dot(lhs, cat([hv.split(z2l), d["gz2m"]], 0))
                gz = dot_t(hv.split(d["g2b"][sl]), z2l)
                bx2 = bx2 - cat(
                    by_head(
                        lambda e, i: dot(
                            cat([(past_t[sl] * gz[rows * i : rows * (i + 1)]).astype(BF), d["ft"][i][sl]], 1),
                            cat([x2[:, e], ul[:, e]], 0),
                        )
                    ),
                    1,
                )
            r0, r1 = d["r"][0][sl], d["r"][1][sl]
            dgz1 = cat([bg1[:, :hid] * r0, bg1[:, hid:] * r1], 1)
            slope = d1_ref[sl, h].astype(F32)
            du = dgz1 * slope
            dub = du.astype(BF)
            dz1 = dgz1 * ud2_ref[sl, h].astype(F32)
            dgz2 = bg2 * d["rp"][sl] + dot_t(dub, d["w2"])
            if s:
                hm = by_head(lambda e, i: (past[sl] * dot_t(dub[:, e], x2[:, e])).astype(BF))
                dgz2 = dgz2 - dot(cat(hm, 1), d["g2m"])
            n, inv = sm_ref[NRM, sl, c], sm_ref[INV, sl, c]
            mis, mn = sm_ref[MIS, sl, c], sm_ref[MEANN, sl, c]
            g = d["g"]
            e = dgz2 * inv
            three = hv.mean(cat([e, e * n, dgz2 * d["gz2"][sl]], 0))
            dmis = e - three[:rows] - n * three[rows : 2 * rows]
            t = dmis * g
            dn = t * g - e * mn - mis * g * three[rows : 2 * rows]
            two = hv.mean(cat([dn, dn * n], 0))
            dz2 = inv * (dn - two[:rows] - n * (two[rows:] + three[2 * rows :]))
            d["dg"] = d["dg"] + jnp.sum(t * n + dmis * mis, axis=0, keepdims=True)
            d["dbe"] = d["dbe"] + jnp.sum(t, axis=0, keepdims=True)
            d["db2"] = d["db2"] + jnp.sum(dz2, axis=0, keepdims=True)
            dz2b = dz2.astype(BF)
            dx2 = bx2 + dot(dz2b, d["w2"])
            if s:
                j = dot_t(hv.split(dz2b), d["g2b"])
                dx2 = dx2 - cat(
                    by_head(lambda e, i: dot((past[sl] * j[rows * i : rows * (i + 1)]).astype(BF), x2[:, e])), 1
                )
            dz1 = dz1 + dx2 * slope
            d["db1"] = d["db1"] + jnp.sum(dz1, axis=0, keepdims=True)
            d["z1"][s], d["z2"][s], d["u"][s] = dz1.astype(BF), dz2b, dub
            d["rg1"][s], d["rg2"][s], d["t"][s] = bg1, bg2, t
    parts = [[], [], [], []]
    rate_cols = []
    for p in range(pairs):
        d = st[p]
        z1, z2, u = cat(d["z1"], 0), cat(d["z2"], 0), cat(d["u"], 0)
        t = cat(d["t"], 0)
        g1 = d["g1"]
        both = cat(
            by_head(
                lambda e, i: (past * dot_t(z1[:, e], g1[:, e]) + past_t * dot_t(g1[:, e], z1[:, e])).astype(BF)
            ),
            1,
        )
        dk = d["dk"] + t + dot_t(z1, d["w1"]) - dot(both, d["km"])
        for i, value in enumerate((d["dq"], dk, -t, d["dgate"])):
            parts[i].append(value.astype(BF))
        dw1 = tdot(cat([d["kb"], d["qb"]], 0), cat([z1, d["da1b"]], 0))
        dw2 = tdot(cat([z2, d["da2b"], d["gz2b"]], 0), cat([d["x2"], d["y2"], u], 0))
        for i in range(2):
            row = 64 * (2 * p + i)
            ig_ref[row : row + 64, :] = dw1[64 * i : 64 * i + 64, hid * i : hid * (i + 1)]
            row = row + 64 * heads
            ig_ref[row : row + 64, :] = dw2[64 * i : 64 * i + 64, hid * i : hid * (i + 1)]
            ig_ref[786 + 2 * p + i : 787 + 2 * p + i, :] = d["db1"][:, hid * i : hid * (i + 1)]
        one = cat(d["rg1"], 0) * g1.astype(F32)
        two = cat(d["rg2"], 0) * d["g2b"].astype(F32)
        two = cat([jnp.where(hv.left, two, 0.0), jnp.where(hv.left, 0.0, two)], 1)
        for i in range(2):
            whole = one[:, hid * i : hid * i + 128] + one[:, hid * i + 128 : hid * (i + 1)]
            whole = whole + two[:, 128 * i : 128 * (i + 1)]
            rate_cols.append(jnp.sum(whole, axis=-1, keepdims=True))
        for j, name in enumerate(("db2", "dg", "dgp", "dbe")):
            piece = 3 * j + p
            ig_ref[792 + piece // 2 : 793 + piece // 2, 128 * (piece % 2) : 128 * (piece % 2) + 128] = d[name]
    lane = lax.broadcasted_iota(jnp.int32, (1, 16), 1)
    dlog = jnp.zeros((length, 16), F32)
    for i, col in enumerate(rate_cols):
        dlog = dlog + jnp.where(lane == i, col, 0.0)
    dlog = dlog * (1.0 - sg)
    ig_ref[798:799, 0:16] = jnp.sum(dlog, axis=0, keepdims=True)
    dmix = [cat(x, 1) for x in parts]
    return dmix, dlog.astype(BF)


def ka_body(layer, *args):
    if layer == 0:
        dl_ref, li_ref = args[:2]
        rest = args[2:]
    else:
        dl_ref, h1_ref, fo_ref, fr_ref = args[:4]
        rest = args[4:]
    wrefs, rest = rest[:10], rest[10:]
    if layer == 1:
        lo_ref, rest = rest[0], rest[1:]
    hb_ref, x1_ref, att_ref = rest[:3]
    saves, scratch = rest[3:14], rest[14:]
    mix_v, inner_v, small_v, rate_v, out_v, sems = scratch
    pick = Pick(layer, sems)
    c_small = pick.start(wrefs[0], wrefs[1], small_v)
    c_mix = pick.start(wrefs[2], wrefs[3], mix_v)
    c_rate = pick.start(wrefs[4], wrefs[5], rate_v)
    c_inner = pick.start(wrefs[6], wrefs[7], inner_v)
    c_out = pick.start(wrefs[8], wrefs[9], out_v)
    length = hb_ref.shape[0]
    steps = length // (2 * MBT)
    begin, cut = doc_places(dl_ref, steps)
    places = block_starts(begin, steps)
    if layer == 0:
        low = gather_rows(li_ref, lax.axis_index("segment"), places)
    else:
        low = (h1_ref[...] + (fo_ref[...].astype(F32) + fr_ref[...].astype(F32))).astype(BF)
        scatter_rows(lo_ref, places, low)
    hb_ref[...] = low
    h = low.astype(F32)
    inv = rms_inv(h)
    c_small.wait()
    x_one = (h * inv * small_v[1:2, 0 : h.shape[1]]).astype(BF)
    x1_ref[...] = x_one
    c_mix.wait()
    c_rate.wait()
    c_inner.wait()
    mixed = mixer_forward(saves, x_one, mix_v, rate_v, inner_v, small_v, (begin, cut), None)
    c_out.wait()
    att_ref[...] = dot(mixed, out_v[...]).astype(BF)


def ffn_forward(h1, small_v, sw_v, dn_v, copies):
    width = h1.shape[1]
    inv = rms_inv(h1)
    x2 = (h1 * inv * small_v[1:2, width : 2 * width]).astype(BF)
    copies[0].wait()
    up_at = sw_v.shape[1] // 2
    gate = dot(x2, sw_v[:, :up_at])
    up = dot(x2, sw_v[:, up_at:])
    sgm = 1.0 / (1.0 + jnp.exp(-gate))
    silu = gate * sgm
    slope = up * (sgm * (1.0 + gate * (1.0 - sgm)))
    hidden = (silu * up).astype(BF)
    copies[1].wait()
    feed = dot(hidden, dn_v[...]).astype(BF)
    return x2, hidden, slope, silu, feed


def ffn_backward(dfe, slope, silu, sw_v, dn_v):
    up_at = sw_v.shape[1] // 2
    dh = dot_t(dfe, dn_v[...])
    dg, du = (dh * slope).astype(BF), (dh * silu).astype(BF)
    dx = dot_t(dg, sw_v[:, :up_at]) + dot_t(du, sw_v[:, up_at:])
    return dg, du, dx.astype(BF)


def pack_ffn(keep_ref, send_ref, x2, dg, du, hidden, dfe):
    first = lax.axis_index("segment") == 0
    width, wide = x2.shape[1], dg.shape[1]
    half = wide // 2

    def put(ref, grad, hid):
        ref[:, 0:width] = x2
        ref[:, width : width + wide] = grad
        ref[:, width + wide : width + wide + half] = hid
        ref[:, width + wide + half :] = dfe

    @pl.when(first)
    def _():
        put(keep_ref, dg, hidden[:, :half])
        put(send_ref, du, hidden[:, half:])

    @pl.when(jnp.logical_not(first))
    def _():
        put(keep_ref, du, hidden[:, half:])
        put(send_ref, dg, hidden[:, :half])


def kf_body(hb_ref, ao_ref, ar_ref, s_own, s_oth, w_own, w_oth, d_own, d_oth,
            h1_ref, x2_ref, hid_ref, sl_ref, si_ref, fe_ref, small_v, sw_v, dn_v, sems):
    pick = Pick(0, sems)
    c_small = pick.start(s_own, s_oth, small_v)
    copies = [pick.start(w_own, w_oth, sw_v), pick.start(d_own, d_oth, dn_v)]
    h1 = hb_ref[...].astype(F32) + (ao_ref[...].astype(F32) + ar_ref[...].astype(F32))
    h1_ref[...] = h1
    c_small.wait()
    x2, hidden, slope, silu, feed = ffn_forward(h1, small_v, sw_v, dn_v, copies)
    x2_ref[...] = x2
    hid_ref[...] = hidden
    sl_ref[...] = slope.astype(BF)
    si_ref[...] = silu.astype(BF)
    fe_ref[...] = feed


def kfb_body(dl_ref, ct_ref, hb_ref, ao_ref, ar_ref, s_own, s_oth, w_own, w_oth, d_own, d_oth,
             h1_ref, fe_ref, dxt_ref, dfe_ref, keep_ref, send_ref, small_v, sw_v, dn_v, sems):
    pick = Pick(1, sems)
    c_small = pick.start(s_own, s_oth, small_v)
    copies = [pick.start(w_own, w_oth, sw_v), pick.start(d_own, d_oth, dn_v)]
    length = hb_ref.shape[0]
    steps = length // (2 * MBT)
    begin, _ = doc_places(dl_ref, steps)
    dfe = gather_rows(ct_ref, lax.axis_index("segment"), block_starts(begin, steps))
    dfe_ref[...] = dfe
    h1 = hb_ref[...].astype(F32) + (ao_ref[...].astype(F32) + ar_ref[...].astype(F32))
    h1_ref[...] = h1
    c_small.wait()
    x2, hidden, slope, silu, feed = ffn_forward(h1, small_v, sw_v, dn_v, copies)
    fe_ref[...] = feed
    dg, du, dx = ffn_backward(dfe, slope, silu, sw_v, dn_v)
    dxt_ref[...] = dx
    pack_ffn(keep_ref, send_ref, x2, dg, du, hidden, dfe)


def norm_back(dx, x, gain, base):
    inv = rms_inv(x)
    e = dx * gain
    grad = base + e * inv - x * (jnp.mean(e * x, axis=-1, keepdims=True) * inv * inv * inv)
    gain_grad = jnp.sum(dx * x * inv, axis=0, keepdims=True)
    return grad, gain_grad


def kbf_body(dl_ref, hb_ref, dh_ref, xo_ref, xr_ref, t_own, t_oth, x2_ref, hid_ref, sl_ref, si_ref,
             w_own, w_oth, d_own, d_oth,
             ig_ref, gg_ref, dfe_ref, dxt_ref, keep_ref, send_ref, small_v, sw_v, dn_v, sems, sems_two):
    above = Pick(1, sems)
    c_small = above.start(t_own, t_oth, small_v)
    pick = Pick(0, sems_two)
    copies = [pick.start(d_own, d_oth, dn_v), pick.start(w_own, w_oth, sw_v)]
    length, width = hb_ref.shape
    steps = length // (2 * MBT)
    begin, _ = doc_places(dl_ref, steps)
    dx = xo_ref[...].astype(F32) + xr_ref[...].astype(F32)
    c_small.wait()
    grad, gain = norm_back(dx, hb_ref[...].astype(F32), small_v[1:2, 0:width], dh_ref[...])
    scatter_rows(ig_ref, block_starts(begin, steps), grad)
    gg_ref[...] = gain
    dfe = grad.astype(BF)
    dfe_ref[...] = dfe
    for c in copies:
        c.wait()
    dg, du, dxt = ffn_backward(dfe, sl_ref[...].astype(F32), si_ref[...].astype(F32), sw_v, dn_v)
    dxt_ref[...] = dxt
    pack_ffn(keep_ref, send_ref, x2_ref[...], dg, du, hid_ref[...], dfe)


def kba_body(layer, dl_ref, xo_ref, xr_ref, dy_ref, h1_ref, x1_ref, mixed_ref, *rest):
    saves, rest = rest[:9], rest[9:]
    wrefs, rest = rest[:10], rest[10:]
    dh_ref, dxo_ref, keep_ref, send_ref, ig_ref, mix_v, inner_v, small_v, rate_v, out_v, sems = rest
    pick = Pick(layer, sems)
    c_small = pick.start(wrefs[0], wrefs[1], small_v)
    c_out = pick.start(wrefs[8], wrefs[9], out_v)
    c_inner = pick.start(wrefs[6], wrefs[7], inner_v)
    c_mix = pick.start(wrefs[2], wrefs[3], mix_v)
    c_rate = pick.start(wrefs[4], wrefs[5], rate_v)
    length, width = h1_ref.shape
    steps = length // (2 * MBT)
    place = doc_places(dl_ref, steps)
    dx = xo_ref[...].astype(F32) + xr_ref[...].astype(F32)
    c_small.wait()
    dh, gain = norm_back(dx, h1_ref[...], small_v[1:2, width : 2 * width], dy_ref[...].astype(F32))
    dh_ref[...] = dh
    ig_ref[768:INNER_ROWS, :] = jnp.zeros((INNER_ROWS - 768, ig_ref.shape[1]), F32)
    for j in range(3):
        ig_ref[799 + j : 800 + j, :] = gain[:, 256 * j : 256 * j + 256]
    da = dh.astype(BF)
    c_out.wait()
    c_inner.wait()
    dmixed = dot_t(da, out_v[...])
    dmix, dlog = mixer_backward(dmixed, saves, inner_v, small_v, place, ig_ref)
    x1 = x1_ref[...]
    drate = tdot(dlog, x1)
    heads = inner_v.shape[0] // 2
    for j in range(3):
        ig_ref[768 + heads * j : 768 + heads * (j + 1), :] = drate[:heads, 256 * j : 256 * j + 256]
    c_mix.wait()
    c_rate.wait()
    dxo_ref[...] = (dot_t(cat(dmix, 1), mix_v[...]) + dot(dlog, rate_v[...])).astype(BF)
    first = lax.axis_index("segment") == 0
    half = width // 2
    wide = 2 * dmix[0].shape[1]

    def put(ref, one, two, att):
        ref[:, 0:width] = x1
        ref[:, width : width + wide // 2] = one
        ref[:, width + wide // 2 : width + wide] = two
        ref[:, width + wide : width + wide + mixed_ref.shape[1]] = mixed_ref[...]
        ref[:, width + wide + mixed_ref.shape[1] :] = att

    @pl.when(first)
    def _():
        put(keep_ref, dmix[0], dmix[1], da[:, :half])
        put(send_ref, dmix[2], dmix[3], da[:, half:])

    @pl.when(jnp.logical_not(first))
    def _():
        put(keep_ref, dmix[2], dmix[3], da[:, half:])
        put(send_ref, dmix[0], dmix[1], da[:, :half])


def ke_body(dl_ref, hb_ref, dh_ref, xo_ref, xr_ref, s_own, s_oth, ig_ref, gg_ref, small_v, sems):
    pick = Pick(0, sems)
    c_small = pick.start(s_own, s_oth, small_v)
    length, width = hb_ref.shape
    steps = length // (2 * MBT)
    begin, _ = doc_places(dl_ref, steps)
    dx = xo_ref[...].astype(F32) + xr_ref[...].astype(F32)
    c_small.wait()
    grad, gain = norm_back(dx, hb_ref[...].astype(F32), small_v[1:2, 0:width], dh_ref[...])
    scatter_rows(ig_ref, block_starts(begin, steps), grad)
    gg_ref[...] = gain


def kgf_body(keep_ref, recv_ref, dsw_ref, ddn_ref):
    both = cat([keep_ref[...], recv_ref[...]], 0)
    width, wide, half = dsw_ref.shape[0], dsw_ref.shape[1], ddn_ref.shape[0]
    dsw_ref[...] = tdot(both[:, :width], both[:, width : width + wide]).astype(BF)
    ddn_ref[...] = tdot(both[:, width + wide : width + wide + half], both[:, width + wide + half :]).astype(BF)


def kga_body(keep_ref, recv_ref, ik_ref, ir_ref, dmx_ref, dow_ref, din_ref):
    both = cat([keep_ref[...], recv_ref[...]], 0)
    width, wide, heads_wide = dmx_ref.shape[0], dmx_ref.shape[1], dow_ref.shape[0]
    dmx_ref[...] = tdot(both[:, :width], both[:, width : width + wide]).astype(BF)
    dow_ref[...] = tdot(both[:, width + wide : width + wide + heads_wide], both[:, width + wide + heads_wide :]).astype(BF)
    rows = din_ref.shape[0]
    at = pl.multiple_of(lax.axis_index("segment") * rows, rows)
    din_ref[...] = (ik_ref[pl.ds(at, rows), :] + ir_ref[pl.ds(at, rows), :]).astype(BF)


def call(body, name, ins, specs, outs, scratch=(), flops=2e8, nbytes=8e6):
    return pl.pallas_call(
        body,
        out_shape=[jax.ShapeDtypeStruct(s, t) for s, t in outs],
        in_specs=specs,
        out_specs=[VMEM] * len(outs),
        scratch_shapes=list(scratch),
        compiler_params=pltpu.CompilerParams(vmem_limit_bytes=48 * 1024 * 1024),
        cost_estimate=pl.CostEstimate(flops=int(flops), bytes_accessed=int(nbytes), transcendentals=0),
        name=name,
    )(*ins)


def swap(value, axis):
    return lax.ppermute(value, axis, [(0, 1), (1, 0)])


def shards(
    layer_input, doc_lengths, norm_gains, mixing, rate_weight, rate_offset, expand, hidden_bias, contract,
    result_bias, head_gains, head_shift, output_proj, swiglu, down_proj, cotangent,
):
    micro, _, length, width = layer_input.shape
    heads = rate_weight.shape[2]
    hid = expand.shape[3]
    wide = heads * 64
    ff = down_proj.shape[1]
    first = lax.axis_index("segment") == 0
    dl = doc_lengths.reshape(micro, 3)
    li = layer_input.reshape(micro, length, width)
    ct = cotangent.reshape(micro, length, width)
    small = jnp.stack(
        [
            hidden_bias.reshape(-1),
            norm_gains.reshape(-1),
            cat([result_bias.reshape(-1), head_gains.reshape(-1), head_shift.reshape(-1)], 0),
            jnp.pad(rate_offset.reshape(-1), (0, heads * hid - heads)),
        ]
    )
    mix = mixing[0].reshape(width, -1)
    rate = jnp.pad(rate_weight[0].T, ((0, 16 - heads), (0, 0)))
    inner = cat([expand[0], jnp.swapaxes(contract[0], 1, 2)], 0).astype(BF)
    ow = output_proj[0]
    sw = swiglu[0].reshape(width, -1)
    dn = down_proj[0]

    def both(x):
        return (x, swap(x, "segment"))

    small_p, mix_p, rate_p, inner_p, ow_p = both(small), both(mix), both(rate), both(inner), both(ow)
    sw_p, dn_p = both(sw), both(dn)
    att_w = small_p + mix_p + rate_p + inner_p + ow_p
    tok = (length, width)
    save_shapes = [
        ((length, wide), BF), ((2, 16), F32), ((length, 2 * wide), BF),
        ((length, heads * hid), BF), ((length, heads * hid), BF), ((length, heads * hid), BF),
        ((length, heads * hid), BF), ((length, heads * hid), BF), ((length, heads * hid), BF),
        ((10, length, wide), F32), ((length, 16), F32),
    ]
    sem = pltpu.SemaphoreType.DMA
    att_scratch = [
        pltpu.VMEM(mix.shape, BF), pltpu.VMEM(inner.shape, BF), pltpu.VMEM(small.shape, F32),
        pltpu.VMEM(rate.shape, BF), pltpu.VMEM(ow.shape, BF), sem((5,)),
    ]
    ffn_scratch = [pltpu.VMEM(small.shape, F32), pltpu.VMEM(sw.shape, BF), pltpu.VMEM(dn.shape, BF)]

    def ka(layer, ins):
        outs = [(tok, BF), (tok, BF), (tok, BF)] + save_shapes
        specs = [SMEM] + [VMEM] * (len(ins) - 1) + [ANY] * 10
        if layer == 1:
            outs = [(tok, BF)] + outs
        return call(functools.partial(ka_body, layer), f"mixer_fwd{layer}", list(ins) + list(att_w), specs, outs,
                    att_scratch, 6e9, 8e6)

    def exchange(x):
        return x, swap(x, "tensor")

    h0, x1_0, att, *save0 = ka(0, (dl, li))
    mixed0, stats0, save0 = save0[0], save0[1], save0[2:]
    ao, ar = exchange(att)
    h1_0, x2_0, hid_0, sl_0, si_0, fe = call(
        kf_body, "ffn_fwd0", [h0, ao, ar, *small_p, *sw_p, *dn_p], [VMEM] * 3 + [ANY] * 6,
        [(tok, F32), (tok, BF)] + [((length, ff), BF)] * 3 + [(tok, BF)], ffn_scratch + [sem((3,))], 1e9, 6e6)
    fo, fr = exchange(fe)
    lo0, hm, x1_1, att, *save1 = ka(1, (dl, h1_0, fo, fr))
    mixed1, stats1, save1 = save1[0], save1[1], save1[2:]
    ao, ar = exchange(att)
    pack_f = (length, 2 * width + ff + ff // 2)
    h1_1, fe, dxt, dfe1, keep, send = call(
        kfb_body, "ffn_both1", [dl, ct, hm, ao, ar, *small_p, *sw_p, *dn_p], [SMEM] + [VMEM] * 4 + [ANY] * 6,
        [(tok, F32), (tok, BF), (tok, BF), (tok, BF), (pack_f, BF), (pack_f, BF)],
        ffn_scratch + [sem((3,))], 2e9, 6e6)

    def grad_ffn(keep, send):
        recv = swap(send, "segment")
        return call(kgf_body, "grad_ffn", [keep, recv], [VMEM] * 2,
                    [((width, ff), BF), ((ff // 2, width), BF)], (), 1e9, 8e6)

    def grad_att(keep, send, ig):
        recv, other = swap(send, "segment"), swap(ig, "segment")
        return call(kga_body, "grad_mixer", [keep, recv, ig, other], [VMEM] * 4,
                    [((width, 2 * wide), BF), ((wide, width // 2), BF), ((INNER_ROWS // 2, hid), BF)], (), 1e9, 8e6)

    xo, xr = exchange(dxt)
    fo, fr = exchange(fe)
    pack_a = (length, width + 2 * wide + wide + width // 2)

    def kba(layer, xo, xr, dy, h1, x1, mixed, save):
        return call(functools.partial(kba_body, layer), f"mixer_bwd{layer}",
                    [dl, xo, xr, dy, h1, x1, mixed, *save, *att_w], [SMEM] + [VMEM] * 15 + [ANY] * 10,
                    [(tok, F32), (tok, BF), (pack_a, BF), (pack_a, BF), ((INNER_ROWS, hid), F32)],
                    att_scratch, 8e9, 8e6)

    dsw1, ddn1 = grad_ffn(keep, send)
    dh, dxo, keep, send, ig = kba(1, xo, xr, dfe1, h1_1, x1_1, mixed1, save1)
    dsw1, ddn1 = lax.psum((dsw1, ddn1), "dp")
    xo, xr = exchange(dxo)
    dmx1, dow1, din1 = grad_att(keep, send, ig)
    dmx1, dow1, din1 = lax.psum((dmx1, dow1, din1), "dp")
    ig1, gg1, dfe0, dxt, keep, send = call(
        kbf_body, "ffn_bwd0",
        [dl, hm, dh, xo, xr, *small_p, x2_0, hid_0, sl_0, si_0, *sw_p, *dn_p],
        [SMEM] + [VMEM] * 4 + [ANY] * 2 + [VMEM] * 4 + [ANY] * 4,
        [(tok, F32), ((1, width), F32), (tok, BF), (tok, BF), (pack_f, BF), (pack_f, BF)],
        ffn_scratch + [sem((1,)), sem((2,))], 1e9, 6e6)
    xo, xr = exchange(dxt)
    dsw0, ddn0 = grad_ffn(keep, send)
    dsw0, ddn0 = lax.psum((dsw0, ddn0), "dp")
    dh, dxo, keep, send, ig = kba(0, xo, xr, dfe0, h1_0, x1_0, mixed0, save0)
    xo, xr = exchange(dxo)
    dmx0, dow0, din0 = grad_att(keep, send, ig)
    dmx0, dow0, din0 = lax.psum((dmx0, dow0, din0), "dp")
    ig0, gg0 = call(ke_body, "input_grad0", [dl, h0, dh, xo, xr, *small_p], [SMEM] + [VMEM] * 4 + [ANY] * 2,
                    [(tok, F32), ((1, width), F32)], [pltpu.VMEM(small.shape, F32), sem((1,))], 1e6, 2e6)

    def lo1_body(dl_ref, h1_ref, fo_ref, fr_ref, lo_ref):
        begin, _ = doc_places(dl_ref, length // (2 * MBT))
        low = (h1_ref[...] + (fo_ref[...].astype(F32) + fr_ref[...].astype(F32))).astype(BF)
        scatter_rows(lo_ref, block_starts(begin, length // (2 * MBT)), low)

    (lo1,) = call(lo1_body, "output1", [dl, h1_1, fo, fr], [SMEM] + [VMEM] * 3, [(tok, BF)], (), 1e6, 2e6)

    def to_one(x):
        return lax.ppermute(x, "segment", [(0, 1)])

    def to_zero(x):
        return lax.ppermute(x, "segment", [(1, 0)])

    def two_rows(zero, one):
        return jnp.where(first, jnp.stack([zero, to_zero(zero)]), jnp.stack([to_one(one), one]))[None, :, None]

    def two_halves(zero, one):
        left = jnp.where(first, zero, to_one(one)).astype(F32)
        right = jnp.where(first, to_zero(zero), one).astype(F32)
        return left, right

    layer_output = two_rows(lo0, lo1)
    input_grads = two_rows(ig0, ig1)
    gains_zero = lax.psum(cat([gg0, gg1], 0), ("segment", "dp"))
    g_mix = cat(two_halves(dmx0, dmx1), 1).reshape(mixing.shape)
    g_out = cat(two_halves(dow0, dow1), 1)[None]
    g_sw = jnp.stack(two_halves(dsw0, dsw1), 1)[None]
    g_dn = cat(two_halves(ddn0, ddn1), 0)[None]
    g_in = cat(two_halves(din0, din1), 0)
    g_expand = g_in[: 64 * heads].reshape(expand.shape)
    g_contract = jnp.swapaxes(g_in[64 * heads : 128 * heads].reshape(1, heads, 64, hid), 2, 3)
    g_rate = cat([g_in[768 + heads * j : 768 + heads * (j + 1)] for j in range(3)], 1).T[None]
    g_hidden = g_in[786 : 786 + heads][None]
    tail = g_in[792:798].reshape(4, heads, 64)
    g_result, g_heads, g_shift = tail[0][None], tail[1:3][None], tail[3][None]
    g_offset = g_in[798, :heads][None]
    g_gain_two = g_in[799:802].reshape(-1)
    gain_one = jnp.where(first, gains_zero[0], gains_zero[1])
    g_gains = jnp.stack([gain_one, g_gain_two])[None]
    stats = jnp.stack([stats0, stats1])[:, :, :heads]
    gathered = lax.all_gather(stats, ("segment", "dp", "tensor"))
    dp = lax.axis_size("dp")
    gathered = gathered.reshape(micro, dp, 2, 2, 2, heads)
    picked = jnp.where(first, gathered[:, :, :, 0], gathered[:, :, :, 1])
    rate_stats = jnp.transpose(picked, (0, 1, 3, 2, 4)).reshape(1, micro, dp, 2, 2 * heads)
    return (
        layer_output, input_grads, g_gains, g_mix, g_rate, g_offset, g_expand, g_hidden, g_contract, g_result,
        g_heads, g_shift, g_out, g_sw, g_dn, rate_stats,
    )


def solution(mesh):
    placed = (
        P(None, "dp", None, None),
        P(None, "dp", None),
        P("segment", None, None),
        P("segment", None, None, "tensor"),
        P("segment", None, "tensor"),
        P("segment", "tensor"),
        P("segment", "tensor", None, None),
        P("segment", "tensor", None),
        P("segment", "tensor", None, None),
        P("segment", "tensor", None),
        P("segment", None, "tensor", None),
        P("segment", "tensor", None),
        P("segment", "tensor", None),
        P("segment", None, None, "tensor"),
        P("segment", "tensor", None),
        P(None, "dp", None, None),
    )
    return jax.shard_map(
        shards,
        mesh=mesh,
        in_specs=placed,
        out_specs=(
            P("segment", None, "dp", None, None),
            P("segment", None, "dp", None, None),
            P("segment", None, None),
            P("segment", None, None, "tensor"),
            P("segment", None, "tensor"),
            P("segment", "tensor"),
            P("segment", "tensor", None, None),
            P("segment", "tensor", None),
            P("segment", "tensor", None, None),
            P("segment", "tensor", None),
            P("segment", None, "tensor", None),
            P("segment", "tensor", None),
            P("segment", "tensor", None),
            P("segment", None, None, "tensor"),
            P("segment", "tensor", None),
            P("segment", None, None, None, None),
        ),
        check_vma=False,
    )
```

```python
import functools
import jax
import jax.numpy as jnp
from jax import lax
from jax.experimental import pallas as pl
from jax.experimental.pallas import tpu as pltpu
from jax.sharding import PartitionSpec as P

MBT = 16
EPS = 1e-06
RATE = 0.125
C0 = 0.7978845608028654
BF = jnp.bfloat16
F32 = jnp.float32
VMEM = pl.BlockSpec(memory_space=pltpu.VMEM)
SMEM = pl.BlockSpec(memory_space=pltpu.SMEM)
HBM = pl.BlockSpec(memory_space=pltpu.HBM)
LOAD = "load"
NRM, INV, MIS, MEANN, GZ2 = range(5)
NA, INVA, NO, INVO, GATE = range(5)
RATE_ROW, HIDDEN_ROW, HEAD_ROW, OFFSET_ROW, GAIN_ROW, STAT_ROW = 0, 18, 24, 30, 31, 40
PACK_ROWS = 1152


def dot(a, b):
    return jnp.dot(a, b, preferred_element_type=F32)


def dot_t(a, b):
    return lax.dot_general(a, b, (((1,), (1,)), ((), ())), preferred_element_type=F32)


def tdot(a, b):
    return lax.dot_general(a, b, (((0,), (0,)), ((), ())), preferred_element_type=F32)


def cat(parts, axis):
    return jnp.concatenate(parts, axis=axis)


def gelu_parts(z):
    z2 = z * z
    t = jnp.tanh(C0 * z * (1.0 + 0.044715 * z2))
    h = 0.5 * (1.0 + t)
    du = C0 * (1.0 + 0.134145 * z2)
    sech = 1.0 - t * t
    value = z * h
    slope = h + 0.5 * z * sech * du
    return value, slope, t, z2, du, sech


def gelu_two(z):
    value, slope, _, _, _, _ = gelu_parts(z)
    return value, slope


def gelu_curve(z):
    _, _, t, z2, du, sech = gelu_parts(z)
    return sech * (C0 * (1.0 + 0.26829 * z2) - z * t * du * du)


def rms_inv(values):
    return lax.rsqrt(jnp.mean(values * values, axis=-1, keepdims=True) + EPS)


class Pick:
    def __init__(self, layer, sems):
        self.own = lax.axis_index("segment") == layer
        self.sems = sems
        self.count = 0

    def start(self, own_ref, other_ref, dst):
        sem = self.sems.at[self.count]
        self.count += 1

        @pl.when(self.own)
        def _():
            pltpu.make_async_copy(own_ref, dst, sem).start()

        @pl.when(jnp.logical_not(self.own))
        def _():
            pltpu.make_async_copy(other_ref, dst, sem).start()

        return pltpu.make_async_copy(own_ref, dst, sem)


def doc_places(dl_ref, steps):
    core = lax.axis_index("segment")
    one, two = dl_ref[core, 0], dl_ref[core, 1]
    begin = jnp.where(one == steps, 0, jnp.where(two == steps, one, one + two))
    cut = jnp.where(one == steps, two, one)
    return begin, cut


def block_starts(begin, steps):
    places = []
    for s in range(steps):
        places.append(pl.multiple_of((begin + s) * MBT, MBT))
        places.append(pl.multiple_of(jnp.where(s < begin, s, s + steps) * MBT, MBT))
    return places


def gather_rows(ref, lead, places):
    return cat([ref[lead, pl.ds(p, MBT), :] for p in places], 0)


def scatter_rows(ref, places, value):
    for i, p in enumerate(places):
        ref[pl.ds(p, MBT), :] = value[i * MBT : (i + 1) * MBT, :]


def masks(cut, length):
    def parts(axis):
        i = lax.broadcasted_iota(jnp.int32, (length, length), axis)
        step, lane, t = i >> 5, (i >> 4) & 1, i & 15
        doc = jnp.where(lane == 0, 0, jnp.where(step < cut, 1, 2))
        return step, lane, t, doc

    s0, l0, t0, d0 = parts(0)
    s1, l1, t1, d1 = parts(1)
    same = d0 == d1
    block = (s0 == s1) & (l0 == l1)
    past = jnp.where(same & (s1 < s0), 1.0 / MBT, 0.0)
    past_t = jnp.where(same & (s0 < s1), 1.0 / MBT, 0.0)
    inside = jnp.where(block & (t1 <= t0), 1.0 / (t0 + 1).astype(F32), 0.0)
    inside_t = jnp.where(block & (t0 <= t1), 1.0 / (t1 + 1).astype(F32), 0.0)
    return past, past + inside, past_t, past_t + inside_t


class Halves:
    def __init__(self):
        lane = lax.broadcasted_iota(jnp.int32, (1, 128), 1)
        self.left = lane < 64
        r = lax.broadcasted_iota(jnp.int32, (256, 128), 0) & 127
        c = lax.broadcasted_iota(jnp.int32, (256, 128), 1)
        self.mean_mat = jnp.where((r < 64) == (c < 64), 1.0 / 64.0, 0.0).astype(BF)

    def mean(self, x):
        high = x.astype(BF)
        low = (x - high.astype(F32)).astype(BF)
        return dot(cat([high, low], 1), self.mean_mat)

    def split(self, x):
        zero = jnp.zeros_like(x)
        return cat([jnp.where(self.left, x, zero), jnp.where(self.left, zero, x)], 0)

    def pack(self, a, b):
        return jnp.where(self.left, a, b)


def pair_weights(inner_ref, small_ref, heads, p, halves):
    width = inner_ref.shape[2]
    zero = jnp.zeros((64, width), BF)

    def blocks(a, b):
        return cat([cat([a, zero], 1), cat([zero, b], 1)], 0)

    def centred(index):
        w = inner_ref[heads + index].astype(F32)
        return (w - jnp.mean(w, axis=0, keepdims=True)).astype(BF)

    w1 = blocks(inner_ref[2 * p], inner_ref[2 * p + 1])
    w2 = blocks(centred(2 * p), centred(2 * p + 1))
    return w1, w2


def pad_rows(parts, rows):
    have = sum(x.shape[0] for x in parts)
    if have < rows:
        parts = parts + [jnp.zeros((rows - have, parts[0].shape[1]), parts[0].dtype)]
    return cat(parts, 0) if len(parts) > 1 else parts[0]


def mixer_forward(refs, x_one, mix_ref, rate_ref, inner_ref, small_ref, begin_cut, x1_ready):
    (mixed_ref, stats_ref, kq_ref, x2_ref, g1_ref, y2_ref, d1_ref, ud2_ref, e1_ref, sm_ref, so_ref, sg_ref) = refs
    _, cut = begin_cut
    length = x_one.shape[0]
    heads = inner_ref.shape[0] // 2
    pairs = heads // 2
    hid = inner_ref.shape[2]
    wide = heads * 64
    steps = length // (2 * MBT)
    rows = 2 * MBT
    past, near, _, _ = masks(cut, length)
    hv = Halves()
    proj = dot(x_one, mix_ref[...])
    logits = dot_t(x_one, rate_ref[...]) + small_ref[3:4, 0:16]
    sg = jax.nn.sigmoid(logits)
    sg_ref[...] = sg
    stats_ref[...] = cat(
        [jnp.mean(sg, axis=0, keepdims=True), jnp.max(sg, axis=0, keepdims=True)], 0
    )
    rates = RATE * sg
    st = []
    for p in range(pairs):
        c = slice(128 * p, 128 * p + 128)
        h = slice(2 * hid * p, 2 * hid * (p + 1))
        q, k, v, gate = [proj[:, wide * i + 128 * p : wide * i + 128 * p + 128] for i in range(4)]
        d = dict(q=q, gate=gate, diff=v - k, c=c, h=h)
        d["w1"], d["w2"] = pair_weights(inner_ref, small_ref, heads, p, hv)
        d["b1"] = small_ref[0:1, h]
        b2 = small_ref[2:3, 128 * p : 128 * p + 128]
        d["b2"] = b2 - hv.mean(jnp.broadcast_to(b2, (8, 128)))[0:1]
        d["g"] = small_ref[2:3, wide + 128 * p : wide + 128 * p + 128]
        d["gp"] = small_ref[2:3, 2 * wide + 128 * p : 2 * wide + 128 * p + 128]
        d["be"] = small_ref[2:3, 3 * wide + 128 * p : 3 * wide + 128 * p + 128]
        d["r"] = [rates[:, 2 * p + i : 2 * p + i + 1] for i in range(2)]
        d["rp"] = hv.pack(d["r"][0], d["r"][1])
        d["kb"], d["qb"] = k.astype(BF), q.astype(BF)
        kq_ref[:, c] = d["kb"]
        kq_ref[:, wide + 128 * p : wide + 128 * p + 128] = d["qb"]
        d["base"] = dot(d["kb"], d["w1"]) + d["b1"]
        kk = dot_t(hv.split(d["kb"]), d["kb"])
        d["m1"] = [(past * (kk[i * length : (i + 1) * length] + 1.0)).astype(BF) for i in range(2)]
        for name in ("x2", "g1", "g2", "z1", "u"):
            d[name] = []
        st.append(d)
    kq_ref.send()
    sg_ref.send()
    for s in range(steps):
        sl = slice(rows * s, rows * s + rows)
        for p in range(pairs):
            d = st[p]
            c, h = d["c"], d["h"]
            z1 = d["base"][sl]
            if s:
                g1 = pad_rows(d["g1"], length)
                x2 = pad_rows(d["x2"], length)
                g2 = pad_rows(d["g2"], length)
                z1 = z1 - cat([dot(d["m1"][i][sl], g1[:, hid * i : hid * (i + 1)]) for i in range(2)], 1)
            act, slope = gelu_two(z1)
            actb = act.astype(BF)
            z2 = dot_t(actb, d["w2"]) + d["b2"]
            if s:
                far = [
                    (past[sl] * (dot_t(actb[:, hid * i : hid * (i + 1)], x2[:, hid * i : hid * (i + 1)]) + 1.0)).astype(BF)
                    for i in range(2)
                ]
                z2 = z2 - dot(cat(far, 1), hv.split(g2))
            inv = lax.rsqrt(hv.mean(z2 * z2) + EPS)
            n = z2 * inv
            mis = n * d["g"] + d["be"] - d["diff"][sl]
            misg = mis * d["g"]
            both = hv.mean(cat([misg, misg * n], 0))
            gz2 = (misg - both[:rows] - n * both[rows:]) * inv
            gz2b = gz2.astype(BF)
            u = dot(gz2b, d["w2"])
            if s:
                f = dot_t(hv.split(gz2b), g2)
                u = u - cat(
                    [
                        dot((past[sl] * f[rows * i : rows * (i + 1)]).astype(BF), x2[:, hid * i : hid * (i + 1)])
                        for i in range(2)
                    ],
                    1,
                )
            gz1 = u * slope
            r0, r1 = d["r"][0][sl], d["r"][1][sl]
            g1n = cat([gz1[:, :hid] * r0, gz1[:, hid:] * r1], 1).astype(BF)
            g2n = (gz2 * d["rp"][sl]).astype(BF)
            d["x2"].append(actb)
            d["g1"].append(g1n)
            d["g2"].append(g2n)
            d["z1"].append(z1)
            d["u"].append(u)
            x2_ref[sl, h] = actb
            g1_ref[sl, h] = g1n
            d1_ref[sl, h] = slope.astype(BF)
            sm_ref[NRM, sl, c] = n
            sm_ref[INV, sl, c] = inv
            sm_ref[MIS, sl, c] = mis
            sm_ref[MEANN, sl, c] = both[rows:]
            sm_ref[GZ2, sl, c] = gz2
    for ref in (x2_ref, g1_ref, d1_ref, sm_ref):
        ref.send()
    mixed = []
    for p in range(pairs):
        d = st[p]
        c, h = d["c"], d["h"]
        g1, x2, g2 = cat(d["g1"], 0), cat(d["x2"], 0), cat(d["g2"], 0)
        ud2_ref[:, h] = (cat(d["u"], 0) * gelu_curve(cat(d["z1"], 0))).astype(BF)
        qk = dot_t(hv.split(d["qb"]), d["kb"])
        corr = [
            dot((near * (qk[length * i : length * (i + 1)] + 1.0)).astype(BF), g1[:, hid * i : hid * (i + 1)])
            for i in range(2)
        ]
        act, slope = gelu_two(dot(d["qb"], d["w1"]) + d["b1"] - cat(corr, 1))
        actb = act.astype(BF)
        y2_ref[:, h] = actb
        e1_ref[:, h] = slope.astype(BF)
        far = [
            (near * (dot_t(actb[:, hid * i : hid * (i + 1)], x2[:, hid * i : hid * (i + 1)]) + 1.0)).astype(BF)
            for i in range(2)
        ]
        a2 = dot_t(actb, d["w2"]) + d["b2"] - dot(cat(far, 1), hv.split(g2))
        inv_a = lax.rsqrt(hv.mean(a2 * a2) + EPS)
        n_a = a2 * inv_a
        out = d["q"] + n_a * d["g"] + d["be"]
        inv_o = lax.rsqrt(hv.mean(out * out) + EPS)
        n_o = out * inv_o
        gated, _ = gelu_two(d["gate"])
        low = (gated * n_o * d["gp"]).astype(BF)
        mixed_ref[:, c] = low
        mixed.append(low)
        so_ref[NA, :, c] = n_a
        so_ref[INVA, :, c] = inv_a
        so_ref[NO, :, c] = n_o
        so_ref[INVO, :, c] = inv_o
        so_ref[GATE, :, c] = d["gate"]
    return cat(mixed, 1)


def mixer_backward(dmixed, mixed_refs, inner_ref, small_ref, begin_cut, ig_ref, ms_ref):
    (kq_ref, x2_ref, g1_ref, y2_ref, d1_ref, ud2_ref, e1_ref, sm_ref, so_ref, sg_ref) = mixed_refs
    _, cut = begin_cut
    length = dmixed.shape[0]
    heads = inner_ref.shape[0] // 2
    pairs = heads // 2
    hid = inner_ref.shape[2]
    wide = heads * 64
    steps = length // (2 * MBT)
    rows = 2 * MBT
    past, near, past_t, near_t = masks(cut, length)
    hv = Halves()
    sg = sg_ref[...]
    rates = RATE * sg

    def by_head(fn):
        return [fn(slice(hid * i, hid * (i + 1)), i) for i in range(2)]

    st = []
    for p in range(pairs):
        c = slice(128 * p, 128 * p + 128)
        h = slice(2 * hid * p, 2 * hid * (p + 1))
        d = dict(c=c, h=h)
        d["w1"], d["w2"] = pair_weights(inner_ref, small_ref, heads, p, hv)
        g = small_ref[2:3, wide + 128 * p : wide + 128 * p + 128]
        gp = small_ref[2:3, 2 * wide + 128 * p : 2 * wide + 128 * p + 128]
        d["g"] = g
        d["r"] = [rates[:, 2 * p + i : 2 * p + i + 1] for i in range(2)]
        d["rp"] = hv.pack(d["r"][0], d["r"][1])
        kb = kq_ref[:, c]
        qb = kq_ref[:, wide + 128 * p : wide + 128 * p + 128]
        x2, g1, y2 = x2_ref[:, h], g1_ref[:, h], y2_ref[:, h]
        gz2 = sm_ref[GZ2, :, c]
        gz2b = gz2.astype(BF)
        g2b = (gz2 * d["rp"]).astype(BF)
        dm = dmixed[:, c]
        gate = so_ref[GATE, :, c]
        n_o, inv_o = so_ref[NO, :, c], so_ref[INVO, :, c]
        n_a, inv_a = so_ref[NA, :, c], so_ref[INVA, :, c]
        gated, gate_slope = gelu_two(gate)
        d["dgate"] = dm * n_o * gp * gate_slope
        drm = dm * gated
        d["dgp"] = jnp.sum(drm * n_o, axis=0, keepdims=True)
        dpg = drm * gp
        do = (dpg - n_o * hv.mean(dpg * n_o)) * inv_o
        dn = do * g
        both = hv.mean(cat([dn, dn * n_a], 0))
        da2 = (dn - both[:length] - n_a * both[length:]) * inv_a
        d["dg"] = jnp.sum(do * n_a, axis=0, keepdims=True)
        d["dbe"] = jnp.sum(do, axis=0, keepdims=True)
        d["db2"] = jnp.sum(da2, axis=0, keepdims=True)
        da2b = da2.astype(BF)
        da2m, g2m = hv.split(da2b), hv.split(g2b)
        km, qm = hv.split(kb), hv.split(qb)

        def weigh(mask, full, i):
            return (mask * full[length * i : length * (i + 1)]).astype(BF)

        p2 = dot_t(da2m, g2b)
        p2t = dot_t(g2m, da2b)
        dy2 = dot(da2b, d["w2"]) - cat(by_head(lambda e, i: dot(weigh(near, p2, i), x2[:, e])), 1)
        d["bx2"] = cat(by_head(lambda e, i: dot(weigh(near_t, p2t, i), y2[:, e])), 1)
        syt = cat(by_head(lambda e, i: (near_t * (dot_t(x2[:, e], y2[:, e]) + 1.0)).astype(BF)), 1)
        d["bg2"] = -dot(syt, da2m)
        da1 = dy2 * e1_ref[:, h].astype(F32)
        da1b = da1.astype(BF)
        d["db1"] = jnp.sum(da1, axis=0, keepdims=True)
        p1 = cat(by_head(lambda e, i: (near * dot_t(da1b[:, e], g1[:, e])).astype(BF)), 1)
        p1t = cat(by_head(lambda e, i: (near_t * dot_t(g1[:, e], da1b[:, e])).astype(BF)), 1)
        d["dq"] = do + dot_t(da1b, d["w1"]) - dot(p1, km)
        d["dk"] = -dot(p1t, qm)
        kq = dot_t(km, qb) + 1.0
        kk = dot_t(km, kb) + 1.0
        d["bg1"] = cat(by_head(lambda e, i: dot(weigh(near_t, kq, i), da1b[:, e])), 1)
        d["m1t"] = [weigh(past_t, kk, i) for i in range(2)]
        d["rx"] = by_head(lambda e, i: (past_t * (dot_t(x2[:, e], x2[:, e]) + 1.0)).astype(BF))
        ft = dot_t(g2m, gz2b)
        d["ft"] = [weigh(past_t, ft, i) for i in range(2)]
        d.update(x2=x2, y2=y2, g1=g1, g2b=g2b, g2m=g2m, gz2=gz2, gz2b=gz2b, gz2m=hv.split(gz2b))
        d.update(km=km, kb=kb, qb=qb, da1b=da1b, da2b=da2b)
        for name in ("z1", "z2", "u", "rg1", "rg2", "t"):
            d[name] = [None] * steps
        st.append(d)
    for s in reversed(range(steps)):
        sl = slice(rows * s, rows * s + rows)
        later = rows * (s + 1)
        for p in range(pairs):
            d = st[p]
            c, h = d["c"], d["h"]
            x2 = d["x2"]
            bg1, bg2, bx2 = -d["bg1"][sl], d["bg2"][sl], -d["bx2"][sl]
            if s < steps - 1:

                def full(parts):
                    done = parts[s + 1 :]
                    return cat([jnp.zeros((later, done[0].shape[1]), BF)] + done, 0)

                z1l, z2l, ul = full(d["z1"]), full(d["z2"]), full(d["u"])
                bg1 = bg1 - cat(by_head(lambda e, i: dot(d["m1t"][i][sl], z1l[:, e])), 1)
                xu = by_head(lambda e, i: (past_t[sl] * dot_t(x2[sl, e], ul[:, e])).astype(BF))
                lhs = cat([d["rx"][0][sl], d["rx"][1][sl]] + xu, 1)
                bg2 = bg2 - dot(lhs, cat([hv.split(z2l), d["gz2m"]], 0))
                gz = dot_t(hv.split(d["g2b"][sl]), z2l)
                bx2 = bx2 - cat(
                    by_head(
                        lambda e, i: dot(
                            cat([(past_t[sl] * gz[rows * i : rows * (i + 1)]).astype(BF), d["ft"][i][sl]], 1),
                            cat([x2[:, e], ul[:, e]], 0),
                        )
                    ),
                    1,
                )
            r0, r1 = d["r"][0][sl], d["r"][1][sl]
            dgz1 = cat([bg1[:, :hid] * r0, bg1[:, hid:] * r1], 1)
            slope = d1_ref[sl, h].astype(F32)
            du = dgz1 * slope
            dub = du.astype(BF)
            dz1 = dgz1 * ud2_ref[sl, h].astype(F32)
            dgz2 = bg2 * d["rp"][sl] + dot_t(dub, d["w2"])
            if s:
                hm = by_head(lambda e, i: (past[sl] * dot_t(dub[:, e], x2[:, e])).astype(BF))
                dgz2 = dgz2 - dot(cat(hm, 1), d["g2m"])
            n, inv = sm_ref[NRM, sl, c], sm_ref[INV, sl, c]
            mis, mn = sm_ref[MIS, sl, c], sm_ref[MEANN, sl, c]
            g = d["g"]
            e = dgz2 * inv
            three = hv.mean(cat([e, e * n, dgz2 * d["gz2"][sl]], 0))
            dmis = e - three[:rows] - n * three[rows : 2 * rows]
            t = dmis * g
            dn = t * g - e * mn - mis * g * three[rows : 2 * rows]
            two = hv.mean(cat([dn, dn * n], 0))
            dz2 = inv * (dn - two[:rows] - n * (two[rows:] + three[2 * rows :]))
            d["dg"] = d["dg"] + jnp.sum(t * n + dmis * mis, axis=0, keepdims=True)
            d["dbe"] = d["dbe"] + jnp.sum(t, axis=0, keepdims=True)
            d["db2"] = d["db2"] + jnp.sum(dz2, axis=0, keepdims=True)
            dz2b = dz2.astype(BF)
            dx2 = bx2 + dot(dz2b, d["w2"])
            if s:
                j = dot_t(hv.split(dz2b), d["g2b"])
                dx2 = dx2 - cat(
                    by_head(lambda e, i: dot((past[sl] * j[rows * i : rows * (i + 1)]).astype(BF), x2[:, e])), 1
                )
            dz1 = dz1 + dx2 * slope
            d["db1"] = d["db1"] + jnp.sum(dz1, axis=0, keepdims=True)
            d["z1"][s], d["z2"][s], d["u"][s] = dz1.astype(BF), dz2b, dub
            d["rg1"][s], d["rg2"][s], d["t"][s] = bg1, bg2, t
    parts = [[], [], [], []]
    rate_cols = []
    for p in range(pairs):
        d = st[p]
        z1, z2, u = cat(d["z1"], 0), cat(d["z2"], 0), cat(d["u"], 0)
        t = cat(d["t"], 0)
        g1 = d["g1"]
        both = cat(
            by_head(
                lambda e, i: (past * dot_t(z1[:, e], g1[:, e]) + past_t * dot_t(g1[:, e], z1[:, e])).astype(BF)
            ),
            1,
        )
        dk = d["dk"] + t + dot_t(z1, d["w1"]) - dot(both, d["km"])
        for i, value in enumerate((d["dq"], dk, -t, d["dgate"])):
            parts[i].append(value.astype(BF))
        dw1 = tdot(cat([d["kb"], d["qb"]], 0), cat([z1, d["da1b"]], 0))
        dw2 = tdot(cat([z2, d["da2b"], d["gz2b"]], 0), cat([d["x2"], d["y2"], u], 0))
        for i in range(2):
            row = 64 * (2 * p + i)
            ig_ref[row : row + 64, :] = dw1[64 * i : 64 * i + 64, hid * i : hid * (i + 1)]
            row = row + 64 * heads
            ig_ref[row : row + 64, :] = dw2[64 * i : 64 * i + 64, hid * i : hid * (i + 1)]
            row = HIDDEN_ROW + 2 * p + i
            ms_ref[row : row + 1, :] = d["db1"][:, hid * i : hid * (i + 1)]
        one = cat(d["rg1"], 0) * g1.astype(F32)
        two = cat(d["rg2"], 0) * d["g2b"].astype(F32)
        two = cat([jnp.where(hv.left, two, 0.0), jnp.where(hv.left, 0.0, two)], 1)
        for i in range(2):
            whole = one[:, hid * i : hid * i + 128] + one[:, hid * i + 128 : hid * (i + 1)]
            whole = whole + two[:, 128 * i : 128 * (i + 1)]
            rate_cols.append(jnp.sum(whole, axis=-1, keepdims=True))
        for j, name in enumerate(("db2", "dg", "dgp", "dbe")):
            piece = 3 * j + p
            row = HEAD_ROW + piece // 2
            ms_ref[row : row + 1, 128 * (piece % 2) : 128 * (piece % 2) + 128] = d[name]
    lane = lax.broadcasted_iota(jnp.int32, (1, 16), 1)
    dlog = jnp.zeros((length, 16), F32)
    for i, col in enumerate(rate_cols):
        dlog = dlog + jnp.where(lane == i, col, 0.0)
    dlog = dlog * (1.0 - sg)
    ms_ref[OFFSET_ROW : OFFSET_ROW + 1, 0:16] = jnp.sum(dlog, axis=0, keepdims=True)
    dmix = [cat(x, 1) for x in parts]
    return dmix, dlog.astype(BF)


def ka_body(layer, *args):
    if layer == 0:
        dl_ref, li_ref = args[:2]
        rest = args[2:]
    else:
        dl_ref, h1_ref, fo_ref, fr_ref = args[:4]
        rest = args[4:]
    wrefs, rest = rest[:10], rest[10:]
    if layer == 1:
        lo_ref, rest = rest[0], rest[1:]
    hb_ref, x1_ref, att_ref = rest[:3]
    saves, scratch = rest[3:15], rest[15:]
    mix_v, inner_v, small_v, rate_v, out_v, sems = scratch
    pick = Pick(layer, sems)
    c_small = pick.start(wrefs[0], wrefs[1], small_v)
    c_mix = pick.start(wrefs[2], wrefs[3], mix_v)
    c_rate = pick.start(wrefs[4], wrefs[5], rate_v)
    c_inner = pick.start(wrefs[6], wrefs[7], inner_v)
    c_out = pick.start(wrefs[8], wrefs[9], out_v)
    length = hb_ref.shape[0]
    steps = length // (2 * MBT)
    begin, cut = doc_places(dl_ref, steps)
    places = block_starts(begin, steps)
    if layer == 0:
        low = gather_rows(li_ref, lax.axis_index("segment"), places)
    else:
        low = (h1_ref[...] + (fo_ref[...].astype(F32) + fr_ref[...].astype(F32))).astype(BF)
        scatter_rows(lo_ref, places, low)
        lo_ref.send()
    hb_ref[...] = low
    hb_ref.send()
    h = low.astype(F32)
    inv = rms_inv(h)
    c_small.wait()
    x_one = (h * inv * small_v[1:2, 0 : h.shape[1]]).astype(BF)
    x1_ref[...] = x_one
    x1_ref.send()
    c_mix.wait()
    c_rate.wait()
    c_inner.wait()
    mixed = mixer_forward(saves, x_one, mix_v, rate_v, inner_v, small_v, (begin, cut), None)
    c_out.wait()
    att_ref[...] = dot(mixed, out_v[...]).astype(BF)


def ffn_forward(h1, small_v, sw_v, dn_v, copies):
    width = h1.shape[1]
    inv = rms_inv(h1)
    x2 = (h1 * inv * small_v[1:2, width : 2 * width]).astype(BF)
    copies[0].wait()
    up_at = sw_v.shape[1] // 2
    gate = dot(x2, sw_v[:, :up_at])
    up = dot(x2, sw_v[:, up_at:])
    sgm = 1.0 / (1.0 + jnp.exp(-gate))
    silu = gate * sgm
    slope = up * (sgm * (1.0 + gate * (1.0 - sgm)))
    hidden = (silu * up).astype(BF)
    copies[1].wait()
    feed = dot(hidden, dn_v[...]).astype(BF)
    return x2, hidden, slope, silu, feed


def ffn_backward(dfe, slope, silu, sw_v, dn_v):
    up_at = sw_v.shape[1] // 2
    dh = dot_t(dfe, dn_v[...])
    dg, du = (dh * slope).astype(BF), (dh * silu).astype(BF)
    dx = dot_t(dg, sw_v[:, :up_at]) + dot_t(du, sw_v[:, up_at:])
    return dg, du, dx.astype(BF)


def pack_ffn(keep_ref, send_ref, x2, dg, du, hidden, dfe):
    first = lax.axis_index("segment") == 0
    width, wide = x2.shape[1], dg.shape[1]
    half = wide // 2

    def put(ref, grad, hid):
        ref[:, 0:width] = x2
        ref[:, width : width + wide] = grad
        ref[:, width + wide : width + wide + half] = hid
        ref[:, width + wide + half :] = dfe

    @pl.when(first)
    def _():
        put(keep_ref, dg, hidden[:, :half])
        put(send_ref, du, hidden[:, half:])

    @pl.when(jnp.logical_not(first))
    def _():
        put(keep_ref, du, hidden[:, half:])
        put(send_ref, dg, hidden[:, :half])


def kf_body(hb_ref, ao_ref, ar_ref, s_own, s_oth, w_own, w_oth, d_own, d_oth,
            h1_ref, x2_ref, hid_ref, sl_ref, si_ref, fe_ref, small_v, sw_v, dn_v, sems):
    pick = Pick(0, sems)
    c_small = pick.start(s_own, s_oth, small_v)
    copies = [pick.start(w_own, w_oth, sw_v), pick.start(d_own, d_oth, dn_v)]
    h1 = hb_ref[...].astype(F32) + (ao_ref[...].astype(F32) + ar_ref[...].astype(F32))
    h1_ref[...] = h1
    h1_ref.send()
    c_small.wait()
    x2, hidden, slope, silu, feed = ffn_forward(h1, small_v, sw_v, dn_v, copies)
    x2_ref[...] = x2
    hid_ref[...] = hidden
    sl_ref[...] = slope.astype(BF)
    si_ref[...] = silu.astype(BF)
    fe_ref[...] = feed


def kfb_body(dl_ref, ct_ref, hb_ref, ao_ref, ar_ref, s_own, s_oth, w_own, w_oth, d_own, d_oth,
             h1_ref, fe_ref, dxt_ref, dfe_ref, keep_ref, send_ref, small_v, sw_v, dn_v, sems):
    pick = Pick(1, sems)
    c_small = pick.start(s_own, s_oth, small_v)
    copies = [pick.start(w_own, w_oth, sw_v), pick.start(d_own, d_oth, dn_v)]
    length = hb_ref.shape[0]
    steps = length // (2 * MBT)
    begin, _ = doc_places(dl_ref, steps)
    dfe = gather_rows(ct_ref, lax.axis_index("segment"), block_starts(begin, steps))
    dfe_ref[...] = dfe
    h1 = hb_ref[...].astype(F32) + (ao_ref[...].astype(F32) + ar_ref[...].astype(F32))
    h1_ref[...] = h1
    h1_ref.send()
    c_small.wait()
    x2, hidden, slope, silu, feed = ffn_forward(h1, small_v, sw_v, dn_v, copies)
    fe_ref[...] = feed
    dg, du, dx = ffn_backward(dfe, slope, silu, sw_v, dn_v)
    dxt_ref[...] = dx
    pack_ffn(keep_ref, send_ref, x2, dg, du, hidden, dfe)


def norm_back(dx, x, gain, base):
    inv = rms_inv(x)
    e = dx * gain
    grad = base + e * inv - x * (jnp.mean(e * x, axis=-1, keepdims=True) * inv * inv * inv)
    gain_grad = jnp.sum(dx * x * inv, axis=0, keepdims=True)
    return grad, gain_grad


def kbf_body(dl_ref, hb_ref, dh_ref, xo_ref, xr_ref, t_own, t_oth, x2_ref, hid_ref, sl_ref, si_ref,
             w_own, w_oth, d_own, d_oth,
             ig_ref, gg_ref, dfe_ref, dxt_ref, keep_ref, send_ref, small_v, sw_v, dn_v, sems, sems_two):
    above = Pick(1, sems)
    c_small = above.start(t_own, t_oth, small_v)
    pick = Pick(0, sems_two)
    copies = [pick.start(d_own, d_oth, dn_v), pick.start(w_own, w_oth, sw_v)]
    length, width = hb_ref.shape
    steps = length // (2 * MBT)
    begin, _ = doc_places(dl_ref, steps)
    dx = xo_ref[...].astype(F32) + xr_ref[...].astype(F32)
    c_small.wait()
    grad, gain = norm_back(dx, hb_ref[...].astype(F32), small_v[1:2, 0:width], dh_ref[...])
    scatter_rows(ig_ref, block_starts(begin, steps), grad)
    ig_ref.send()
    gg_ref[...] = gain
    dfe = grad.astype(BF)
    dfe_ref[...] = dfe
    for c in copies:
        c.wait()
    dg, du, dxt = ffn_backward(dfe, sl_ref[...].astype(F32), si_ref[...].astype(F32), sw_v, dn_v)
    dxt_ref[...] = dxt
    pack_ffn(keep_ref, send_ref, x2_ref[...], dg, du, hid_ref[...], dfe)


def stat_rows(own, other, dp):
    zero = lax.axis_index("tensor") == 0
    low, high = jnp.where(zero, own, other), jnp.where(zero, other, own)
    line = cat([low[0:1], high[0:1], low[1:2], high[1:2], jnp.zeros((1, 64), F32)], 1)
    core = lax.axis_index("segment")
    line = cat([jnp.where(core == 0, line, 0.0), jnp.where(core == 0, 0.0, line)], 1)
    row = lax.broadcasted_iota(jnp.int32, (dp, 256), 0)
    return jnp.where(row == lax.axis_index("dp"), line, 0.0)


def kba_body(layer, dp, dl_ref, xo_ref, xr_ref, dy_ref, h1_ref, x1_ref, mixed_ref, so_ref, sr_ref, *rest):
    saves, rest = rest[:10], rest[10:]
    wrefs, rest = rest[:10], rest[10:]
    dh_ref, dxo_ref, keep_ref, send_ref, ig_ref, ms_ref, mix_v, inner_v, small_v, rate_v, out_v, sems = rest
    pick = Pick(layer, sems)
    kq, x2, g1, y2, d1, ud2, e1, sm, so, sg = saves
    c_small = pick.start(wrefs[0], wrefs[1], small_v)
    h1_ref.start()
    c_out = pick.start(wrefs[8], wrefs[9], out_v)
    c_inner = pick.start(wrefs[6], wrefs[7], inner_v)
    for ref in (so, sg, sm, kq, x2, g1, y2, e1, d1, ud2, x1_ref, mixed_ref):
        ref.start()
    c_mix = pick.start(wrefs[2], wrefs[3], mix_v)
    c_rate = pick.start(wrefs[4], wrefs[5], rate_v)
    length, width = h1_ref.shape
    steps = length // (2 * MBT)
    place = doc_places(dl_ref, steps)
    dx = xo_ref[...].astype(F32) + xr_ref[...].astype(F32)
    c_small.wait()
    dh, gain = norm_back(dx, h1_ref[...], small_v[1:2, width : 2 * width], dy_ref[...].astype(F32))
    dh_ref[...] = dh
    dh_ref.send()
    ms_ref[...] = jnp.zeros(ms_ref.shape, F32)
    at = slice(2 * layer, 2 * layer + 2)
    ms_ref[STAT_ROW : STAT_ROW + dp, :] = stat_rows(so_ref[at, :], sr_ref[at, :], dp)
    for j in range(3):
        ms_ref[GAIN_ROW + j : GAIN_ROW + j + 1, :] = gain[:, 256 * j : 256 * j + 256]
    da = dh.astype(BF)
    c_out.wait()
    c_inner.wait()
    dmixed = dot_t(da, out_v[...])
    dmix, dlog = mixer_backward(dmixed, saves, inner_v, small_v, place, ig_ref, ms_ref)
    x1 = x1_ref[...]
    drate = tdot(dlog, x1)
    heads = inner_v.shape[0] // 2
    for j in range(3):
        row = RATE_ROW + heads * j
        ms_ref[row : row + heads, :] = drate[:heads, 256 * j : 256 * j + 256]
    c_mix.wait()
    c_rate.wait()
    dxo_ref[...] = (dot_t(cat(dmix, 1), mix_v[...]) + dot(dlog, rate_v[...])).astype(BF)
    first = lax.axis_index("segment") == 0
    half = width // 2
    wide = 2 * dmix[0].shape[1]
    mixed = mixed_ref[...]

    def put(ref, one, two, att):
        ref[:, 0:width] = x1
        ref[:, width : width + wide // 2] = one
        ref[:, width + wide // 2 : width + wide] = two
        ref[:, width + wide : width + wide + mixed.shape[1]] = mixed
        ref[:, width + wide + mixed.shape[1] :] = att

    @pl.when(first)
    def _():
        put(keep_ref, dmix[0], dmix[1], da[:, :half])
        put(send_ref, dmix[2], dmix[3], da[:, half:])

    @pl.when(jnp.logical_not(first))
    def _():
        put(keep_ref, dmix[2], dmix[3], da[:, half:])
        put(send_ref, dmix[0], dmix[1], da[:, :half])


def ke_body(dl_ref, hb_ref, dh_ref, xo_ref, xr_ref, s_own, s_oth, ig_ref, gg_ref, small_v, sems):
    pick = Pick(0, sems)
    c_small = pick.start(s_own, s_oth, small_v)
    length, width = hb_ref.shape
    steps = length // (2 * MBT)
    begin, _ = doc_places(dl_ref, steps)
    dx = xo_ref[...].astype(F32) + xr_ref[...].astype(F32)
    c_small.wait()
    grad, gain = norm_back(dx, hb_ref[...].astype(F32), small_v[1:2, 0:width], dh_ref[...])
    scatter_rows(ig_ref, block_starts(begin, steps), grad)
    gg_ref[...] = gain


def grad_body(kf_ref, rf_ref, ka_ref, ra_ref, ik_ref, ir_ref, out_ref):
    width, wide = 768, 1024
    half = wide // 2

    def both(one, two, low, high):
        return cat([one[:, low:high], two[:, low:high]], 0)

    base = lax.axis_index("segment") * 384
    for k in range(2):
        rows = slice(384 * k, 384 * (k + 1))
        x = both(kf_ref, rf_ref, 384 * k, 384 * (k + 1))
        out_ref[rows, 0:wide] = tdot(x, both(kf_ref, rf_ref, width, width + wide)).astype(BF)
        x = both(ka_ref, ra_ref, 384 * k, 384 * (k + 1))
        out_ref[rows, wide:] = tdot(x, both(ka_ref, ra_ref, width, 2 * width)).astype(BF)
        out_ref.send(384 * k, 384 * (k + 1))
    down = tdot(both(kf_ref, rf_ref, width + wide, width + wide + half),
                both(kf_ref, rf_ref, width + wide + half, 2 * width + wide + half)).astype(BF)
    out_ref[768:1152, 0:width] = down[0:384]
    for k in range(3):
        out_ref[768 + 128 * k : 768 + 128 * (k + 1), width:wide] = down[384:512, 256 * k : 256 * (k + 1)]
    out = tdot(both(ka_ref, ra_ref, 1536, 1920), both(ka_ref, ra_ref, 1920, 2304)).astype(BF)
    out_ref[768:960, wide : wide + 384] = out[0:192]
    out_ref[768:960, wide + 384 :] = out[192:384]
    for k in range(3):
        rows = pl.ds(pl.multiple_of(base + 128 * k, 128), 128)
        out_ref[960:1088, wide + 256 * k : wide + 256 * (k + 1)] = (ik_ref[rows, :] + ir_ref[rows, :]).astype(BF)
    out_ref[1088:PACK_ROWS, wide:] = jnp.zeros((PACK_ROWS - 1088, width), BF)
    out_ref.send(768, PACK_ROWS)


def final_body(turn, in_ref, sw_ref, dn_ref, mx_ref, ow_ref, ex_ref, co_ref, buf, sems):
    copies = []
    rows = PACK_ROWS // 8
    for k in range(8):
        at = rows * k
        if turn:
            at = pl.multiple_of(lax.rem(k + lax.axis_index("segment"), 8) * rows, 16)
        copies.append(pltpu.make_async_copy(in_ref.at[pl.ds(at, rows)], buf.at[rows * k : rows * (k + 1)], sems.at[k]))
    for copy in copies:
        copy.start()
    ready = 0

    def wait(upto):
        nonlocal ready
        while ready * rows < upto:
            copies[ready].wait()
            ready += 1

    for h in range(4):
        wait(192 * (h + 1))
        part = slice(192 * h, 192 * (h + 1))
        for c in range(2):
            base = 1792 * c
            sw_ref[part, c, :] = buf[part, base : base + 1024].astype(F32)
            for j in range(2):
                at = base + 1024 + 384 * j
                mx_ref[part, 2 * c + j, :] = buf[part, at : at + 384].astype(F32)
        sw_ref.send(192 * h, 192 * (h + 1))
        mx_ref.send(192 * h, 192 * (h + 1))
    wait(PACK_ROWS)
    for c in range(2):
        base = 1792 * c
        dn_ref[512 * c : 512 * c + 384, :] = buf[768:1152, base : base + 768].astype(F32)
        for k in range(3):
            part = buf[768 + 128 * k : 768 + 128 * (k + 1), base + 768 : base + 1024]
            dn_ref[512 * c + 384 : 512 * (c + 1), 256 * k : 256 * (k + 1)] = part.astype(F32)
        dn_ref.send(512 * c, 512 * (c + 1))
        base = base + 1024
        for j in range(2):
            at = base + 384 * j
            ow_ref[192 * j : 192 * (j + 1), 384 * c : 384 * (c + 1)] = buf[768:960, at : at + 384].astype(F32)
        ref = (ex_ref, co_ref)[c]
        for k in range(3):
            ref[128 * k : 128 * (k + 1), :] = buf[960:1088, base + 256 * k : base + 256 * (k + 1)].astype(F32)


class Loaded:
    def __init__(self, src, buf, sem):
        self.buf, self.shape = buf, buf.shape
        self.copy = pltpu.make_async_copy(src, buf, sem)
        self.started, self.waiting = False, True

    def start(self):
        if not self.started:
            self.copy.start()
            self.started = True

    def __getitem__(self, at):
        if self.waiting:
            self.start()
            self.copy.wait()
            self.waiting = False
        return self.buf[at]


class Stored:
    def __init__(self, dst, buf, sems):
        self.dst, self.buf, self.sems, self.shape = dst, buf, sems, buf.shape
        self.parts = []

    def __setitem__(self, at, value):
        self.buf[at] = value

    def send(self, low=None, high=None):
        k = len(self.parts)
        if low is None:
            copy = pltpu.make_async_copy(self.buf, self.dst, self.sems.at[k])
        else:
            at = slice(low, high)
            copy = pltpu.make_async_copy(self.buf.at[at], self.dst.at[at], self.sems.at[k])
        copy.start()
        self.parts.append(copy)

    def wait(self):
        for copy in self.parts:
            copy.wait()


def in_hbm(x):
    return pltpu.with_memory_space_constraint(x, pltpu.HBM)


def call(body, name, ins, specs, outs, scratch=(), deps=(), vmem=36, lazy=False):
    ins = [in_hbm(x) if spec is LOAD or spec is HBM else x for x, spec in zip(ins, specs)]
    deps = [in_hbm(x) for x in deps]
    have, extra, results, own = len(ins), len(deps), len(outs), len(scratch)
    loads = [k for k, spec in enumerate(specs) if spec is LOAD]
    stores = [k for k, out in enumerate(outs) if len(out) == 3]
    buffers = [pltpu.VMEM(ins[k].shape, ins[k].dtype) for k in loads]
    buffers += [pltpu.VMEM(outs[k][0], outs[k][1]) for k in stores]
    sems = [pltpu.SemaphoreType.DMA((max(1, len(loads)),))]
    sems += [pltpu.SemaphoreType.DMA((outs[k][2],)) for k in stores]

    def inside(*refs):
        operands, rest = list(refs[:have]), refs[have + extra :]
        written, rest = list(rest[:results]), rest[results:]
        own_refs, rest = rest[:own], rest[own:]
        bufs, (load_sems, *store_sems) = rest[: len(buffers)], rest[len(buffers) :]
        for i, k in enumerate(loads):
            operands[k] = Loaded(operands[k], bufs[i], load_sems.at[i])
            if not lazy:
                operands[k].start()
        done = []
        for i, k in enumerate(stores):
            written[k] = Stored(written[k], bufs[len(loads) + i], store_sems[i])
            done.append(written[k])
        body(*operands, *written, *own_refs)
        for one in done:
            if not one.parts:
                one.send()
        for one in done:
            one.wait()
        for k in loads:
            operands[k][0:1]

    return pl.pallas_call(
        inside,
        out_shape=[(pltpu.HBM if len(o) == 3 else jax.ShapeDtypeStruct)(o[0], o[1]) for o in outs],
        in_specs=[HBM if spec is LOAD else spec for spec in specs] + [HBM] * extra,
        out_specs=[HBM if len(o) == 3 else VMEM for o in outs],
        scratch_shapes=list(scratch) + buffers + sems,
        compiler_params=pltpu.CompilerParams(vmem_limit_bytes=vmem * 1024 * 1024),
        cost_estimate=pl.CostEstimate(flops=0, bytes_accessed=0, transcendentals=0),
        name=name,
    )(*ins, *deps)


def gate_body(*refs):
    pass


def pack_body(hb_ref, ng_ref, ro_ref, rb_ref, hg_ref, hs_ref, rw_ref, ex_ref, co_ref, small_ref, rate_ref, inner_ref):
    heads, hid, width = ex_ref.shape[0], ex_ref.shape[2], ng_ref.shape[1]
    wide = 64 * heads
    small_ref[...] = jnp.zeros(small_ref.shape, F32)
    for k in range(2):
        small_ref[1:2, width * k : width * (k + 1)] = ng_ref[k : k + 1, :]
    small_ref[3:4, 0:heads] = ro_ref[...]
    for h in range(heads):
        small_ref[0:1, hid * h : hid * (h + 1)] = hb_ref[h]
        at = slice(64 * h, 64 * (h + 1))
        small_ref[2:3, at] = rb_ref[h]
        for k in range(2):
            small_ref[2:3, wide * (k + 1) + 64 * h : wide * (k + 1) + 64 * (h + 1)] = hg_ref[h, k : k + 1, :]
        small_ref[2:3, wide * 3 + 64 * h : wide * 3 + 64 * (h + 1)] = hs_ref[h]
    rate_ref[...] = jnp.zeros(rate_ref.shape, BF)
    rate_ref[0:heads, :] = rw_ref[...]
    inner_ref[0:heads] = ex_ref[...].astype(BF)
    inner_ref[heads:] = co_ref[...].astype(BF)


def swap(value, axis):
    return lax.ppermute(value, axis, [(0, 1), (1, 0)])


def shards(
    layer_input, doc_lengths, norm_gains, mixing, rate_weight, rate_offset, expand, hidden_bias, contract,
    result_bias, head_gains, head_shift, output_proj, swiglu, down_proj, cotangent,
):
    micro, _, length, width = layer_input.shape
    heads = rate_weight.shape[2]
    hid = expand.shape[3]
    wide = heads * 64
    ff = down_proj.shape[1]
    first = lax.axis_index("segment") == 0
    dl = doc_lengths.reshape(micro, 3)
    li = layer_input.reshape(micro, length, width)
    ct = cotangent.reshape(micro, length, width)
    mix = mixing[0].reshape(width, -1)
    ow = output_proj[0]
    dn = down_proj[0]
    small, rate, inner = call(
        pack_body, "pack",
        [hidden_bias.reshape(heads, 1, hid), norm_gains[0], rate_offset, result_bias.reshape(heads, 1, 64),
         jnp.transpose(head_gains[0], (1, 0, 2)), head_shift.reshape(heads, 1, 64), rate_weight[0].T, expand[0],
         jnp.swapaxes(contract[0], 1, 2)],
        [VMEM] * 9, [((4, heads * hid), F32), ((16, width), BF), ((2 * heads, 64, hid), BF)])
    sw = swiglu[0].reshape(width, -1)

    def both(x):
        return in_hbm(x), in_hbm(swap(x, "segment"))

    small_p, mix_p, rate_p, inner_p, ow_p = both(small), both(mix), both(rate), both(inner), both(ow)
    sw = pl.pallas_call(
        gate_body, out_shape=pltpu.HBM(sw.shape, BF), in_specs=[HBM] * 6, out_specs=HBM,
        input_output_aliases={0: 0}, name="gate",
    )(sw, *[in_hbm(pair[1]) for pair in (small_p, mix_p, rate_p, inner_p, ow_p)])
    sw_p, dn_p = both(sw), both(dn)
    att_w = small_p + mix_p + rate_p + inner_p + ow_p
    tok = (length, width)
    save_shapes = [
        ((length, wide), BF, 1), ((2, 16), F32), ((length, 2 * wide), BF, 1),
        ((length, heads * hid), BF, 1), ((length, heads * hid), BF, 1), ((length, heads * hid), BF, 1),
        ((length, heads * hid), BF, 1), ((length, heads * hid), BF, 1), ((length, heads * hid), BF, 1),
        ((5, length, wide), F32, 1), ((5, length, wide), F32, 1), ((length, 16), F32, 1),
    ]
    sem = pltpu.SemaphoreType.DMA
    att_scratch = [
        pltpu.VMEM(mix.shape, BF), pltpu.VMEM(inner.shape, BF), pltpu.VMEM(small.shape, F32),
        pltpu.VMEM(rate.shape, BF), pltpu.VMEM(ow.shape, BF), sem((5,)),
    ]
    ffn_scratch = [pltpu.VMEM(small.shape, F32), pltpu.VMEM(sw.shape, BF), pltpu.VMEM(dn.shape, BF)]

    def ka(layer, ins):
        outs = [(tok, BF, 1), (tok, BF, 1), (tok, BF)] + save_shapes
        specs = [SMEM, LOAD] + [VMEM] * (len(ins) - 2) + [HBM] * 10
        if layer == 1:
            outs = [(tok, BF, 1)] + outs
        return call(functools.partial(ka_body, layer), f"mixer_fwd{layer}", list(ins) + list(att_w), specs, outs,
                    att_scratch)

    def exchange(x):
        return x, swap(x, "tensor")

    h0, x1_0, att, *save0 = ka(0, (dl, li))
    mixed0, stats0, save0 = save0[0], save0[1], save0[2:]
    ao, ar = exchange(att)
    h1_0, x2_0, hid_0, sl_0, si_0, fe = call(
        kf_body, "ffn_fwd0", [h0, ao, ar, *small_p, *sw_p, *dn_p], [LOAD] + [VMEM] * 2 + [HBM] * 6,
        [(tok, F32, 1), (tok, BF, 1)] + [((length, ff), BF, 1)] * 3 + [(tok, BF)], ffn_scratch + [sem((3,))])
    fo, fr = exchange(fe)
    lo0, hm, x1_1, att, *save1 = ka(1, (dl, h1_0, fo, fr))
    mixed1, stats1, save1 = save1[0], save1[1], save1[2:]
    ao, ar = exchange(att)
    pack_f = (length, 2 * width + ff + ff // 2)
    h1_1, fe, dxt, dfe1, keep, send = call(
        kfb_body, "ffn_both1", [dl, ct, hm, ao, ar, *small_p, *sw_p, *dn_p], [SMEM, LOAD, LOAD] + [VMEM] * 2 + [HBM] * 6,
        [(tok, F32, 1), (tok, BF), (tok, BF), (tok, BF), (pack_f, BF, 1), (pack_f, BF)],
        ffn_scratch + [sem((3,))])

    dp = lax.axis_size("dp")
    ring = [0, 2, 4, 6, 7, 5, 3, 1] if dp == 8 else list(range(dp))

    stats = cat([stats0, stats1], 0)
    stats_in = swap(stats, "tensor")
    xo, xr = exchange(dxt)
    fo, fr = exchange(fe)
    pack_a = (length, width + 2 * wide + wide + width // 2)

    def kba(layer, xo, xr, dy, h1, x1, mixed, save, deps=()):
        return call(functools.partial(kba_body, layer, dp), f"mixer_bwd{layer}",
                    [dl, xo, xr, dy, h1, x1, mixed, stats, stats_in, *save, *att_w],
                    [SMEM] + [VMEM] * 3 + [LOAD] * 3 + [VMEM] * 2 + [LOAD] * 10 + [HBM] * 10,
                    [(tok, F32, 1), (tok, BF), (pack_a, BF, 1), (pack_a, BF), ((2 * wide, hid), F32, 1),
                     ((STAT_ROW + dp, hid), F32)],
                    att_scratch, deps, lazy=True)

    turn = 1 if dp == 8 else 0

    def reduced(keep_f, recv_f, keep_a, send_a, ig, by, deps=()):
        (pack,) = call(grad_body, "grads",
                       [keep_f, recv_f, keep_a, swap(send_a, "segment"), ig, swap(ig, "segment")], [LOAD] * 6,
                       [((PACK_ROWS, ff + width), BF, 3)], (), deps)
        return pack, lax.psum_scatter(pack, "dp", scatter_dimension=0, axis_index_groups=[ring[by:] + ring[:by]], tiled=True)

    keep_f = keep
    recv_f = swap(send, "segment")
    dh, dxo, keep, send, ig, misc1 = kba(1, xo, xr, dfe1, h1_1, x1_1, mixed1, save1)
    xo, xr = exchange(dxo)
    pack1, part1 = reduced(keep_f, recv_f, keep, send, ig, turn)
    ig1, gg1, dfe0, dxt, keep_f, send_f = call(
        kbf_body, "ffn_bwd0",
        [dl, hm, dh, xo, xr, *small_p, x2_0, hid_0, sl_0, si_0, *sw_p, *dn_p],
        [SMEM, LOAD, LOAD] + [VMEM] * 2 + [HBM] * 2 + [LOAD] * 4 + [HBM] * 4,
        [(tok, F32, 1), ((1, width), F32), (tok, BF), (tok, BF), (pack_f, BF, 1), (pack_f, BF)],
        ffn_scratch + [sem((1,)), sem((2,))], (pack1,))
    recv_f = swap(send_f, "segment")
    xo, xr = exchange(dxt)
    dh, dxo, keep, send, ig, misc0 = kba(0, xo, xr, dfe0, h1_0, x1_0, mixed0, save0)
    xo, xr = exchange(dxo)
    pack0, part0 = reduced(keep_f, recv_f, keep, send, ig, 0, () if turn else (part1,))
    ig0, gg0 = call(ke_body, "input_grad0", [dl, h0, dh, xo, xr, *small_p],
                    [SMEM, LOAD, LOAD] + [VMEM] * 2 + [HBM] * 2, [(tok, F32, 1), ((1, width), F32)], [pltpu.VMEM(small.shape, F32), sem((1,))], (pack0,))

    left = jnp.where(first, part0, lax.ppermute(part1, "segment", [(0, 1)]))
    right = jnp.where(first, lax.ppermute(part0, "segment", [(1, 0)]), part1)
    whole = lax.all_gather(cat([left, right], 1), "dp", axis=0, axis_index_groups=[ring], tiled=True)

    def lo1_body(dl_ref, h1_ref, fo_ref, fr_ref, lo_ref):
        begin, _ = doc_places(dl_ref, length // (2 * MBT))
        low = (h1_ref[...] + (fo_ref[...].astype(F32) + fr_ref[...].astype(F32))).astype(BF)
        scatter_rows(lo_ref, block_starts(begin, length // (2 * MBT)), low)

    (lo1,) = call(lo1_body, "output1", [dl, h1_1, fo, fr], [SMEM, LOAD] + [VMEM] * 2, [(tok, BF, 1)], (), (pack0,))

    def two_rows(zero, one):
        mine, theirs = jnp.where(first, zero, one), swap(jnp.where(first, one, zero), "segment")
        return jnp.where(first, jnp.stack([mine, theirs]), jnp.stack([theirs, mine]))[None, :, None]

    layer_output = two_rows(lo0, lo1)
    input_grads = two_rows(ig0, ig1)
    total = cat([misc0, misc1, gg0.reshape(3, hid), gg1.reshape(3, hid)], 0)
    total = total + swap(total, "segment")
    for k in range(dp.bit_length() - 1):
        total = total + lax.ppermute(total, "dp", [(i, i ^ (1 << k)) for i in range(dp)])
    rows = STAT_ROW + dp
    tail = total[2 * rows :]
    misc = jnp.where(first, total[:rows], total[rows : 2 * rows])
    gain_one = jnp.where(first, tail[:3], tail[3:]).reshape(width)
    g_rate = cat([misc[RATE_ROW + heads * j : RATE_ROW + heads * (j + 1)] for j in range(3)], 1).T[None]
    g_hidden = misc[HIDDEN_ROW : HIDDEN_ROW + heads][None]
    tail = misc[HEAD_ROW : HEAD_ROW + 6].reshape(4, heads, 64)
    g_result, g_heads, g_shift = tail[0][None], tail[1:3][None], tail[3][None]
    g_offset = misc[OFFSET_ROW, :heads][None]
    g_gains = jnp.stack([gain_one, misc[GAIN_ROW : GAIN_ROW + 3].reshape(width)])[None]
    rate_stats = misc[STAT_ROW:].reshape(dp, micro, 128)[:, :, :64].reshape(dp, micro, 2, 2, 16)
    rate_stats = jnp.transpose(rate_stats[..., :heads], (1, 0, 2, 3, 4)).reshape(1, micro, dp, 2, 2 * heads)
    g_sw, g_dn, g_mix, g_out, g_expand, g_contract = call(
        functools.partial(final_body, turn), "final", [whole], [HBM],
        [((width, 2, ff), F32, 4), ((ff, width), F32, 2), ((width, 4, wide), F32, 4), ((wide, width), F32, 1),
         ((wide, hid), F32, 1), ((wide, hid), F32, 1)],
        [pltpu.VMEM(whole.shape, BF), sem((8,))], vmem=40)
    g_expand = g_expand.reshape(expand.shape)
    g_contract = jnp.swapaxes(g_contract.reshape(1, heads, 64, hid), 2, 3)
    return (
        layer_output, input_grads, g_gains, g_mix[None], g_rate, g_offset, g_expand, g_hidden, g_contract, g_result,
        g_heads, g_shift, g_out[None], g_sw[None], g_dn[None], rate_stats,
    )


def solution(mesh):
    placed = (
        P(None, "dp", None, None),
        P(None, "dp", None),
        P("segment", None, None),
        P("segment", None, None, "tensor"),
        P("segment", None, "tensor"),
        P("segment", "tensor"),
        P("segment", "tensor", None, None),
        P("segment", "tensor", None),
        P("segment", "tensor", None, None),
        P("segment", "tensor", None),
        P("segment", None, "tensor", None),
        P("segment", "tensor", None),
        P("segment", "tensor", None),
        P("segment", None, None, "tensor"),
        P("segment", "tensor", None),
        P(None, "dp", None, None),
    )
    return jax.shard_map(
        shards,
        mesh=mesh,
        in_specs=placed,
        out_specs=(
            P("segment", None, "dp", None, None),
            P("segment", None, "dp", None, None),
            P("segment", None, None),
            P("segment", None, None, "tensor"),
            P("segment", None, "tensor"),
            P("segment", "tensor"),
            P("segment", "tensor", None, None),
            P("segment", "tensor", None),
            P("segment", "tensor", None, None),
            P("segment", "tensor", None),
            P("segment", None, "tensor", None),
            P("segment", "tensor", None),
            P("segment", "tensor", None),
            P("segment", None, None, "tensor"),
            P("segment", "tensor", None),
            P("segment", None, None, None, None),
        ),
        check_vma=False,
    )
```

```python
import functools
import jax
import jax.numpy as jnp
from jax import lax
from jax.experimental import pallas as pl
from jax.experimental.pallas import tpu as pltpu
from jax.sharding import PartitionSpec as P

MBT = 16
EPS = 1e-06
RATE = 0.125
C0 = 0.7978845608028654
BF = jnp.bfloat16
F32 = jnp.float32
VMEM = pl.BlockSpec(memory_space=pltpu.VMEM)
SMEM = pl.BlockSpec(memory_space=pltpu.SMEM)
HBM = pl.BlockSpec(memory_space=pltpu.HBM)
LOAD = "load"
NRM, INV, MIS, MEANN, GZ2 = range(5)
NA, INVA, NO, INVO, GATE = range(5)
RATE_ROW, HIDDEN_ROW, HEAD_ROW, OFFSET_ROW, GAIN_ROW, STAT_ROW = 0, 18, 24, 30, 31, 40
PACK_ROWS = 1152


def dot(a, b):
    return jnp.dot(a, b, preferred_element_type=F32)


def dot_t(a, b):
    return lax.dot_general(a, b, (((1,), (1,)), ((), ())), preferred_element_type=F32)


def tdot(a, b):
    return lax.dot_general(a, b, (((0,), (0,)), ((), ())), preferred_element_type=F32)


def cat(parts, axis):
    return jnp.concatenate(parts, axis=axis)


def gelu_parts(z):
    z2 = z * z
    t = jnp.tanh(C0 * z * (1.0 + 0.044715 * z2))
    h = 0.5 * (1.0 + t)
    du = C0 * (1.0 + 0.134145 * z2)
    sech = 1.0 - t * t
    value = z * h
    slope = h + 0.5 * z * sech * du
    return value, slope, t, z2, du, sech


def gelu_two(z):
    value, slope, _, _, _, _ = gelu_parts(z)
    return value, slope


def gelu_curve(z):
    _, _, t, z2, du, sech = gelu_parts(z)
    return sech * (C0 * (1.0 + 0.26829 * z2) - z * t * du * du)


def rms_inv(values):
    return lax.rsqrt(jnp.mean(values * values, axis=-1, keepdims=True) + EPS)


class Pick:
    def __init__(self, layer, sems):
        self.own = lax.axis_index("segment") == layer
        self.sems = sems
        self.count = 0

    def start(self, own_ref, other_ref, dst):
        sem = self.sems.at[self.count]
        self.count += 1

        @pl.when(self.own)
        def _():
            pltpu.make_async_copy(own_ref, dst, sem).start()

        @pl.when(jnp.logical_not(self.own))
        def _():
            pltpu.make_async_copy(other_ref, dst, sem).start()

        return pltpu.make_async_copy(own_ref, dst, sem)


def doc_places(dl_ref, steps):
    core = lax.axis_index("segment")
    one, two = dl_ref[core, 0], dl_ref[core, 1]
    begin = jnp.where(one == steps, 0, jnp.where(two == steps, one, one + two))
    cut = jnp.where(one == steps, two, one)
    return begin, cut


def block_starts(begin, steps):
    places = []
    for s in range(steps):
        places.append(pl.multiple_of((begin + s) * MBT, MBT))
        places.append(pl.multiple_of(jnp.where(s < begin, s, s + steps) * MBT, MBT))
    return places


def gather_rows(ref, lead, places):
    return cat([ref[lead, pl.ds(p, MBT), :] for p in places], 0)


def scatter_rows(ref, places, value):
    for i, p in enumerate(places):
        ref[pl.ds(p, MBT), :] = value[i * MBT : (i + 1) * MBT, :]


def turned_mask(cut, length):
    i = lax.broadcasted_iota(jnp.int32, (length, length), 0)
    j = lax.broadcasted_iota(jnp.int32, (length, length), 1)
    si, li, sj, lj = i >> 5, (i >> 4) & 1, length // 32 - 1 - (j >> 5), (j >> 4) & 1
    di = jnp.where(li == 0, 0, jnp.where(si < cut, 1, 2))
    dj = jnp.where(lj == 0, 0, jnp.where(sj < cut, 1, 2))
    return jnp.where((di == dj) & (si < sj), 1.0 / MBT, 0.0)


def masks(cut, length):
    def parts(axis):
        i = lax.broadcasted_iota(jnp.int32, (length, length), axis)
        step, lane, t = i >> 5, (i >> 4) & 1, i & 15
        doc = jnp.where(lane == 0, 0, jnp.where(step < cut, 1, 2))
        return step, lane, t, doc

    s0, l0, t0, d0 = parts(0)
    s1, l1, t1, d1 = parts(1)
    same = d0 == d1
    block = (s0 == s1) & (l0 == l1)
    past = jnp.where(same & (s1 < s0), 1.0 / MBT, 0.0)
    past_t = jnp.where(same & (s0 < s1), 1.0 / MBT, 0.0)
    inside = jnp.where(block & (t1 <= t0), 1.0 / (t0 + 1).astype(F32), 0.0)
    inside_t = jnp.where(block & (t0 <= t1), 1.0 / (t1 + 1).astype(F32), 0.0)
    return past, past + inside, past_t, past_t + inside_t


class Halves:
    def __init__(self):
        lane = lax.broadcasted_iota(jnp.int32, (1, 128), 1)
        self.left = lane < 64
        r = lax.broadcasted_iota(jnp.int32, (256, 128), 0) & 127
        c = lax.broadcasted_iota(jnp.int32, (256, 128), 1)
        self.mean_mat = jnp.where((r < 64) == (c < 64), 1.0 / 64.0, 0.0).astype(BF)

    def mean(self, x):
        high = x.astype(BF)
        low = (x - high.astype(F32)).astype(BF)
        return dot(cat([high, low], 1), self.mean_mat)

    def split(self, x):
        zero = jnp.zeros_like(x)
        return cat([jnp.where(self.left, x, zero), jnp.where(self.left, zero, x)], 0)

    def pack(self, a, b):
        return jnp.where(self.left, a, b)

    def both(self, weights, values):
        rows = weights[0].shape[0]
        full = dot(cat(weights, 0), values)
        return self.pack(full[:rows], full[rows:])


def pair_weights(inner_ref, small_ref, heads, p, halves):
    width = inner_ref.shape[2]
    zero = jnp.zeros((64, width), BF)

    def blocks(a, b):
        return cat([cat([a, zero], 1), cat([zero, b], 1)], 0)

    def centred(index):
        w = inner_ref[heads + index].astype(F32)
        return (w - jnp.mean(w, axis=0, keepdims=True)).astype(BF)

    w1 = blocks(inner_ref[2 * p], inner_ref[2 * p + 1])
    w2 = blocks(centred(2 * p), centred(2 * p + 1))
    return w1, w2


def join(parts):
    return cat(parts, 0) if len(parts) > 1 else parts[0]


def pad_rows(parts, rows):
    have = sum(x.shape[0] for x in parts)
    if have < rows:
        parts = parts + [jnp.zeros((rows - have, parts[0].shape[1]), parts[0].dtype)]
    return cat(parts, 0) if len(parts) > 1 else parts[0]


def mixer_forward(refs, x_one, mix_ref, rate_ref, inner_ref, small_ref, begin_cut, x1_ready):
    (mixed_ref, stats_ref, kq_ref, x2_ref, g1_ref, y2_ref, d1_ref, ud2_ref, e1_ref, sm_ref, so_ref, sg_ref) = refs
    _, cut = begin_cut
    length = x_one.shape[0]
    heads = inner_ref.shape[0] // 2
    pairs = heads // 2
    hid = inner_ref.shape[2]
    wide = heads * 64
    steps = length // (2 * MBT)
    rows = 2 * MBT
    past, near, _, _ = masks(cut, length)
    hv = Halves()
    proj = dot(x_one, mix_ref[...])
    logits = dot_t(x_one, rate_ref[...]) + small_ref[3:4, 0:16]
    sg = jax.nn.sigmoid(logits)
    sg_ref[...] = sg
    stats_ref[...] = cat(
        [jnp.mean(sg, axis=0, keepdims=True), jnp.max(sg, axis=0, keepdims=True)], 0
    )
    rates = RATE * sg
    st = []
    for p in range(pairs):
        c = slice(128 * p, 128 * p + 128)
        h = slice(2 * hid * p, 2 * hid * (p + 1))
        q, k, v, gate = [proj[:, wide * i + 128 * p : wide * i + 128 * p + 128] for i in range(4)]
        d = dict(q=q, gate=gate, diff=v - k, c=c, h=h)
        d["w1"], d["w2"] = pair_weights(inner_ref, small_ref, heads, p, hv)
        d["b1"] = small_ref[0:1, h]
        b2 = small_ref[2:3, 128 * p : 128 * p + 128]
        d["b2"] = b2 - hv.mean(jnp.broadcast_to(b2, (8, 128)))[0:1]
        d["g"] = small_ref[2:3, wide + 128 * p : wide + 128 * p + 128]
        d["gp"] = small_ref[2:3, 2 * wide + 128 * p : 2 * wide + 128 * p + 128]
        d["be"] = small_ref[2:3, 3 * wide + 128 * p : 3 * wide + 128 * p + 128]
        d["r"] = [rates[:, 2 * p + i : 2 * p + i + 1] for i in range(2)]
        d["rp"] = hv.pack(d["r"][0], d["r"][1])
        d["kb"], d["qb"] = k.astype(BF), q.astype(BF)
        kq_ref[:, c] = d["kb"]
        kq_ref[:, wide + 128 * p : wide + 128 * p + 128] = d["qb"]
        d["base"] = dot(d["kb"], d["w1"]) + d["b1"]
        kk = dot_t(hv.split(d["kb"]), d["kb"])
        d["m1"] = [(past * (kk[i * length : (i + 1) * length] + 1.0)).astype(BF) for i in range(2)]
        for name in ("x2", "g1", "g2", "z1", "u"):
            d[name] = []
        st.append(d)
    kq_ref.send()
    sg_ref.send()
    for s in range(steps):
        sl = slice(rows * s, rows * s + rows)
        for p in range(pairs):
            d = st[p]
            c, h = d["c"], d["h"]
            z1 = d["base"][sl]
            if s:
                g1 = pad_rows(d["g1"], length)
                x2 = pad_rows(d["x2"], length)
                g2 = pad_rows(d["g2"], length)
                z1 = z1 - cat([dot(d["m1"][i][sl], g1[:, hid * i : hid * (i + 1)]) for i in range(2)], 1)
            act, slope = gelu_two(z1)
            actb = act.astype(BF)
            z2 = dot_t(actb, d["w2"]) + d["b2"]
            if s:
                far = [
                    (past[sl] * (dot_t(actb[:, hid * i : hid * (i + 1)], x2[:, hid * i : hid * (i + 1)]) + 1.0)).astype(BF)
                    for i in range(2)
                ]
                z2 = z2 - dot(cat(far, 1), hv.split(g2))
            inv = lax.rsqrt(hv.mean(z2 * z2) + EPS)
            n = z2 * inv
            mis = n * d["g"] + d["be"] - d["diff"][sl]
            misg = mis * d["g"]
            both = hv.mean(cat([misg, misg * n], 0))
            gz2 = (misg - both[:rows] - n * both[rows:]) * inv
            gz2b = gz2.astype(BF)
            u = dot(gz2b, d["w2"])
            if s:
                f = dot_t(hv.split(gz2b), g2)
                u = u - cat(
                    [
                        dot((past[sl] * f[rows * i : rows * (i + 1)]).astype(BF), x2[:, hid * i : hid * (i + 1)])
                        for i in range(2)
                    ],
                    1,
                )
            gz1 = u * slope
            r0, r1 = d["r"][0][sl], d["r"][1][sl]
            g1n = cat([gz1[:, :hid] * r0, gz1[:, hid:] * r1], 1).astype(BF)
            g2n = (gz2 * d["rp"][sl]).astype(BF)
            d["x2"].append(actb)
            d["g1"].append(g1n)
            d["g2"].append(g2n)
            d["z1"].append(z1)
            d["u"].append(u)
            x2_ref[sl, h] = actb
            g1_ref[sl, h] = g1n
            d1_ref[sl, h] = slope.astype(BF)
            sm_ref[NRM, sl, c] = n
            sm_ref[INV, sl, c] = inv
            sm_ref[MIS, sl, c] = mis
            sm_ref[MEANN, sl, c] = both[rows:]
            sm_ref[GZ2, sl, c] = gz2
    for ref in (x2_ref, g1_ref, d1_ref, sm_ref):
        ref.send()
    mixed = []
    for p in range(pairs):
        d = st[p]
        c, h = d["c"], d["h"]
        g1, x2, g2 = cat(d["g1"], 0), cat(d["x2"], 0), cat(d["g2"], 0)
        ud2_ref[:, h] = (cat(d["u"], 0) * gelu_curve(cat(d["z1"], 0))).astype(BF)
        qk = dot_t(hv.split(d["qb"]), d["kb"])
        corr = [
            dot((near * (qk[length * i : length * (i + 1)] + 1.0)).astype(BF), g1[:, hid * i : hid * (i + 1)])
            for i in range(2)
        ]
        act, slope = gelu_two(dot(d["qb"], d["w1"]) + d["b1"] - cat(corr, 1))
        actb = act.astype(BF)
        y2_ref[:, h] = actb
        e1_ref[:, h] = slope.astype(BF)
        far = [
            (near * (dot_t(actb[:, hid * i : hid * (i + 1)], x2[:, hid * i : hid * (i + 1)]) + 1.0)).astype(BF)
            for i in range(2)
        ]
        a2 = dot_t(actb, d["w2"]) + d["b2"] - dot(cat(far, 1), hv.split(g2))
        inv_a = lax.rsqrt(hv.mean(a2 * a2) + EPS)
        n_a = a2 * inv_a
        out = d["q"] + n_a * d["g"] + d["be"]
        inv_o = lax.rsqrt(hv.mean(out * out) + EPS)
        n_o = out * inv_o
        gated, _ = gelu_two(d["gate"])
        low = (gated * n_o * d["gp"]).astype(BF)
        mixed_ref[:, c] = low
        mixed.append(low)
        so_ref[NA, :, c] = n_a
        so_ref[INVA, :, c] = inv_a
        so_ref[NO, :, c] = n_o
        so_ref[INVO, :, c] = inv_o
        so_ref[GATE, :, c] = d["gate"]
    return cat(mixed, 1)


def mixer_backward(dmixed, mixed_refs, inner_ref, small_ref, begin_cut, ig_ref, ms_ref):
    (kq_ref, x2_ref, g1_ref, y2_ref, d1_ref, ud2_ref, e1_ref, sm_ref, so_ref, sg_ref) = mixed_refs
    _, cut = begin_cut
    length = dmixed.shape[0]
    heads = inner_ref.shape[0] // 2
    pairs = heads // 2
    hid = inner_ref.shape[2]
    wide = heads * 64
    steps = length // (2 * MBT)
    rows = 2 * MBT
    past, near, past_t, near_t = masks(cut, length)
    hv = Halves()

    def turned(x):
        return cat([x[rows * k : rows * (k + 1)] for k in reversed(range(steps))], 0)

    past_b = turned_mask(cut, length)
    sg = sg_ref[...]
    rates = RATE * sg

    def by_head(fn):
        return [fn(slice(hid * i, hid * (i + 1)), i) for i in range(2)]

    st = []
    for p in range(pairs):
        c = slice(128 * p, 128 * p + 128)
        h = slice(2 * hid * p, 2 * hid * (p + 1))
        d = dict(c=c, h=h)
        d["w1"], d["w2"] = pair_weights(inner_ref, small_ref, heads, p, hv)
        g = small_ref[2:3, wide + 128 * p : wide + 128 * p + 128]
        gp = small_ref[2:3, 2 * wide + 128 * p : 2 * wide + 128 * p + 128]
        d["g"] = g
        d["r"] = [rates[:, 2 * p + i : 2 * p + i + 1] for i in range(2)]
        d["rp"] = hv.pack(d["r"][0], d["r"][1])
        kb = kq_ref[:, c]
        qb = kq_ref[:, wide + 128 * p : wide + 128 * p + 128]
        x2, g1, y2 = x2_ref[:, h], g1_ref[:, h], y2_ref[:, h]
        gz2 = sm_ref[GZ2, :, c]
        gz2b = gz2.astype(BF)
        g2b = (gz2 * d["rp"]).astype(BF)
        dm = dmixed[:, c]
        gate = so_ref[GATE, :, c]
        n_o, inv_o = so_ref[NO, :, c], so_ref[INVO, :, c]
        n_a, inv_a = so_ref[NA, :, c], so_ref[INVA, :, c]
        gated, gate_slope = gelu_two(gate)
        d["dgate"] = dm * n_o * gp * gate_slope
        drm = dm * gated
        d["dgp"] = jnp.sum(drm * n_o, axis=0, keepdims=True)
        dpg = drm * gp
        do = (dpg - n_o * hv.mean(dpg * n_o)) * inv_o
        dn = do * g
        both = hv.mean(cat([dn, dn * n_a], 0))
        da2 = (dn - both[:length] - n_a * both[length:]) * inv_a
        d["dg"] = jnp.sum(do * n_a, axis=0, keepdims=True)
        d["dbe"] = jnp.sum(do, axis=0, keepdims=True)
        d["db2"] = jnp.sum(da2, axis=0, keepdims=True)
        da2b = da2.astype(BF)
        da2m, g2m = hv.split(da2b), hv.split(g2b)
        km = hv.split(kb)

        def weigh(mask, full, i):
            return (mask * full[length * i : length * (i + 1)]).astype(BF)

        p2 = dot_t(da2m, g2b)
        p2t = dot_t(g2m, da2b)
        dy2 = dot(da2b, d["w2"]) - cat(by_head(lambda e, i: dot(weigh(near, p2, i), x2[:, e])), 1)
        d["bx2"] = cat(by_head(lambda e, i: dot(weigh(near_t, p2t, i), y2[:, e])), 1)
        syt = by_head(lambda e, i: (near_t * (dot_t(x2[:, e], y2[:, e]) + 1.0)).astype(BF))
        d["bg2"] = -hv.both(syt, da2b)
        da1 = dy2 * e1_ref[:, h].astype(F32)
        da1b = da1.astype(BF)
        d["db1"] = jnp.sum(da1, axis=0, keepdims=True)
        p1 = by_head(lambda e, i: (near * dot_t(da1b[:, e], g1[:, e])).astype(BF))
        p1t = by_head(lambda e, i: (near_t * dot_t(g1[:, e], da1b[:, e])).astype(BF))
        d["dq"] = do + dot_t(da1b, d["w1"]) - hv.both(p1, kb)
        d["dk"] = -hv.both(p1t, qb)
        kq = dot_t(km, qb) + 1.0
        kk = dot_t(km, turned(kb)) + 1.0
        d["bg1"] = cat(by_head(lambda e, i: dot(weigh(near_t, kq, i), da1b[:, e])), 1)
        x2r, gz2r = turned(x2), turned(gz2b)
        d["m1t"] = [weigh(past_b, kk, i) for i in range(2)]
        d["rx"] = by_head(lambda e, i: (past_b * (dot_t(x2[:, e], x2r[:, e]) + 1.0)).astype(BF))
        ft = dot_t(g2m, gz2r)
        d["ft"] = [weigh(past_b, ft, i) for i in range(2)]
        d.update(x2=x2, y2=y2, g1=g1, g2b=g2b, gz2=gz2, gz2b=gz2b, x2r=x2r, gz2r=gz2r)
        d.update(kb=kb, qb=qb, da1b=da1b, da2b=da2b)
        for name in ("z1", "z2", "u", "rg1", "rg2", "t"):
            d[name] = [None] * steps
        st.append(d)
    for s in reversed(range(steps)):
        sl = slice(rows * s, rows * s + rows)
        later = length - rows * (s + 1)
        mask = past_b[sl, :later]
        for p in range(pairs):
            d = st[p]
            c, h = d["c"], d["h"]
            x2, x2e, g2e = d["x2"], d["x2"][: rows * s], d["g2b"][: rows * s]
            bg1, bg2, bx2 = -d["bg1"][sl], d["bg2"][sl], -d["bx2"][sl]
            if s < steps - 1:

                def full(parts):
                    return join(parts[: s : -1])

                z1l, z2l, ul = full(d["z1"]), full(d["z2"]), full(d["u"])
                x2l = d["x2r"][:later]
                bg1 = bg1 - cat(by_head(lambda e, i: dot(d["m1t"][i][sl, :later], z1l[:, e])), 1)
                xu = by_head(lambda e, i: (mask * dot_t(x2[sl, e], ul[:, e])).astype(BF))
                bg2 = bg2 - hv.both([d["rx"][i][sl, :later] for i in range(2)], z2l) - hv.both(xu, d["gz2r"][:later])
                gz = dot_t(hv.split(d["g2b"][sl]), z2l)
                bx2 = bx2 - cat(
                    by_head(
                        lambda e, i: dot((mask * gz[rows * i : rows * (i + 1)]).astype(BF), x2l[:, e])
                        + dot(d["ft"][i][sl, :later], ul[:, e])
                    ),
                    1,
                )
            r0, r1 = d["r"][0][sl], d["r"][1][sl]
            dgz1 = cat([bg1[:, :hid] * r0, bg1[:, hid:] * r1], 1)
            slope = d1_ref[sl, h].astype(F32)
            du = dgz1 * slope
            dub = du.astype(BF)
            dz1 = dgz1 * ud2_ref[sl, h].astype(F32)
            dgz2 = bg2 * d["rp"][sl] + dot_t(dub, d["w2"])
            if s:
                hm = by_head(lambda e, i: (past[sl, : rows * s] * dot_t(dub[:, e], x2e[:, e])).astype(BF))
                dgz2 = dgz2 - hv.both(hm, g2e)
            n, inv = sm_ref[NRM, sl, c], sm_ref[INV, sl, c]
            mis, mn = sm_ref[MIS, sl, c], sm_ref[MEANN, sl, c]
            g = d["g"]
            e = dgz2 * inv
            three = hv.mean(cat([e, e * n, dgz2 * d["gz2"][sl]], 0))
            dmis = e - three[:rows] - n * three[rows : 2 * rows]
            t = dmis * g
            dn = t * g - e * mn - mis * g * three[rows : 2 * rows]
            two = hv.mean(cat([dn, dn * n], 0))
            dz2 = inv * (dn - two[:rows] - n * (two[rows:] + three[2 * rows :]))
            d["dg"] = d["dg"] + jnp.sum(t * n + dmis * mis, axis=0, keepdims=True)
            d["dbe"] = d["dbe"] + jnp.sum(t, axis=0, keepdims=True)
            d["db2"] = d["db2"] + jnp.sum(dz2, axis=0, keepdims=True)
            dz2b = dz2.astype(BF)
            dx2 = bx2 + dot(dz2b, d["w2"])
            if s:
                j = dot_t(hv.split(dz2b), g2e)
                dx2 = dx2 - cat(
                    by_head(
                        lambda e, i: dot((past[sl, : rows * s] * j[rows * i : rows * (i + 1)]).astype(BF), x2e[:, e])
                    ),
                    1,
                )
            dz1 = dz1 + dx2 * slope
            d["db1"] = d["db1"] + jnp.sum(dz1, axis=0, keepdims=True)
            d["z1"][s], d["z2"][s], d["u"][s] = dz1.astype(BF), dz2b, dub
            d["rg1"][s], d["rg2"][s], d["t"][s] = bg1, bg2, t
    parts = [[], [], [], []]
    rate_cols = []
    for p in range(pairs):
        d = st[p]
        z1, z2, u = cat(d["z1"], 0), cat(d["z2"], 0), cat(d["u"], 0)
        t = cat(d["t"], 0)
        g1 = d["g1"]
        both = by_head(
            lambda e, i: (past * dot_t(z1[:, e], g1[:, e]) + past_t * dot_t(g1[:, e], z1[:, e])).astype(BF)
        )
        dk = d["dk"] + t + dot_t(z1, d["w1"]) - hv.both(both, d["kb"])
        for i, value in enumerate((d["dq"], dk, -t, d["dgate"])):
            parts[i].append(value.astype(BF))
        dw1 = tdot(cat([d["kb"], d["qb"]], 0), cat([z1, d["da1b"]], 0))
        dw2 = tdot(cat([z2, d["da2b"], d["gz2b"]], 0), cat([d["x2"], d["y2"], u], 0))
        for i in range(2):
            row = 64 * (2 * p + i)
            ig_ref[row : row + 64, :] = dw1[64 * i : 64 * i + 64, hid * i : hid * (i + 1)].astype(BF)
            row = row + 64 * heads
            ig_ref[row : row + 64, :] = dw2[64 * i : 64 * i + 64, hid * i : hid * (i + 1)].astype(BF)
            row = HIDDEN_ROW + 2 * p + i
            ms_ref[row : row + 1, :] = d["db1"][:, hid * i : hid * (i + 1)]
        one = cat(d["rg1"], 0) * g1.astype(F32)
        two = cat(d["rg2"], 0) * d["g2b"].astype(F32)
        two = cat([jnp.where(hv.left, two, 0.0), jnp.where(hv.left, 0.0, two)], 1)
        for i in range(2):
            whole = one[:, hid * i : hid * i + 128] + one[:, hid * i + 128 : hid * (i + 1)]
            whole = whole + two[:, 128 * i : 128 * (i + 1)]
            rate_cols.append(jnp.sum(whole, axis=-1, keepdims=True))
        for j, name in enumerate(("db2", "dg", "dgp", "dbe")):
            piece = 3 * j + p
            row = HEAD_ROW + piece // 2
            ms_ref[row : row + 1, 128 * (piece % 2) : 128 * (piece % 2) + 128] = d[name]
    lane = lax.broadcasted_iota(jnp.int32, (1, 16), 1)
    dlog = jnp.zeros((length, 16), F32)
    for i, col in enumerate(rate_cols):
        dlog = dlog + jnp.where(lane == i, col, 0.0)
    dlog = dlog * (1.0 - sg)
    ms_ref[OFFSET_ROW : OFFSET_ROW + 1, 0:16] = jnp.sum(dlog, axis=0, keepdims=True)
    dmix = [cat(x, 1) for x in parts]
    return dmix, dlog.astype(BF)


def ka_body(layer, *args):
    if layer == 0:
        dl_ref, li_ref = args[:2]
        rest = args[2:]
    else:
        dl_ref, h1_ref, fo_ref, fr_ref = args[:4]
        rest = args[4:]
    wrefs, rest = rest[:10], rest[10:]
    if layer == 1:
        lo_ref, rest = rest[0], rest[1:]
    hb_ref, x1_ref, att_ref = rest[:3]
    saves, scratch = rest[3:15], rest[15:]
    mix_v, inner_v, small_v, rate_v, out_v, sems = scratch
    pick = Pick(layer, sems)
    c_small = pick.start(wrefs[0], wrefs[1], small_v)
    c_mix = pick.start(wrefs[2], wrefs[3], mix_v)
    c_rate = pick.start(wrefs[4], wrefs[5], rate_v)
    c_inner = pick.start(wrefs[6], wrefs[7], inner_v)
    c_out = pick.start(wrefs[8], wrefs[9], out_v)
    length = hb_ref.shape[0]
    steps = length // (2 * MBT)
    begin, cut = doc_places(dl_ref, steps)
    places = block_starts(begin, steps)
    if layer == 0:
        low = gather_rows(li_ref, lax.axis_index("segment"), places)
    else:
        low = (h1_ref[...] + (fo_ref[...].astype(F32) + fr_ref[...].astype(F32))).astype(BF)
        scatter_rows(lo_ref, places, low)
        lo_ref.send()
    hb_ref[...] = low
    hb_ref.send()
    h = low.astype(F32)
    inv = rms_inv(h)
    c_small.wait()
    x_one = (h * inv * small_v[1:2, 0 : h.shape[1]]).astype(BF)
    x1_ref[...] = x_one
    x1_ref.send()
    c_mix.wait()
    c_rate.wait()
    c_inner.wait()
    mixed = mixer_forward(saves, x_one, mix_v, rate_v, inner_v, small_v, (begin, cut), None)
    c_out.wait()
    att_ref[...] = dot(mixed, out_v[...]).astype(BF)


def ffn_forward(h1, small_v, sw_v, dn_v, copies):
    width = h1.shape[1]
    inv = rms_inv(h1)
    x2 = (h1 * inv * small_v[1:2, width : 2 * width]).astype(BF)
    copies[0].wait()
    up_at = sw_v.shape[1] // 2
    gate = dot(x2, sw_v[:, :up_at])
    up = dot(x2, sw_v[:, up_at:])
    sgm = 1.0 / (1.0 + jnp.exp(-gate))
    silu = gate * sgm
    slope = up * (sgm * (1.0 + gate * (1.0 - sgm)))
    hidden = (silu * up).astype(BF)
    copies[1].wait()
    feed = dot(hidden, dn_v[...]).astype(BF)
    return x2, hidden, slope, silu, feed


def ffn_backward(dfe, slope, silu, sw_v, dn_v):
    up_at = sw_v.shape[1] // 2
    dh = dot_t(dfe, dn_v[...])
    dg, du = (dh * slope).astype(BF), (dh * silu).astype(BF)
    dx = dot_t(dg, sw_v[:, :up_at]) + dot_t(du, sw_v[:, up_at:])
    return dg, du, dx.astype(BF)


def pack_ffn(keep_ref, send_ref, x2, dg, du, hidden, dfe):
    first = lax.axis_index("segment") == 0
    width, wide = x2.shape[1], dg.shape[1]
    half = wide // 2

    def put(ref, grad, hid):
        ref[:, 0:width] = x2
        ref[:, width : width + wide] = grad
        ref[:, width + wide : width + wide + half] = hid
        ref[:, width + wide + half :] = dfe

    @pl.when(first)
    def _():
        put(keep_ref, dg, hidden[:, :half])
        put(send_ref, du, hidden[:, half:])

    @pl.when(jnp.logical_not(first))
    def _():
        put(keep_ref, du, hidden[:, half:])
        put(send_ref, dg, hidden[:, :half])


def kf_body(hb_ref, ao_ref, ar_ref, s_own, s_oth, w_own, w_oth, d_own, d_oth,
            h1_ref, x2_ref, hid_ref, sl_ref, si_ref, fe_ref, small_v, sw_v, dn_v, sems):
    pick = Pick(0, sems)
    c_small = pick.start(s_own, s_oth, small_v)
    copies = [pick.start(w_own, w_oth, sw_v), pick.start(d_own, d_oth, dn_v)]
    h1 = hb_ref[...].astype(F32) + (ao_ref[...].astype(F32) + ar_ref[...].astype(F32))
    h1_ref[...] = h1
    h1_ref.send()
    c_small.wait()
    x2, hidden, slope, silu, feed = ffn_forward(h1, small_v, sw_v, dn_v, copies)
    x2_ref[...] = x2
    hid_ref[...] = hidden
    sl_ref[...] = slope.astype(BF)
    si_ref[...] = silu.astype(BF)
    fe_ref[...] = feed


def kfb_body(dl_ref, ct_ref, hb_ref, ao_ref, ar_ref, s_own, s_oth, w_own, w_oth, d_own, d_oth,
             h1_ref, fe_ref, dxt_ref, dfe_ref, keep_ref, send_ref, small_v, sw_v, dn_v, sems):
    pick = Pick(1, sems)
    c_small = pick.start(s_own, s_oth, small_v)
    copies = [pick.start(w_own, w_oth, sw_v), pick.start(d_own, d_oth, dn_v)]
    length = hb_ref.shape[0]
    steps = length // (2 * MBT)
    begin, _ = doc_places(dl_ref, steps)
    dfe = gather_rows(ct_ref, lax.axis_index("segment"), block_starts(begin, steps))
    dfe_ref[...] = dfe
    h1 = hb_ref[...].astype(F32) + (ao_ref[...].astype(F32) + ar_ref[...].astype(F32))
    h1_ref[...] = h1
    h1_ref.send()
    c_small.wait()
    x2, hidden, slope, silu, feed = ffn_forward(h1, small_v, sw_v, dn_v, copies)
    fe_ref[...] = feed
    dg, du, dx = ffn_backward(dfe, slope, silu, sw_v, dn_v)
    dxt_ref[...] = dx
    pack_ffn(keep_ref, send_ref, x2, dg, du, hidden, dfe)


def norm_back(dx, x, gain, base):
    inv = rms_inv(x)
    e = dx * gain
    grad = base + e * inv - x * (jnp.mean(e * x, axis=-1, keepdims=True) * inv * inv * inv)
    gain_grad = jnp.sum(dx * x * inv, axis=0, keepdims=True)
    return grad, gain_grad


def kbf_body(dl_ref, hb_ref, dh_ref, xo_ref, xr_ref, t_own, t_oth, x2_ref, hid_ref, sl_ref, si_ref,
             w_own, w_oth, d_own, d_oth,
             ig_ref, gg_ref, dfe_ref, dxt_ref, keep_ref, send_ref, small_v, sw_v, dn_v, sems, sems_two):
    above = Pick(1, sems)
    c_small = above.start(t_own, t_oth, small_v)
    pick = Pick(0, sems_two)
    copies = [pick.start(d_own, d_oth, dn_v), pick.start(w_own, w_oth, sw_v)]
    length, width = hb_ref.shape
    steps = length // (2 * MBT)
    begin, _ = doc_places(dl_ref, steps)
    dx = xo_ref[...].astype(F32) + xr_ref[...].astype(F32)
    c_small.wait()
    grad, gain = norm_back(dx, hb_ref[...].astype(F32), small_v[1:2, 0:width], dh_ref[...])
    scatter_rows(ig_ref, block_starts(begin, steps), grad)
    ig_ref.send()
    gg_ref[...] = gain
    dfe = grad.astype(BF)
    dfe_ref[...] = dfe
    for c in copies:
        c.wait()
    dg, du, dxt = ffn_backward(dfe, sl_ref[...].astype(F32), si_ref[...].astype(F32), sw_v, dn_v)
    dxt_ref[...] = dxt
    pack_ffn(keep_ref, send_ref, x2_ref[...], dg, du, hid_ref[...], dfe)


def stat_rows(own, other, dp):
    zero = lax.axis_index("tensor") == 0
    low, high = jnp.where(zero, own, other), jnp.where(zero, other, own)
    line = cat([low[0:1], high[0:1], low[1:2], high[1:2], jnp.zeros((1, 64), F32)], 1)
    core = lax.axis_index("segment")
    line = cat([jnp.where(core == 0, line, 0.0), jnp.where(core == 0, 0.0, line)], 1)
    row = lax.broadcasted_iota(jnp.int32, (dp, 256), 0)
    return jnp.where(row == lax.axis_index("dp"), line, 0.0)


def kba_body(layer, dp, dl_ref, xo_ref, xr_ref, dy_ref, h1_ref, x1_ref, mixed_ref, so_ref, sr_ref, *rest):
    saves, rest = rest[:10], rest[10:]
    wrefs, rest = rest[:10], rest[10:]
    dh_ref, dxo_ref, keep_ref, send_ref, ig_ref, ms_ref, mix_v, inner_v, small_v, rate_v, out_v, sems = rest
    pick = Pick(layer, sems)
    kq, x2, g1, y2, d1, ud2, e1, sm, so, sg = saves
    c_small = pick.start(wrefs[0], wrefs[1], small_v)
    h1_ref.start()
    c_out = pick.start(wrefs[8], wrefs[9], out_v)
    c_inner = pick.start(wrefs[6], wrefs[7], inner_v)
    for ref in (so, sg, sm, kq, x2, g1, y2, e1, d1, ud2, x1_ref, mixed_ref):
        ref.start()
    c_mix = pick.start(wrefs[2], wrefs[3], mix_v)
    c_rate = pick.start(wrefs[4], wrefs[5], rate_v)
    length, width = h1_ref.shape
    steps = length // (2 * MBT)
    place = doc_places(dl_ref, steps)
    dx = xo_ref[...].astype(F32) + xr_ref[...].astype(F32)
    c_small.wait()
    dh, gain = norm_back(dx, h1_ref[...], small_v[1:2, width : 2 * width], dy_ref[...].astype(F32))
    dh_ref[...] = dh
    dh_ref.send()
    ms_ref[...] = jnp.zeros(ms_ref.shape, F32)
    at = slice(2 * layer, 2 * layer + 2)
    ms_ref[STAT_ROW : STAT_ROW + dp, :] = stat_rows(so_ref[at, :], sr_ref[at, :], dp)
    for j in range(3):
        ms_ref[GAIN_ROW + j : GAIN_ROW + j + 1, :] = gain[:, 256 * j : 256 * j + 256]
    da = dh.astype(BF)
    c_out.wait()
    c_inner.wait()
    dmixed = dot_t(da, out_v[...])
    dmix, dlog = mixer_backward(dmixed, saves, inner_v, small_v, place, ig_ref, ms_ref)
    x1 = x1_ref[...]
    drate = tdot(dlog, x1)
    heads = inner_v.shape[0] // 2
    for j in range(3):
        row = RATE_ROW + heads * j
        ms_ref[row : row + heads, :] = drate[:heads, 256 * j : 256 * j + 256]
    c_mix.wait()
    c_rate.wait()
    dxo_ref[...] = (dot_t(cat(dmix, 1), mix_v[...]) + dot(dlog, rate_v[...])).astype(BF)
    first = lax.axis_index("segment") == 0
    half = width // 2
    wide = 2 * dmix[0].shape[1]
    mixed = mixed_ref[...]

    def put(ref, one, two, att):
        ref[:, 0:width] = x1
        ref[:, width : width + wide // 2] = one
        ref[:, width + wide // 2 : width + wide] = two
        ref[:, width + wide : width + wide + mixed.shape[1]] = mixed
        ref[:, width + wide + mixed.shape[1] :] = att

    @pl.when(first)
    def _():
        put(keep_ref, dmix[0], dmix[1], da[:, :half])
        put(send_ref, dmix[2], dmix[3], da[:, half:])

    @pl.when(jnp.logical_not(first))
    def _():
        put(keep_ref, dmix[2], dmix[3], da[:, half:])
        put(send_ref, dmix[0], dmix[1], da[:, :half])


def ke_body(dl_ref, hb_ref, dh_ref, xo_ref, xr_ref, s_own, s_oth, ig_ref, gg_ref, small_v, sems):
    pick = Pick(0, sems)
    c_small = pick.start(s_own, s_oth, small_v)
    length, width = hb_ref.shape
    steps = length // (2 * MBT)
    begin, _ = doc_places(dl_ref, steps)
    dx = xo_ref[...].astype(F32) + xr_ref[...].astype(F32)
    c_small.wait()
    grad, gain = norm_back(dx, hb_ref[...].astype(F32), small_v[1:2, 0:width], dh_ref[...])
    scatter_rows(ig_ref, block_starts(begin, steps), grad)
    gg_ref[...] = gain


def beside(one, two, low, high):
    return cat([one[:, low:high], two[:, low:high]], 0)


class Columns:
    def __init__(self, dst, buf, at, sems):
        self.dst, self.buf, self.at, self.sems, self.copies = dst, buf, at, sems, []

    def send(self, low, high):
        copy = pltpu.make_async_copy(
            self.buf.at[low:high], self.dst.at[low:high, self.at : self.at + self.buf.shape[1]],
            self.sems.at[len(self.copies)],
        )
        copy.start()
        self.copies.append(copy)

    def wait(self):
        for copy in self.copies:
            copy.wait()


def grad_ffn_body(kf_ref, rf_ref, out_ref, buf, sems):
    width, wide = 768, 1024
    half = wide // 2
    out = Columns(out_ref, buf, 0, sems)
    for k in range(2):
        rows = slice(384 * k, 384 * (k + 1))
        x = beside(kf_ref, rf_ref, 384 * k, 384 * (k + 1))
        buf[rows, :] = tdot(x, beside(kf_ref, rf_ref, width, width + wide)).astype(BF)
        out.send(384 * k, 384 * (k + 1))
    down = tdot(beside(kf_ref, rf_ref, width + wide, width + wide + half),
                beside(kf_ref, rf_ref, width + wide + half, 2 * width + wide + half)).astype(BF)
    buf[768:1152, 0:width] = down[0:384]
    for k in range(3):
        buf[768 + 128 * k : 768 + 128 * (k + 1), width:wide] = down[384:512, 256 * k : 256 * (k + 1)]
    out.send(768, PACK_ROWS)
    out.wait()


def grad_mix_body(pack_ref, ka_ref, ra_ref, ik_ref, ir_ref, out_ref, buf, sems):
    width = 768
    out = Columns(out_ref, buf, 1024, sems)
    base = lax.axis_index("segment") * 384
    for k in range(2):
        rows = slice(384 * k, 384 * (k + 1))
        x = beside(ka_ref, ra_ref, 384 * k, 384 * (k + 1))
        buf[rows, :] = tdot(x, beside(ka_ref, ra_ref, width, 2 * width)).astype(BF)
        out.send(384 * k, 384 * (k + 1))
    grad = tdot(beside(ka_ref, ra_ref, 1536, 1920), beside(ka_ref, ra_ref, 1920, 2304)).astype(BF)
    buf[768:960, 0:384] = grad[0:192]
    buf[768:960, 384:768] = grad[192:384]
    for k in range(3):
        rows = pl.ds(pl.multiple_of(base + 128 * k, 128), 128)
        value = ik_ref[rows, :].astype(F32) + ir_ref[rows, :].astype(F32)
        buf[960:1088, 256 * k : 256 * (k + 1)] = value.astype(BF)
    buf[1088:PACK_ROWS, :] = jnp.zeros((PACK_ROWS - 1088, width), BF)
    out.send(768, PACK_ROWS)
    out.wait()


def final_body(turn, in_ref, sw_ref, dn_ref, mx_ref, ow_ref, ex_ref, co_ref, buf, sems):
    copies = []
    rows = PACK_ROWS // 8
    for k in range(8):
        at = rows * k
        if turn:
            at = pl.multiple_of(lax.rem(k + lax.axis_index("segment"), 8) * rows, 16)
        copies.append(pltpu.make_async_copy(in_ref.at[pl.ds(at, rows)], buf.at[rows * k : rows * (k + 1)], sems.at[k]))
    for copy in copies:
        copy.start()
    ready = 0

    def wait(upto):
        nonlocal ready
        while ready * rows < upto:
            copies[ready].wait()
            ready += 1

    for h in range(4):
        wait(192 * (h + 1))
        part = slice(192 * h, 192 * (h + 1))
        for c in range(2):
            base = 1792 * c
            sw_ref[part, c, :] = buf[part, base : base + 1024].astype(F32)
            for j in range(2):
                at = base + 1024 + 384 * j
                mx_ref[part, 2 * c + j, :] = buf[part, at : at + 384].astype(F32)
        sw_ref.send(192 * h, 192 * (h + 1))
        mx_ref.send(192 * h, 192 * (h + 1))
    wait(PACK_ROWS)
    for c in range(2):
        base = 1792 * c
        dn_ref[512 * c : 512 * c + 384, :] = buf[768:1152, base : base + 768].astype(F32)
        for k in range(3):
            part = buf[768 + 128 * k : 768 + 128 * (k + 1), base + 768 : base + 1024]
            dn_ref[512 * c + 384 : 512 * (c + 1), 256 * k : 256 * (k + 1)] = part.astype(F32)
        dn_ref.send(512 * c, 512 * (c + 1))
        base = base + 1024
        for j in range(2):
            at = base + 384 * j
            ow_ref[192 * j : 192 * (j + 1), 384 * c : 384 * (c + 1)] = buf[768:960, at : at + 384].astype(F32)
        ref = (ex_ref, co_ref)[c]
        for k in range(3):
            ref[128 * k : 128 * (k + 1), :] = buf[960:1088, base + 256 * k : base + 256 * (k + 1)].astype(F32)


class Loaded:
    def __init__(self, src, buf, sem):
        self.buf, self.shape = buf, buf.shape
        self.copy = pltpu.make_async_copy(src, buf, sem)
        self.started, self.waiting = False, True

    def start(self):
        if not self.started:
            self.copy.start()
            self.started = True

    def __getitem__(self, at):
        if self.waiting:
            self.start()
            self.copy.wait()
            self.waiting = False
        return self.buf[at]


class Stored:
    def __init__(self, dst, buf, sems):
        self.dst, self.buf, self.sems, self.shape = dst, buf, sems, buf.shape
        self.parts = []

    def __setitem__(self, at, value):
        self.buf[at] = value

    def send(self, low=None, high=None):
        k = len(self.parts)
        if low is None:
            copy = pltpu.make_async_copy(self.buf, self.dst, self.sems.at[k])
        else:
            at = slice(low, high)
            copy = pltpu.make_async_copy(self.buf.at[at], self.dst.at[at], self.sems.at[k])
        copy.start()
        self.parts.append(copy)

    def wait(self):
        for copy in self.parts:
            copy.wait()


def in_hbm(x):
    return pltpu.with_memory_space_constraint(x, pltpu.HBM)


def call(body, name, ins, specs, outs, scratch=(), deps=(), vmem=36, lazy=False):
    ins = [in_hbm(x) if spec is LOAD or spec is HBM else x for x, spec in zip(ins, specs)]
    deps = [in_hbm(x) for x in deps]
    have, extra, results, own = len(ins), len(deps), len(outs), len(scratch)
    loads = [k for k, spec in enumerate(specs) if spec is LOAD]
    stores = [k for k, out in enumerate(outs) if len(out) == 3]
    buffers = [pltpu.VMEM(ins[k].shape, ins[k].dtype) for k in loads]
    buffers += [pltpu.VMEM(outs[k][0], outs[k][1]) for k in stores]
    sems = [pltpu.SemaphoreType.DMA((max(1, len(loads)),))]
    sems += [pltpu.SemaphoreType.DMA((outs[k][2],)) for k in stores]

    def inside(*refs):
        operands, rest = list(refs[:have]), refs[have + extra :]
        written, rest = list(rest[:results]), rest[results:]
        own_refs, rest = rest[:own], rest[own:]
        bufs, (load_sems, *store_sems) = rest[: len(buffers)], rest[len(buffers) :]
        for i, k in enumerate(loads):
            operands[k] = Loaded(operands[k], bufs[i], load_sems.at[i])
            if not lazy:
                operands[k].start()
        done = []
        for i, k in enumerate(stores):
            written[k] = Stored(written[k], bufs[len(loads) + i], store_sems[i])
            done.append(written[k])
        body(*operands, *written, *own_refs)
        for one in done:
            if not one.parts:
                one.send()
        for one in done:
            one.wait()
        for k in loads:
            operands[k][0:1]

    return pl.pallas_call(
        inside,
        out_shape=[(pltpu.HBM if len(o) == 3 else jax.ShapeDtypeStruct)(o[0], o[1]) for o in outs],
        in_specs=[HBM if spec is LOAD else spec for spec in specs] + [HBM] * extra,
        out_specs=[HBM if len(o) == 3 else VMEM for o in outs],
        scratch_shapes=list(scratch) + buffers + sems,
        compiler_params=pltpu.CompilerParams(vmem_limit_bytes=vmem * 1024 * 1024),
        cost_estimate=pl.CostEstimate(flops=0, bytes_accessed=0, transcendentals=0),
        name=name,
    )(*ins, *deps)


def gate_body(*refs):
    pass


def pack_body(hb_ref, ng_ref, ro_ref, rb_ref, hg_ref, hs_ref, rw_ref, ex_ref, co_ref, small_ref, rate_ref, inner_ref):
    heads, hid, width = ex_ref.shape[0], ex_ref.shape[2], ng_ref.shape[1]
    wide = 64 * heads
    small_ref[...] = jnp.zeros(small_ref.shape, F32)
    for k in range(2):
        small_ref[1:2, width * k : width * (k + 1)] = ng_ref[k : k + 1, :]
    small_ref[3:4, 0:heads] = ro_ref[...]
    for h in range(heads):
        small_ref[0:1, hid * h : hid * (h + 1)] = hb_ref[h]
        at = slice(64 * h, 64 * (h + 1))
        small_ref[2:3, at] = rb_ref[h]
        for k in range(2):
            small_ref[2:3, wide * (k + 1) + 64 * h : wide * (k + 1) + 64 * (h + 1)] = hg_ref[h, k : k + 1, :]
        small_ref[2:3, wide * 3 + 64 * h : wide * 3 + 64 * (h + 1)] = hs_ref[h]
    rate_ref[...] = jnp.zeros(rate_ref.shape, BF)
    rate_ref[0:heads, :] = rw_ref[...]
    inner_ref[0:heads] = ex_ref[...].astype(BF)
    inner_ref[heads:] = co_ref[...].astype(BF)


def swap(value, axis):
    return lax.ppermute(value, axis, [(0, 1), (1, 0)])


def shards(
    layer_input, doc_lengths, norm_gains, mixing, rate_weight, rate_offset, expand, hidden_bias, contract,
    result_bias, head_gains, head_shift, output_proj, swiglu, down_proj, cotangent,
):
    micro, _, length, width = layer_input.shape
    heads = rate_weight.shape[2]
    hid = expand.shape[3]
    wide = heads * 64
    ff = down_proj.shape[1]
    first = lax.axis_index("segment") == 0
    dl = doc_lengths.reshape(micro, 3)
    li = layer_input.reshape(micro, length, width)
    ct = cotangent.reshape(micro, length, width)
    mix = mixing[0].reshape(width, -1)
    ow = output_proj[0]
    dn = down_proj[0]
    small, rate, inner = call(
        pack_body, "pack",
        [hidden_bias.reshape(heads, 1, hid), norm_gains[0], rate_offset, result_bias.reshape(heads, 1, 64),
         jnp.transpose(head_gains[0], (1, 0, 2)), head_shift.reshape(heads, 1, 64), rate_weight[0].T, expand[0],
         jnp.swapaxes(contract[0], 1, 2)],
        [VMEM] * 9, [((4, heads * hid), F32), ((16, width), BF), ((2 * heads, 64, hid), BF)])
    sw = swiglu[0].reshape(width, -1)

    def both(x):
        return in_hbm(x), in_hbm(swap(x, "segment"))

    small_p, mix_p, rate_p, inner_p, ow_p = both(small), both(mix), both(rate), both(inner), both(ow)
    sw = pl.pallas_call(
        gate_body, out_shape=pltpu.HBM(sw.shape, BF), in_specs=[HBM] * 6, out_specs=HBM,
        input_output_aliases={0: 0}, name="gate",
    )(sw, *[in_hbm(pair[1]) for pair in (small_p, mix_p, rate_p, inner_p, ow_p)])
    sw_p, dn_p = both(sw), both(dn)
    att_w = small_p + mix_p + rate_p + inner_p + ow_p
    tok = (length, width)
    save_shapes = [
        ((length, wide), BF, 1), ((2, 16), F32), ((length, 2 * wide), BF, 1),
        ((length, heads * hid), BF, 1), ((length, heads * hid), BF, 1), ((length, heads * hid), BF, 1),
        ((length, heads * hid), BF, 1), ((length, heads * hid), BF, 1), ((length, heads * hid), BF, 1),
        ((5, length, wide), F32, 1), ((5, length, wide), F32, 1), ((length, 16), F32, 1),
    ]
    sem = pltpu.SemaphoreType.DMA
    att_scratch = [
        pltpu.VMEM(mix.shape, BF), pltpu.VMEM(inner.shape, BF), pltpu.VMEM(small.shape, F32),
        pltpu.VMEM(rate.shape, BF), pltpu.VMEM(ow.shape, BF), sem((5,)),
    ]
    ffn_scratch = [pltpu.VMEM(small.shape, F32), pltpu.VMEM(sw.shape, BF), pltpu.VMEM(dn.shape, BF)]

    def ka(layer, ins):
        outs = [(tok, BF, 1), (tok, BF, 1), (tok, BF)] + save_shapes
        specs = [SMEM, LOAD] + [VMEM] * (len(ins) - 2) + [HBM] * 10
        if layer == 1:
            outs = [(tok, BF, 1)] + outs
        return call(functools.partial(ka_body, layer), f"mixer_fwd{layer}", list(ins) + list(att_w), specs, outs,
                    att_scratch)

    def exchange(x):
        return x, swap(x, "tensor")

    h0, x1_0, att, *save0 = ka(0, (dl, li))
    mixed0, stats0, save0 = save0[0], save0[1], save0[2:]
    ao, ar = exchange(att)
    h1_0, x2_0, hid_0, sl_0, si_0, fe = call(
        kf_body, "ffn_fwd0", [h0, ao, ar, *small_p, *sw_p, *dn_p], [LOAD] + [VMEM] * 2 + [HBM] * 6,
        [(tok, F32, 1), (tok, BF, 1)] + [((length, ff), BF, 1)] * 3 + [(tok, BF)], ffn_scratch + [sem((3,))])
    fo, fr = exchange(fe)
    lo0, hm, x1_1, att, *save1 = ka(1, (dl, h1_0, fo, fr))
    mixed1, stats1, save1 = save1[0], save1[1], save1[2:]
    ao, ar = exchange(att)
    pack_f = (length, 2 * width + ff + ff // 2)
    h1_1, fe, dxt, dfe1, keep, send = call(
        kfb_body, "ffn_both1", [dl, ct, hm, ao, ar, *small_p, *sw_p, *dn_p], [SMEM, LOAD, LOAD] + [VMEM] * 2 + [HBM] * 6,
        [(tok, F32, 1), (tok, BF), (tok, BF), (tok, BF), (pack_f, BF), (pack_f, BF)],
        ffn_scratch + [sem((3,))])

    dp = lax.axis_size("dp")
    ring = [0, 2, 4, 6, 7, 5, 3, 1] if dp == 8 else list(range(dp))

    stats = cat([stats0, stats1], 0)
    stats_in = swap(stats, "tensor")
    xo, xr = exchange(dxt)
    fo, fr = exchange(fe)
    pack_a = (length, width + 2 * wide + wide + width // 2)

    def kba(layer, xo, xr, dy, h1, x1, mixed, save, deps=()):
        return call(functools.partial(kba_body, layer, dp), f"mixer_bwd{layer}",
                    [dl, xo, xr, dy, h1, x1, mixed, stats, stats_in, *save, *att_w],
                    [SMEM] + [VMEM] * 3 + [LOAD] * 3 + [VMEM] * 2 + [LOAD] * 10 + [HBM] * 10,
                    [(tok, F32, 1), (tok, BF), (pack_a, BF), (pack_a, BF), ((2 * wide, hid), BF),
                     ((STAT_ROW + dp, hid), F32)],
                    att_scratch, deps, lazy=True)

    turn = 1 if dp == 8 else 0
    params = pltpu.CompilerParams(vmem_limit_bytes=36 * 1024 * 1024)
    pack_shape = (PACK_ROWS, ff + width)

    def grad_ffn(keep, send):
        return pl.pallas_call(
            grad_ffn_body, out_shape=pltpu.HBM(pack_shape, BF), in_specs=[VMEM] * 2, out_specs=HBM,
            scratch_shapes=[pltpu.VMEM((PACK_ROWS, ff), BF), sem((3,))], compiler_params=params, name="grad_ffn",
        )(keep, swap(send, "segment"))

    def grad_mix(pack, keep, send, ig):
        return pl.pallas_call(
            grad_mix_body, out_shape=pltpu.HBM(pack_shape, BF), in_specs=[HBM] + [VMEM] * 4, out_specs=HBM,
            scratch_shapes=[pltpu.VMEM((PACK_ROWS, width), BF), sem((3,))], compiler_params=params, name="grad_mix",
            input_output_aliases={0: 0},
        )(in_hbm(pack), keep, swap(send, "segment"), ig, swap(ig, "segment"))

    def scatter(pack, by):
        order = [ring[by:] + ring[:by]]
        return lax.psum_scatter(pack, "dp", scatter_dimension=0, axis_index_groups=order, tiled=True)

    pack1 = grad_ffn(keep, send)
    dh, dxo, keep, send, ig, misc1 = kba(1, xo, xr, dfe1, h1_1, x1_1, mixed1, save1, (pack1,))
    xo, xr = exchange(dxo)
    pack1 = grad_mix(pack1, keep, send, ig)
    part1 = scatter(pack1, turn)
    ig1, gg1, dfe0, dxt, keep, send = call(
        kbf_body, "ffn_bwd0",
        [dl, hm, dh, xo, xr, *small_p, x2_0, hid_0, sl_0, si_0, *sw_p, *dn_p],
        [SMEM, LOAD, LOAD] + [VMEM] * 2 + [HBM] * 2 + [LOAD] * 4 + [HBM] * 4,
        [(tok, F32, 1), ((1, width), F32), (tok, BF), (tok, BF), (pack_f, BF), (pack_f, BF)],
        ffn_scratch + [sem((1,)), sem((2,))], (pack1,))
    pack0 = grad_ffn(keep, send)
    xo, xr = exchange(dxt)
    after = (pack0,) if turn else (pack0, part1)
    dh, dxo, keep, send, ig, misc0 = kba(0, xo, xr, dfe0, h1_0, x1_0, mixed0, save0, after)
    xo, xr = exchange(dxo)
    pack0 = grad_mix(pack0, keep, send, ig)
    part0 = scatter(pack0, 0)
    ig0, gg0 = call(ke_body, "input_grad0", [dl, h0, dh, xo, xr, *small_p],
                    [SMEM, LOAD, LOAD] + [VMEM] * 2 + [HBM] * 2, [(tok, F32, 1), ((1, width), F32)],
                    [pltpu.VMEM(small.shape, F32), sem((1,))], (pack0,))

    left = jnp.where(first, part0, lax.ppermute(part1, "segment", [(0, 1)]))
    right = jnp.where(first, lax.ppermute(part0, "segment", [(1, 0)]), part1)
    whole = lax.all_gather(cat([left, right], 1), "dp", axis=0, axis_index_groups=[ring], tiled=True)

    def lo1_body(dl_ref, h1_ref, fo_ref, fr_ref, lo_ref):
        begin, _ = doc_places(dl_ref, length // (2 * MBT))
        low = (h1_ref[...] + (fo_ref[...].astype(F32) + fr_ref[...].astype(F32))).astype(BF)
        scatter_rows(lo_ref, block_starts(begin, length // (2 * MBT)), low)

    (lo1,) = call(lo1_body, "output1", [dl, h1_1, fo, fr], [SMEM, LOAD] + [VMEM] * 2, [(tok, BF, 1)], (), (pack0,))

    def two_rows(zero, one):
        mine, theirs = jnp.where(first, zero, one), swap(jnp.where(first, one, zero), "segment")
        return jnp.where(first, jnp.stack([mine, theirs]), jnp.stack([theirs, mine]))[None, :, None]

    layer_output = two_rows(lo0, lo1)
    input_grads = two_rows(ig0, ig1)
    total = cat([misc0, misc1, gg0.reshape(3, hid), gg1.reshape(3, hid)], 0)
    total = total + swap(total, "segment")
    for k in range(dp.bit_length() - 1):
        total = total + lax.ppermute(total, "dp", [(i, i ^ (1 << k)) for i in range(dp)])
    rows = STAT_ROW + dp
    tail = total[2 * rows :]
    misc = jnp.where(first, total[:rows], total[rows : 2 * rows])
    gain_one = jnp.where(first, tail[:3], tail[3:]).reshape(width)
    g_rate = cat([misc[RATE_ROW + heads * j : RATE_ROW + heads * (j + 1)] for j in range(3)], 1).T[None]
    g_hidden = misc[HIDDEN_ROW : HIDDEN_ROW + heads][None]
    tail = misc[HEAD_ROW : HEAD_ROW + 6].reshape(4, heads, 64)
    g_result, g_heads, g_shift = tail[0][None], tail[1:3][None], tail[3][None]
    g_offset = misc[OFFSET_ROW, :heads][None]
    g_gains = jnp.stack([gain_one, misc[GAIN_ROW : GAIN_ROW + 3].reshape(width)])[None]
    rate_stats = misc[STAT_ROW:].reshape(dp, micro, 128)[:, :, :64].reshape(dp, micro, 2, 2, 16)
    rate_stats = jnp.transpose(rate_stats[..., :heads], (1, 0, 2, 3, 4)).reshape(1, micro, dp, 2, 2 * heads)
    g_sw, g_dn, g_mix, g_out, g_expand, g_contract = call(
        functools.partial(final_body, turn), "final", [whole], [HBM],
        [((width, 2, ff), F32, 4), ((ff, width), F32, 2), ((width, 4, wide), F32, 4), ((wide, width), F32, 1),
         ((wide, hid), F32, 1), ((wide, hid), F32, 1)],
        [pltpu.VMEM(whole.shape, BF), sem((8,))], vmem=40)
    g_expand = g_expand.reshape(expand.shape)
    g_contract = jnp.swapaxes(g_contract.reshape(1, heads, 64, hid), 2, 3)
    return (
        layer_output, input_grads, g_gains, g_mix[None], g_rate, g_offset, g_expand, g_hidden, g_contract, g_result,
        g_heads, g_shift, g_out[None], g_sw[None], g_dn[None], rate_stats,
    )


def solution(mesh):
    placed = (
        P(None, "dp", None, None),
        P(None, "dp", None),
        P("segment", None, None),
        P("segment", None, None, "tensor"),
        P("segment", None, "tensor"),
        P("segment", "tensor"),
        P("segment", "tensor", None, None),
        P("segment", "tensor", None),
        P("segment", "tensor", None, None),
        P("segment", "tensor", None),
        P("segment", None, "tensor", None),
        P("segment", "tensor", None),
        P("segment", "tensor", None),
        P("segment", None, None, "tensor"),
        P("segment", "tensor", None),
        P(None, "dp", None, None),
    )
    return jax.shard_map(
        shards,
        mesh=mesh,
        in_specs=placed,
        out_specs=(
            P("segment", None, "dp", None, None),
            P("segment", None, "dp", None, None),
            P("segment", None, None),
            P("segment", None, None, "tensor"),
            P("segment", None, "tensor"),
            P("segment", "tensor"),
            P("segment", "tensor", None, None),
            P("segment", "tensor", None),
            P("segment", "tensor", None, None),
            P("segment", "tensor", None),
            P("segment", None, "tensor", None),
            P("segment", "tensor", None),
            P("segment", "tensor", None),
            P("segment", None, None, "tensor"),
            P("segment", "tensor", None),
            P("segment", None, None, None, None),
        ),
        check_vma=False,
    )
```

```python
import functools
import jax
import jax.numpy as jnp
from jax import lax
from jax.experimental import pallas as pl
from jax.experimental.pallas import tpu as pltpu
from jax.sharding import PartitionSpec as P

MBT = 16
EPS = 1e-06
RATE = 0.125
C0 = 0.7978845608028654
BF = jnp.bfloat16
F32 = jnp.float32
VMEM = pl.BlockSpec(memory_space=pltpu.VMEM)
SMEM = pl.BlockSpec(memory_space=pltpu.SMEM)
HBM = pl.BlockSpec(memory_space=pltpu.HBM)
LOAD = "load"
NRM, INV, MIS, MEANN, GZ2 = range(5)
NA, INVA, NO, INVO, GATE = range(5)
RATE_ROW, HIDDEN_ROW, HEAD_ROW, OFFSET_ROW, GAIN_ROW, STAT_ROW = 0, 18, 24, 30, 31, 40
PACK_ROWS = 1152


def dot(a, b):
    return jnp.dot(a, b, preferred_element_type=F32)


def dot_t(a, b):
    return lax.dot_general(a, b, (((1,), (1,)), ((), ())), preferred_element_type=F32)


def tdot(a, b):
    return lax.dot_general(a, b, (((0,), (0,)), ((), ())), preferred_element_type=F32)


def cat(parts, axis):
    return jnp.concatenate(parts, axis=axis)


def gelu_parts(z):
    z2 = z * z
    t = jnp.tanh(C0 * z * (1.0 + 0.044715 * z2))
    h = 0.5 * (1.0 + t)
    du = C0 * (1.0 + 0.134145 * z2)
    sech = 1.0 - t * t
    value = z * h
    slope = h + 0.5 * z * sech * du
    return value, slope, t, z2, du, sech


def gelu_two(z):
    value, slope, _, _, _, _ = gelu_parts(z)
    return value, slope


def gelu_curve(z):
    _, _, t, z2, du, sech = gelu_parts(z)
    return sech * (C0 * (1.0 + 0.26829 * z2) - z * t * du * du)


def rms_inv(values):
    return lax.rsqrt(jnp.mean(values * values, axis=-1, keepdims=True) + EPS)


class Pick:
    def __init__(self, layer, sems):
        self.own = lax.axis_index("segment") == layer
        self.sems = sems
        self.count = 0

    def start(self, own_ref, other_ref, dst):
        sem = self.sems.at[self.count]
        self.count += 1

        @pl.when(self.own)
        def _():
            pltpu.make_async_copy(own_ref, dst, sem).start()

        @pl.when(jnp.logical_not(self.own))
        def _():
            pltpu.make_async_copy(other_ref, dst, sem).start()

        return pltpu.make_async_copy(own_ref, dst, sem)


def doc_places(dl_ref, steps):
    core = lax.axis_index("segment")
    one, two = dl_ref[core, 0], dl_ref[core, 1]
    begin = jnp.where(one == steps, 0, jnp.where(two == steps, one, one + two))
    cut = jnp.where(one == steps, two, one)
    return begin, cut


def block_starts(begin, steps):
    places = []
    for s in range(steps):
        places.append(pl.multiple_of((begin + s) * MBT, MBT))
        places.append(pl.multiple_of(jnp.where(s < begin, s, s + steps) * MBT, MBT))
    return places


def gather_rows(ref, lead, places):
    return cat([ref[lead, pl.ds(p, MBT), :] for p in places], 0)


def scatter_rows(ref, places, value):
    for i, p in enumerate(places):
        ref[pl.ds(p, MBT), :] = value[i * MBT : (i + 1) * MBT, :]


def turned_mask(cut, length):
    i = lax.broadcasted_iota(jnp.int32, (length, length), 0)
    j = lax.broadcasted_iota(jnp.int32, (length, length), 1)
    si, li, sj, lj = i >> 5, (i >> 4) & 1, length // 32 - 1 - (j >> 5), (j >> 4) & 1
    di = jnp.where(li == 0, 0, jnp.where(si < cut, 1, 2))
    dj = jnp.where(lj == 0, 0, jnp.where(sj < cut, 1, 2))
    return jnp.where((di == dj) & (si < sj), 1.0 / MBT, 0.0)


def masks(cut, length):
    def parts(axis):
        i = lax.broadcasted_iota(jnp.int32, (length, length), axis)
        step, lane, t = i >> 5, (i >> 4) & 1, i & 15
        doc = jnp.where(lane == 0, 0, jnp.where(step < cut, 1, 2))
        return step, lane, t, doc

    s0, l0, t0, d0 = parts(0)
    s1, l1, t1, d1 = parts(1)
    same = d0 == d1
    block = (s0 == s1) & (l0 == l1)
    past = jnp.where(same & (s1 < s0), 1.0 / MBT, 0.0)
    past_t = jnp.where(same & (s0 < s1), 1.0 / MBT, 0.0)
    inside = jnp.where(block & (t1 <= t0), 1.0 / (t0 + 1).astype(F32), 0.0)
    inside_t = jnp.where(block & (t0 <= t1), 1.0 / (t1 + 1).astype(F32), 0.0)
    return past, past + inside, past_t, past_t + inside_t


class Halves:
    def __init__(self):
        lane = lax.broadcasted_iota(jnp.int32, (1, 128), 1)
        self.left = lane < 64
        r = lax.broadcasted_iota(jnp.int32, (256, 128), 0) & 127
        c = lax.broadcasted_iota(jnp.int32, (256, 128), 1)
        self.mean_mat = jnp.where((r < 64) == (c < 64), 1.0 / 64.0, 0.0).astype(BF)

    def mean(self, x):
        high = x.astype(BF)
        low = (x - high.astype(F32)).astype(BF)
        return dot(cat([high, low], 1), self.mean_mat)

    def split(self, x):
        zero = jnp.zeros_like(x)
        return cat([jnp.where(self.left, x, zero), jnp.where(self.left, zero, x)], 0)

    def pack(self, a, b):
        return jnp.where(self.left, a, b)

    def both(self, weights, values):
        rows = weights[0].shape[0]
        full = dot(cat(weights, 0), values)
        return self.pack(full[:rows], full[rows:])


def pair_weights(inner_ref, small_ref, heads, p, halves):
    width = inner_ref.shape[2]
    zero = jnp.zeros((64, width), BF)

    def blocks(a, b):
        return cat([cat([a, zero], 1), cat([zero, b], 1)], 0)

    def centred(index):
        w = inner_ref[heads + index].astype(F32)
        return (w - jnp.mean(w, axis=0, keepdims=True)).astype(BF)

    w1 = blocks(inner_ref[2 * p], inner_ref[2 * p + 1])
    w2 = blocks(centred(2 * p), centred(2 * p + 1))
    return w1, w2


def join(parts):
    return cat(parts, 0) if len(parts) > 1 else parts[0]


def pad_rows(parts, rows):
    have = sum(x.shape[0] for x in parts)
    if have < rows:
        parts = parts + [jnp.zeros((rows - have, parts[0].shape[1]), parts[0].dtype)]
    return cat(parts, 0) if len(parts) > 1 else parts[0]


def mixer_unrolled(refs, x_one, mix_ref, rate_ref, inner_ref, small_ref, begin_cut, x1_ready):
    (mixed_ref, stats_ref, kq_ref, x2_ref, g1_ref, y2_ref, d1_ref, ud2_ref, e1_ref, sm_ref, so_ref, sg_ref) = refs
    _, cut = begin_cut
    length = x_one.shape[0]
    heads = inner_ref.shape[0] // 2
    pairs = heads // 2
    hid = inner_ref.shape[2]
    wide = heads * 64
    steps = length // (2 * MBT)
    rows = 2 * MBT
    past, near, _, _ = masks(cut, length)
    hv = Halves()
    proj = dot(x_one, mix_ref[...])
    logits = dot_t(x_one, rate_ref[...]) + small_ref[3:4, 0:16]
    sg = jax.nn.sigmoid(logits)
    sg_ref[...] = sg
    stats_ref[...] = cat(
        [jnp.mean(sg, axis=0, keepdims=True), jnp.max(sg, axis=0, keepdims=True)], 0
    )
    rates = RATE * sg
    st = []
    for p in range(pairs):
        c = slice(128 * p, 128 * p + 128)
        h = slice(2 * hid * p, 2 * hid * (p + 1))
        q, k, v, gate = [proj[:, wide * i + 128 * p : wide * i + 128 * p + 128] for i in range(4)]
        d = dict(q=q, gate=gate, diff=v - k, c=c, h=h)
        d["w1"], d["w2"] = pair_weights(inner_ref, small_ref, heads, p, hv)
        d["b1"] = small_ref[0:1, h]
        b2 = small_ref[2:3, 128 * p : 128 * p + 128]
        d["b2"] = b2 - hv.mean(jnp.broadcast_to(b2, (8, 128)))[0:1]
        d["g"] = small_ref[2:3, wide + 128 * p : wide + 128 * p + 128]
        d["gp"] = small_ref[2:3, 2 * wide + 128 * p : 2 * wide + 128 * p + 128]
        d["be"] = small_ref[2:3, 3 * wide + 128 * p : 3 * wide + 128 * p + 128]
        d["r"] = [rates[:, 2 * p + i : 2 * p + i + 1] for i in range(2)]
        d["rp"] = hv.pack(d["r"][0], d["r"][1])
        d["kb"], d["qb"] = k.astype(BF), q.astype(BF)
        kq_ref[:, c] = d["kb"]
        kq_ref[:, wide + 128 * p : wide + 128 * p + 128] = d["qb"]
        d["base"] = dot(d["kb"], d["w1"]) + d["b1"]
        kk = dot_t(hv.split(d["kb"]), d["kb"])
        d["m1"] = [(past * (kk[i * length : (i + 1) * length] + 1.0)).astype(BF) for i in range(2)]
        for name in ("x2", "g1", "g2", "z1", "u"):
            d[name] = []
        st.append(d)
    kq_ref.send()
    sg_ref.send()
    for s in range(steps):
        sl = slice(rows * s, rows * s + rows)
        for p in range(pairs):
            d = st[p]
            c, h = d["c"], d["h"]
            z1 = d["base"][sl]
            if s:
                g1 = pad_rows(d["g1"], length)
                x2 = pad_rows(d["x2"], length)
                g2 = pad_rows(d["g2"], length)
                z1 = z1 - cat([dot(d["m1"][i][sl], g1[:, hid * i : hid * (i + 1)]) for i in range(2)], 1)
            act, slope = gelu_two(z1)
            actb = act.astype(BF)
            z2 = dot_t(actb, d["w2"]) + d["b2"]
            if s:
                far = [
                    (past[sl] * (dot_t(actb[:, hid * i : hid * (i + 1)], x2[:, hid * i : hid * (i + 1)]) + 1.0)).astype(BF)
                    for i in range(2)
                ]
                z2 = z2 - dot(cat(far, 1), hv.split(g2))
            inv = lax.rsqrt(hv.mean(z2 * z2) + EPS)
            n = z2 * inv
            mis = n * d["g"] + d["be"] - d["diff"][sl]
            misg = mis * d["g"]
            both = hv.mean(cat([misg, misg * n], 0))
            gz2 = (misg - both[:rows] - n * both[rows:]) * inv
            gz2b = gz2.astype(BF)
            u = dot(gz2b, d["w2"])
            if s:
                f = dot_t(hv.split(gz2b), g2)
                u = u - cat(
                    [
                        dot((past[sl] * f[rows * i : rows * (i + 1)]).astype(BF), x2[:, hid * i : hid * (i + 1)])
                        for i in range(2)
                    ],
                    1,
                )
            gz1 = u * slope
            r0, r1 = d["r"][0][sl], d["r"][1][sl]
            g1n = cat([gz1[:, :hid] * r0, gz1[:, hid:] * r1], 1).astype(BF)
            g2n = (gz2 * d["rp"][sl]).astype(BF)
            d["x2"].append(actb)
            d["g1"].append(g1n)
            d["g2"].append(g2n)
            d["z1"].append(z1)
            d["u"].append(u)
            x2_ref[sl, h] = actb
            g1_ref[sl, h] = g1n
            d1_ref[sl, h] = slope.astype(BF)
            sm_ref[NRM, sl, c] = n
            sm_ref[INV, sl, c] = inv
            sm_ref[MIS, sl, c] = mis
            sm_ref[MEANN, sl, c] = both[rows:]
            sm_ref[GZ2, sl, c] = gz2
    for ref in (x2_ref, g1_ref, d1_ref, sm_ref):
        ref.send()
    mixed = []
    for p in range(pairs):
        d = st[p]
        c, h = d["c"], d["h"]
        g1, x2, g2 = cat(d["g1"], 0), cat(d["x2"], 0), cat(d["g2"], 0)
        ud2_ref[:, h] = (cat(d["u"], 0) * gelu_curve(cat(d["z1"], 0))).astype(BF)
        qk = dot_t(hv.split(d["qb"]), d["kb"])
        corr = [
            dot((near * (qk[length * i : length * (i + 1)] + 1.0)).astype(BF), g1[:, hid * i : hid * (i + 1)])
            for i in range(2)
        ]
        act, slope = gelu_two(dot(d["qb"], d["w1"]) + d["b1"] - cat(corr, 1))
        actb = act.astype(BF)
        y2_ref[:, h] = actb
        e1_ref[:, h] = slope.astype(BF)
        far = [
            (near * (dot_t(actb[:, hid * i : hid * (i + 1)], x2[:, hid * i : hid * (i + 1)]) + 1.0)).astype(BF)
            for i in range(2)
        ]
        a2 = dot_t(actb, d["w2"]) + d["b2"] - dot(cat(far, 1), hv.split(g2))
        inv_a = lax.rsqrt(hv.mean(a2 * a2) + EPS)
        n_a = a2 * inv_a
        out = d["q"] + n_a * d["g"] + d["be"]
        inv_o = lax.rsqrt(hv.mean(out * out) + EPS)
        n_o = out * inv_o
        gated, _ = gelu_two(d["gate"])
        low = (gated * n_o * d["gp"]).astype(BF)
        mixed_ref[:, c] = low
        mixed.append(low)
        so_ref[NA, :, c] = n_a
        so_ref[INVA, :, c] = inv_a
        so_ref[NO, :, c] = n_o
        so_ref[INVO, :, c] = inv_o
        so_ref[GATE, :, c] = d["gate"]
    return cat(mixed, 1)


def mixer_forward(refs, x_one, mix_ref, rate_ref, inner_ref, small_ref, begin_cut, work):
    (mixed_ref, stats_ref, kq_ref, x2_ref, g1_ref, y2_ref, d1_ref, ud2_ref, e1_ref, sm_ref, so_ref, sg_ref) = refs
    base_ref, z1_ref, u_ref, m1_ref, g2_ref, w2_ref, past_ref, diff_ref, b2_ref = work
    x2_buf, g1_buf = x2_ref.buf, g1_ref.buf
    _, cut = begin_cut
    length = x_one.shape[0]
    heads = inner_ref.shape[0] // 2
    pairs = heads // 2
    hid = inner_ref.shape[2]
    wide = heads * 64
    steps = length // (2 * MBT)
    rows = 2 * MBT
    past, near, _, _ = masks(cut, length)
    past_ref[...] = past
    hv = Halves()
    proj = dot(x_one, mix_ref[...])
    logits = dot_t(x_one, rate_ref[...]) + small_ref[3:4, 0:16]
    sg = jax.nn.sigmoid(logits)
    sg_ref[...] = sg
    stats_ref[...] = cat(
        [jnp.mean(sg, axis=0, keepdims=True), jnp.max(sg, axis=0, keepdims=True)], 0
    )
    x2_buf[...] = jnp.zeros(x2_buf.shape, BF)
    g1_buf[...] = jnp.zeros(g1_buf.shape, BF)
    g2_ref[...] = jnp.zeros(g2_ref.shape, BF)

    def lanes(p):
        return slice(128 * p, 128 * p + 128), slice(2 * hid * p, 2 * hid * (p + 1))

    def row_of(k, p):
        return small_ref[2:3, wide * k + 128 * p : wide * k + 128 * p + 128]

    firsts = []
    for p in range(pairs):
        c, h = lanes(p)
        q, k, v, gate = [proj[:, wide * i + 128 * p : wide * i + 128 * p + 128] for i in range(4)]
        w1, w2_ref[p] = pair_weights(inner_ref, small_ref, heads, p, hv)
        b2 = row_of(0, p)
        b2_ref[0:1, c] = b2 - hv.mean(jnp.broadcast_to(b2, (8, 128)))[0:1]
        kb, qb = k.astype(BF), q.astype(BF)
        kq_ref[:, c] = kb
        kq_ref[:, wide + 128 * p : wide + 128 * p + 128] = qb
        diff_ref[:, c] = v - k
        so_ref[GATE, :, c] = gate
        base_ref[:, h] = dot(kb, w1) + small_ref[0:1, h]
        kk = dot_t(hv.split(kb), kb)
        for i in range(2):
            m1_ref[2 * p + i] = (past * (kk[i * length : (i + 1) * length] + 1.0)).astype(BF)
        firsts.append((q, kb, qb, w1))
    kq_ref.send()
    sg_ref.send()

    def step(s, carry, start=False):
        at = slice(0, rows) if start else pl.ds(pl.multiple_of(s * rows, rows), rows)
        hv = Halves()
        mask = past_ref[at, :]
        rates = RATE * sg_ref.buf[at, :]
        for p in range(pairs):
            c, h = lanes(p)

            def half(i):
                return slice(2 * hid * p + hid * i, 2 * hid * p + hid * (i + 1))

            w2, g2 = w2_ref[p], g2_ref[p]
            g = row_of(1, p)
            z1 = base_ref[at, h]
            if not start:
                z1 = z1 - cat([dot(m1_ref[2 * p + i, at, :], g1_buf[:, half(i)]) for i in range(2)], 1)
            act, slope = gelu_two(z1)
            actb = act.astype(BF)
            z2 = dot_t(actb, w2) + b2_ref[0:1, c]
            if not start:
                far = [
                    (mask * (dot_t(actb[:, hid * i : hid * (i + 1)], x2_buf[:, half(i)]) + 1.0)).astype(BF)
                    for i in range(2)
                ]
                z2 = z2 - hv.both(far, g2)
            inv = lax.rsqrt(hv.mean(z2 * z2) + EPS)
            n = z2 * inv
            mis = n * g + row_of(3, p) - diff_ref[at, c]
            misg = mis * g
            both = hv.mean(cat([misg, misg * n], 0))
            gz2 = (misg - both[:rows] - n * both[rows:]) * inv
            gz2b = gz2.astype(BF)
            u = dot(gz2b, w2)
            if not start:
                f = dot_t(hv.split(gz2b), g2)
                u = u - cat(
                    [dot((mask * f[rows * i : rows * (i + 1)]).astype(BF), x2_buf[:, half(i)]) for i in range(2)], 1
                )
            gz1 = u * slope
            r0, r1 = rates[:, 2 * p : 2 * p + 1], rates[:, 2 * p + 1 : 2 * p + 2]
            x2_buf[at, h] = actb
            g1_buf[at, h] = cat([gz1[:, :hid] * r0, gz1[:, hid:] * r1], 1).astype(BF)
            g2_ref[p, at, :] = (gz2 * hv.pack(r0, r1)).astype(BF)
            z1_ref[at, h] = z1
            u_ref[at, h] = u
            d1_ref[at, h] = slope.astype(BF)
            sm_ref[NRM, at, c] = n
            sm_ref[INV, at, c] = inv
            sm_ref[MIS, at, c] = mis
            sm_ref[MEANN, at, c] = both[rows:]
            sm_ref[GZ2, at, c] = gz2
        return carry

    step(0, 0, True)
    lax.fori_loop(1, steps, step, 0)
    for ref in (x2_ref, g1_ref, d1_ref, sm_ref):
        ref.send()
    mixed = []
    for p in range(pairs):
        c, h = lanes(p)
        q, kb, qb, w1 = firsts[p]
        g1, x2, g2, w2 = g1_buf[:, h], x2_buf[:, h], g2_ref[p], w2_ref[p]
        ud2_ref[:, h] = (u_ref[:, h] * gelu_curve(z1_ref[:, h])).astype(BF)
        qk = dot_t(hv.split(qb), kb)
        corr = [
            dot((near * (qk[length * i : length * (i + 1)] + 1.0)).astype(BF), g1[:, hid * i : hid * (i + 1)])
            for i in range(2)
        ]
        act, slope = gelu_two(dot(qb, w1) + small_ref[0:1, h] - cat(corr, 1))
        actb = act.astype(BF)
        y2_ref[:, h] = actb
        e1_ref[:, h] = slope.astype(BF)
        far = [
            (near * (dot_t(actb[:, hid * i : hid * (i + 1)], x2[:, hid * i : hid * (i + 1)]) + 1.0)).astype(BF)
            for i in range(2)
        ]
        a2 = dot_t(actb, w2) + b2_ref[0:1, c] - hv.both(far, g2)
        inv_a = lax.rsqrt(hv.mean(a2 * a2) + EPS)
        n_a = a2 * inv_a
        out = q + n_a * row_of(1, p) + row_of(3, p)
        inv_o = lax.rsqrt(hv.mean(out * out) + EPS)
        n_o = out * inv_o
        gated, _ = gelu_two(so_ref.buf[GATE, :, c])
        low = (gated * n_o * row_of(2, p)).astype(BF)
        mixed_ref[:, c] = low
        mixed.append(low)
        so_ref[NA, :, c] = n_a
        so_ref[INVA, :, c] = inv_a
        so_ref[NO, :, c] = n_o
        so_ref[INVO, :, c] = inv_o
    return cat(mixed, 1)


def mixer_backward(dmixed, mixed_refs, inner_ref, small_ref, begin_cut, ig_ref, ms_ref):
    (kq_ref, x2_ref, g1_ref, y2_ref, d1_ref, ud2_ref, e1_ref, sm_ref, so_ref, sg_ref) = mixed_refs
    _, cut = begin_cut
    length = dmixed.shape[0]
    heads = inner_ref.shape[0] // 2
    pairs = heads // 2
    hid = inner_ref.shape[2]
    wide = heads * 64
    steps = length // (2 * MBT)
    rows = 2 * MBT
    past, near, past_t, near_t = masks(cut, length)
    hv = Halves()

    def turned(x):
        return cat([x[rows * k : rows * (k + 1)] for k in reversed(range(steps))], 0)

    past_b = turned_mask(cut, length)
    sg = sg_ref[...]
    rates = RATE * sg

    def by_head(fn):
        return [fn(slice(hid * i, hid * (i + 1)), i) for i in range(2)]

    st = []
    for p in range(pairs):
        c = slice(128 * p, 128 * p + 128)
        h = slice(2 * hid * p, 2 * hid * (p + 1))
        d = dict(c=c, h=h)
        d["w1"], d["w2"] = pair_weights(inner_ref, small_ref, heads, p, hv)
        g = small_ref[2:3, wide + 128 * p : wide + 128 * p + 128]
        gp = small_ref[2:3, 2 * wide + 128 * p : 2 * wide + 128 * p + 128]
        d["g"] = g
        d["r"] = [rates[:, 2 * p + i : 2 * p + i + 1] for i in range(2)]
        d["rp"] = hv.pack(d["r"][0], d["r"][1])
        kb = kq_ref[:, c]
        qb = kq_ref[:, wide + 128 * p : wide + 128 * p + 128]
        x2, g1, y2 = x2_ref[:, h], g1_ref[:, h], y2_ref[:, h]
        gz2 = sm_ref[GZ2, :, c]
        gz2b = gz2.astype(BF)
        g2b = (gz2 * d["rp"]).astype(BF)
        dm = dmixed[:, c]
        gate = so_ref[GATE, :, c]
        n_o, inv_o = so_ref[NO, :, c], so_ref[INVO, :, c]
        n_a, inv_a = so_ref[NA, :, c], so_ref[INVA, :, c]
        gated, gate_slope = gelu_two(gate)
        d["dgate"] = dm * n_o * gp * gate_slope
        drm = dm * gated
        d["dgp"] = jnp.sum(drm * n_o, axis=0, keepdims=True)
        dpg = drm * gp
        do = (dpg - n_o * hv.mean(dpg * n_o)) * inv_o
        dn = do * g
        both = hv.mean(cat([dn, dn * n_a], 0))
        da2 = (dn - both[:length] - n_a * both[length:]) * inv_a
        d["dg"] = jnp.sum(do * n_a, axis=0, keepdims=True)
        d["dbe"] = jnp.sum(do, axis=0, keepdims=True)
        d["db2"] = jnp.sum(da2, axis=0, keepdims=True)
        da2b = da2.astype(BF)
        da2m, g2m = hv.split(da2b), hv.split(g2b)
        km = hv.split(kb)

        def weigh(mask, full, i):
            return (mask * full[length * i : length * (i + 1)]).astype(BF)

        p2 = dot_t(da2m, g2b)
        p2t = dot_t(g2m, da2b)
        dy2 = dot(da2b, d["w2"]) - cat(by_head(lambda e, i: dot(weigh(near, p2, i), x2[:, e])), 1)
        d["bx2"] = cat(by_head(lambda e, i: dot(weigh(near_t, p2t, i), y2[:, e])), 1)
        syt = by_head(lambda e, i: (near_t * (dot_t(x2[:, e], y2[:, e]) + 1.0)).astype(BF))
        d["bg2"] = -hv.both(syt, da2b)
        da1 = dy2 * e1_ref[:, h].astype(F32)
        da1b = da1.astype(BF)
        d["db1"] = jnp.sum(da1, axis=0, keepdims=True)
        p1 = by_head(lambda e, i: (near * dot_t(da1b[:, e], g1[:, e])).astype(BF))
        p1t = by_head(lambda e, i: (near_t * dot_t(g1[:, e], da1b[:, e])).astype(BF))
        d["dq"] = do + dot_t(da1b, d["w1"]) - hv.both(p1, kb)
        d["dk"] = -hv.both(p1t, qb)
        kq = dot_t(km, qb) + 1.0
        kk = dot_t(km, turned(kb)) + 1.0
        d["bg1"] = cat(by_head(lambda e, i: dot(weigh(near_t, kq, i), da1b[:, e])), 1)
        x2r, gz2r = turned(x2), turned(gz2b)
        d["m1t"] = [weigh(past_b, kk, i) for i in range(2)]
        d["rx"] = by_head(lambda e, i: (past_b * (dot_t(x2[:, e], x2r[:, e]) + 1.0)).astype(BF))
        ft = dot_t(g2m, gz2r)
        d["ft"] = [weigh(past_b, ft, i) for i in range(2)]
        d.update(x2=x2, y2=y2, g1=g1, g2b=g2b, gz2=gz2, gz2b=gz2b, x2r=x2r, gz2r=gz2r)
        d.update(kb=kb, qb=qb, da1b=da1b, da2b=da2b)
        for name in ("z1", "z2", "u", "rg1", "rg2", "t"):
            d[name] = [None] * steps
        st.append(d)
    for s in reversed(range(steps)):
        sl = slice(rows * s, rows * s + rows)
        later = length - rows * (s + 1)
        mask = past_b[sl, :later]
        for p in range(pairs):
            d = st[p]
            c, h = d["c"], d["h"]
            x2, x2e, g2e = d["x2"], d["x2"][: rows * s], d["g2b"][: rows * s]
            bg1, bg2, bx2 = -d["bg1"][sl], d["bg2"][sl], -d["bx2"][sl]
            if s < steps - 1:

                def full(parts):
                    return join(parts[: s : -1])

                z1l, z2l, ul = full(d["z1"]), full(d["z2"]), full(d["u"])
                x2l = d["x2r"][:later]
                bg1 = bg1 - cat(by_head(lambda e, i: dot(d["m1t"][i][sl, :later], z1l[:, e])), 1)
                xu = by_head(lambda e, i: (mask * dot_t(x2[sl, e], ul[:, e])).astype(BF))
                bg2 = bg2 - hv.both([d["rx"][i][sl, :later] for i in range(2)], z2l) - hv.both(xu, d["gz2r"][:later])
                gz = dot_t(hv.split(d["g2b"][sl]), z2l)
                bx2 = bx2 - cat(
                    by_head(
                        lambda e, i: dot((mask * gz[rows * i : rows * (i + 1)]).astype(BF), x2l[:, e])
                        + dot(d["ft"][i][sl, :later], ul[:, e])
                    ),
                    1,
                )
            r0, r1 = d["r"][0][sl], d["r"][1][sl]
            dgz1 = cat([bg1[:, :hid] * r0, bg1[:, hid:] * r1], 1)
            slope = d1_ref[sl, h].astype(F32)
            du = dgz1 * slope
            dub = du.astype(BF)
            dz1 = dgz1 * ud2_ref[sl, h].astype(F32)
            dgz2 = bg2 * d["rp"][sl] + dot_t(dub, d["w2"])
            if s:
                hm = by_head(lambda e, i: (past[sl, : rows * s] * dot_t(dub[:, e], x2e[:, e])).astype(BF))
                dgz2 = dgz2 - hv.both(hm, g2e)
            n, inv = sm_ref[NRM, sl, c], sm_ref[INV, sl, c]
            mis, mn = sm_ref[MIS, sl, c], sm_ref[MEANN, sl, c]
            g = d["g"]
            e = dgz2 * inv
            three = hv.mean(cat([e, e * n, dgz2 * d["gz2"][sl]], 0))
            dmis = e - three[:rows] - n * three[rows : 2 * rows]
            t = dmis * g
            dn = t * g - e * mn - mis * g * three[rows : 2 * rows]
            two = hv.mean(cat([dn, dn * n], 0))
            dz2 = inv * (dn - two[:rows] - n * (two[rows:] + three[2 * rows :]))
            d["dg"] = d["dg"] + jnp.sum(t * n + dmis * mis, axis=0, keepdims=True)
            d["dbe"] = d["dbe"] + jnp.sum(t, axis=0, keepdims=True)
            d["db2"] = d["db2"] + jnp.sum(dz2, axis=0, keepdims=True)
            dz2b = dz2.astype(BF)
            dx2 = bx2 + dot(dz2b, d["w2"])
            if s:
                j = dot_t(hv.split(dz2b), g2e)
                dx2 = dx2 - cat(
                    by_head(
                        lambda e, i: dot((past[sl, : rows * s] * j[rows * i : rows * (i + 1)]).astype(BF), x2e[:, e])
                    ),
                    1,
                )
            dz1 = dz1 + dx2 * slope
            d["db1"] = d["db1"] + jnp.sum(dz1, axis=0, keepdims=True)
            d["z1"][s], d["z2"][s], d["u"][s] = dz1.astype(BF), dz2b, dub
            d["rg1"][s], d["rg2"][s], d["t"][s] = bg1, bg2, t
    parts = [[], [], [], []]
    rate_cols = []
    for p in range(pairs):
        d = st[p]
        z1, z2, u = cat(d["z1"], 0), cat(d["z2"], 0), cat(d["u"], 0)
        t = cat(d["t"], 0)
        g1 = d["g1"]
        both = by_head(
            lambda e, i: (past * dot_t(z1[:, e], g1[:, e]) + past_t * dot_t(g1[:, e], z1[:, e])).astype(BF)
        )
        dk = d["dk"] + t + dot_t(z1, d["w1"]) - hv.both(both, d["kb"])
        for i, value in enumerate((d["dq"], dk, -t, d["dgate"])):
            parts[i].append(value.astype(BF))
        dw1 = tdot(cat([d["kb"], d["qb"]], 0), cat([z1, d["da1b"]], 0))
        dw2 = tdot(cat([z2, d["da2b"], d["gz2b"]], 0), cat([d["x2"], d["y2"], u], 0))
        for i in range(2):
            row = 64 * (2 * p + i)
            ig_ref[row : row + 64, :] = dw1[64 * i : 64 * i + 64, hid * i : hid * (i + 1)].astype(BF)
            row = row + 64 * heads
            ig_ref[row : row + 64, :] = dw2[64 * i : 64 * i + 64, hid * i : hid * (i + 1)].astype(BF)
            row = HIDDEN_ROW + 2 * p + i
            ms_ref[row : row + 1, :] = d["db1"][:, hid * i : hid * (i + 1)]
        one = cat(d["rg1"], 0) * g1.astype(F32)
        two = cat(d["rg2"], 0) * d["g2b"].astype(F32)
        two = cat([jnp.where(hv.left, two, 0.0), jnp.where(hv.left, 0.0, two)], 1)
        for i in range(2):
            whole = one[:, hid * i : hid * i + 128] + one[:, hid * i + 128 : hid * (i + 1)]
            whole = whole + two[:, 128 * i : 128 * (i + 1)]
            rate_cols.append(jnp.sum(whole, axis=-1, keepdims=True))
        for j, name in enumerate(("db2", "dg", "dgp", "dbe")):
            piece = 3 * j + p
            row = HEAD_ROW + piece // 2
            ms_ref[row : row + 1, 128 * (piece % 2) : 128 * (piece % 2) + 128] = d[name]
    lane = lax.broadcasted_iota(jnp.int32, (1, 16), 1)
    dlog = jnp.zeros((length, 16), F32)
    for i, col in enumerate(rate_cols):
        dlog = dlog + jnp.where(lane == i, col, 0.0)
    dlog = dlog * (1.0 - sg)
    ms_ref[OFFSET_ROW : OFFSET_ROW + 1, 0:16] = jnp.sum(dlog, axis=0, keepdims=True)
    dmix = [cat(x, 1) for x in parts]
    return dmix, dlog.astype(BF)


def ka_body(layer, *args):
    if layer == 0:
        dl_ref, li_ref = args[:2]
        rest = args[2:]
    else:
        dl_ref, h1_ref, fo_ref, fr_ref = args[:4]
        rest = args[4:]
    wrefs, rest = rest[:10], rest[10:]
    if layer == 1:
        lo_ref, rest = rest[0], rest[1:]
    hb_ref, x1_ref, att_ref = rest[:3]
    saves, scratch = rest[3:15], rest[15:]
    mix_v, inner_v, small_v, rate_v, out_v, sems = scratch[:6]
    pick = Pick(layer, sems)
    c_small = pick.start(wrefs[0], wrefs[1], small_v)
    c_mix = pick.start(wrefs[2], wrefs[3], mix_v)
    c_rate = pick.start(wrefs[4], wrefs[5], rate_v)
    c_inner = pick.start(wrefs[6], wrefs[7], inner_v)
    c_out = pick.start(wrefs[8], wrefs[9], out_v)
    length = hb_ref.shape[0]
    steps = length // (2 * MBT)
    begin, cut = doc_places(dl_ref, steps)
    places = block_starts(begin, steps)
    if layer == 0:
        low = gather_rows(li_ref, lax.axis_index("segment"), places)
    else:
        low = (h1_ref[...] + (fo_ref[...].astype(F32) + fr_ref[...].astype(F32))).astype(BF)
        scatter_rows(lo_ref, places, low)
        lo_ref.send()
    hb_ref[...] = low
    hb_ref.send()
    h = low.astype(F32)
    inv = rms_inv(h)
    c_small.wait()
    x_one = (h * inv * small_v[1:2, 0 : h.shape[1]]).astype(BF)
    x1_ref[...] = x_one
    x1_ref.send()
    c_mix.wait()
    c_rate.wait()
    c_inner.wait()
    forward = mixer_unrolled if layer else mixer_forward
    mixed = forward(saves, x_one, mix_v, rate_v, inner_v, small_v, (begin, cut), scratch[6:])
    c_out.wait()
    att_ref[...] = dot(mixed, out_v[...]).astype(BF)


def ffn_forward(h1, small_v, sw_v, dn_v, copies):
    width = h1.shape[1]
    inv = rms_inv(h1)
    x2 = (h1 * inv * small_v[1:2, width : 2 * width]).astype(BF)
    copies[0].wait()
    up_at = sw_v.shape[1] // 2
    gate = dot(x2, sw_v[:, :up_at])
    up = dot(x2, sw_v[:, up_at:])
    sgm = 1.0 / (1.0 + jnp.exp(-gate))
    silu = gate * sgm
    slope = up * (sgm * (1.0 + gate * (1.0 - sgm)))
    hidden = (silu * up).astype(BF)
    copies[1].wait()
    feed = dot(hidden, dn_v[...]).astype(BF)
    return x2, hidden, slope, silu, feed


def ffn_backward(dfe, slope, silu, sw_v, dn_v):
    up_at = sw_v.shape[1] // 2
    dh = dot_t(dfe, dn_v[...])
    dg, du = (dh * slope).astype(BF), (dh * silu).astype(BF)
    dx = dot_t(dg, sw_v[:, :up_at]) + dot_t(du, sw_v[:, up_at:])
    return dg, du, dx.astype(BF)


def pack_ffn(keep_ref, send_ref, x2, dg, du, hidden, dfe):
    first = lax.axis_index("segment") == 0
    width, wide = x2.shape[1], dg.shape[1]
    half = wide // 2

    def put(ref, grad, hid):
        ref[:, 0:width] = x2
        ref[:, width : width + wide] = grad
        ref[:, width + wide : width + wide + half] = hid
        ref[:, width + wide + half :] = dfe

    @pl.when(first)
    def _():
        put(keep_ref, dg, hidden[:, :half])
        put(send_ref, du, hidden[:, half:])

    @pl.when(jnp.logical_not(first))
    def _():
        put(keep_ref, du, hidden[:, half:])
        put(send_ref, dg, hidden[:, :half])


def kf_body(hb_ref, ao_ref, ar_ref, s_own, s_oth, w_own, w_oth, d_own, d_oth,
            h1_ref, x2_ref, hid_ref, sl_ref, si_ref, fe_ref, small_v, sw_v, dn_v, sems):
    pick = Pick(0, sems)
    c_small = pick.start(s_own, s_oth, small_v)
    copies = [pick.start(w_own, w_oth, sw_v), pick.start(d_own, d_oth, dn_v)]
    h1 = hb_ref[...].astype(F32) + (ao_ref[...].astype(F32) + ar_ref[...].astype(F32))
    h1_ref[...] = h1
    h1_ref.send()
    c_small.wait()
    x2, hidden, slope, silu, feed = ffn_forward(h1, small_v, sw_v, dn_v, copies)
    x2_ref[...] = x2
    hid_ref[...] = hidden
    sl_ref[...] = slope.astype(BF)
    si_ref[...] = silu.astype(BF)
    fe_ref[...] = feed


def kfb_body(dl_ref, ct_ref, hb_ref, ao_ref, ar_ref, s_own, s_oth, w_own, w_oth, d_own, d_oth,
             h1_ref, fe_ref, dxt_ref, dfe_ref, keep_ref, send_ref, small_v, sw_v, dn_v, sems):
    pick = Pick(1, sems)
    c_small = pick.start(s_own, s_oth, small_v)
    copies = [pick.start(w_own, w_oth, sw_v), pick.start(d_own, d_oth, dn_v)]
    length = hb_ref.shape[0]
    steps = length // (2 * MBT)
    begin, _ = doc_places(dl_ref, steps)
    dfe = gather_rows(ct_ref, lax.axis_index("segment"), block_starts(begin, steps))
    dfe_ref[...] = dfe
    h1 = hb_ref[...].astype(F32) + (ao_ref[...].astype(F32) + ar_ref[...].astype(F32))
    h1_ref[...] = h1
    h1_ref.send()
    c_small.wait()
    x2, hidden, slope, silu, feed = ffn_forward(h1, small_v, sw_v, dn_v, copies)
    fe_ref[...] = feed
    dg, du, dx = ffn_backward(dfe, slope, silu, sw_v, dn_v)
    dxt_ref[...] = dx
    pack_ffn(keep_ref, send_ref, x2, dg, du, hidden, dfe)


def norm_back(dx, x, gain, base):
    inv = rms_inv(x)
    e = dx * gain
    grad = base + e * inv - x * (jnp.mean(e * x, axis=-1, keepdims=True) * inv * inv * inv)
    gain_grad = jnp.sum(dx * x * inv, axis=0, keepdims=True)
    return grad, gain_grad


def kbf_body(dl_ref, hb_ref, dh_ref, xo_ref, xr_ref, t_own, t_oth, x2_ref, hid_ref, sl_ref, si_ref,
             w_own, w_oth, d_own, d_oth,
             ig_ref, gg_ref, dfe_ref, dxt_ref, keep_ref, send_ref, small_v, sw_v, dn_v, sems, sems_two):
    above = Pick(1, sems)
    c_small = above.start(t_own, t_oth, small_v)
    pick = Pick(0, sems_two)
    copies = [pick.start(d_own, d_oth, dn_v), pick.start(w_own, w_oth, sw_v)]
    length, width = hb_ref.shape
    steps = length // (2 * MBT)
    begin, _ = doc_places(dl_ref, steps)
    dx = xo_ref[...].astype(F32) + xr_ref[...].astype(F32)
    c_small.wait()
    grad, gain = norm_back(dx, hb_ref[...].astype(F32), small_v[1:2, 0:width], dh_ref[...])
    scatter_rows(ig_ref, block_starts(begin, steps), grad)
    ig_ref.send()
    gg_ref[...] = gain
    dfe = grad.astype(BF)
    dfe_ref[...] = dfe
    for c in copies:
        c.wait()
    dg, du, dxt = ffn_backward(dfe, sl_ref[...].astype(F32), si_ref[...].astype(F32), sw_v, dn_v)
    dxt_ref[...] = dxt
    pack_ffn(keep_ref, send_ref, x2_ref[...], dg, du, hid_ref[...], dfe)


def stat_rows(own, other, dp):
    zero = lax.axis_index("tensor") == 0
    low, high = jnp.where(zero, own, other), jnp.where(zero, other, own)
    line = cat([low[0:1], high[0:1], low[1:2], high[1:2], jnp.zeros((1, 64), F32)], 1)
    core = lax.axis_index("segment")
    line = cat([jnp.where(core == 0, line, 0.0), jnp.where(core == 0, 0.0, line)], 1)
    row = lax.broadcasted_iota(jnp.int32, (dp, 256), 0)
    return jnp.where(row == lax.axis_index("dp"), line, 0.0)


def kba_body(layer, dp, dl_ref, xo_ref, xr_ref, dy_ref, h1_ref, x1_ref, mixed_ref, so_ref, sr_ref, *rest):
    saves, rest = rest[:10], rest[10:]
    wrefs, rest = rest[:10], rest[10:]
    dh_ref, dxo_ref, keep_ref, send_ref, ig_ref, ms_ref, mix_v, inner_v, small_v, rate_v, out_v, sems = rest
    pick = Pick(layer, sems)
    kq, x2, g1, y2, d1, ud2, e1, sm, so, sg = saves
    c_small = pick.start(wrefs[0], wrefs[1], small_v)
    h1_ref.start()
    c_out = pick.start(wrefs[8], wrefs[9], out_v)
    c_inner = pick.start(wrefs[6], wrefs[7], inner_v)
    for ref in (so, sg, sm, kq, x2, g1, y2, e1, d1, ud2, x1_ref, mixed_ref):
        ref.start()
    c_mix = pick.start(wrefs[2], wrefs[3], mix_v)
    c_rate = pick.start(wrefs[4], wrefs[5], rate_v)
    length, width = h1_ref.shape
    steps = length // (2 * MBT)
    place = doc_places(dl_ref, steps)
    dx = xo_ref[...].astype(F32) + xr_ref[...].astype(F32)
    c_small.wait()
    dh, gain = norm_back(dx, h1_ref[...], small_v[1:2, width : 2 * width], dy_ref[...].astype(F32))
    dh_ref[...] = dh
    dh_ref.send()
    ms_ref[...] = jnp.zeros(ms_ref.shape, F32)
    at = slice(2 * layer, 2 * layer + 2)
    ms_ref[STAT_ROW : STAT_ROW + dp, :] = stat_rows(so_ref[at, :], sr_ref[at, :], dp)
    for j in range(3):
        ms_ref[GAIN_ROW + j : GAIN_ROW + j + 1, :] = gain[:, 256 * j : 256 * j + 256]
    da = dh.astype(BF)
    c_out.wait()
    c_inner.wait()
    dmixed = dot_t(da, out_v[...])
    dmix, dlog = mixer_backward(dmixed, saves, inner_v, small_v, place, ig_ref, ms_ref)
    x1 = x1_ref[...]
    drate = tdot(dlog, x1)
    heads = inner_v.shape[0] // 2
    for j in range(3):
        row = RATE_ROW + heads * j
        ms_ref[row : row + heads, :] = drate[:heads, 256 * j : 256 * j + 256]
    c_mix.wait()
    c_rate.wait()
    dxo_ref[...] = (dot_t(cat(dmix, 1), mix_v[...]) + dot(dlog, rate_v[...])).astype(BF)
    first = lax.axis_index("segment") == 0
    half = width // 2
    wide = 2 * dmix[0].shape[1]
    mixed = mixed_ref[...]

    def put(ref, one, two, att):
        ref[:, 0:width] = x1
        ref[:, width : width + wide // 2] = one
        ref[:, width + wide // 2 : width + wide] = two
        ref[:, width + wide : width + wide + mixed.shape[1]] = mixed
        ref[:, width + wide + mixed.shape[1] :] = att

    @pl.when(first)
    def _():
        put(keep_ref, dmix[0], dmix[1], da[:, :half])
        put(send_ref, dmix[2], dmix[3], da[:, half:])

    @pl.when(jnp.logical_not(first))
    def _():
        put(keep_ref, dmix[2], dmix[3], da[:, half:])
        put(send_ref, dmix[0], dmix[1], da[:, :half])


def ke_body(dl_ref, hb_ref, dh_ref, xo_ref, xr_ref, s_own, s_oth, ig_ref, gg_ref, small_v, sems):
    pick = Pick(0, sems)
    c_small = pick.start(s_own, s_oth, small_v)
    length, width = hb_ref.shape
    steps = length // (2 * MBT)
    begin, _ = doc_places(dl_ref, steps)
    dx = xo_ref[...].astype(F32) + xr_ref[...].astype(F32)
    c_small.wait()
    grad, gain = norm_back(dx, hb_ref[...].astype(F32), small_v[1:2, 0:width], dh_ref[...])
    scatter_rows(ig_ref, block_starts(begin, steps), grad)
    gg_ref[...] = gain


def beside(one, two, low, high):
    return cat([one[:, low:high], two[:, low:high]], 0)


class Columns:
    def __init__(self, dst, buf, at, sems):
        self.dst, self.buf, self.at, self.sems, self.copies = dst, buf, at, sems, []

    def send(self, low, high):
        copy = pltpu.make_async_copy(
            self.buf.at[low:high], self.dst.at[low:high, self.at : self.at + self.buf.shape[1]],
            self.sems.at[len(self.copies)],
        )
        copy.start()
        self.copies.append(copy)

    def wait(self):
        for copy in self.copies:
            copy.wait()


def grad_ffn_body(kf_ref, rf_ref, out_ref, buf, sems):
    width, wide = 768, 1024
    half = wide // 2
    out = Columns(out_ref, buf, 0, sems)
    for k in range(2):
        rows = slice(384 * k, 384 * (k + 1))
        x = beside(kf_ref, rf_ref, 384 * k, 384 * (k + 1))
        buf[rows, :] = tdot(x, beside(kf_ref, rf_ref, width, width + wide)).astype(BF)
        out.send(384 * k, 384 * (k + 1))
    down = tdot(beside(kf_ref, rf_ref, width + wide, width + wide + half),
                beside(kf_ref, rf_ref, width + wide + half, 2 * width + wide + half)).astype(BF)
    buf[768:1152, 0:width] = down[0:384]
    for k in range(3):
        buf[768 + 128 * k : 768 + 128 * (k + 1), width:wide] = down[384:512, 256 * k : 256 * (k + 1)]
    out.send(768, PACK_ROWS)
    out.wait()


def grad_mix_body(pack_ref, ka_ref, ra_ref, ik_ref, ir_ref, out_ref, buf, sems):
    width = 768
    out = Columns(out_ref, buf, 1024, sems)
    base = lax.axis_index("segment") * 384
    for k in range(2):
        rows = slice(384 * k, 384 * (k + 1))
        x = beside(ka_ref, ra_ref, 384 * k, 384 * (k + 1))
        buf[rows, :] = tdot(x, beside(ka_ref, ra_ref, width, 2 * width)).astype(BF)
        out.send(384 * k, 384 * (k + 1))
    grad = tdot(beside(ka_ref, ra_ref, 1536, 1920), beside(ka_ref, ra_ref, 1920, 2304)).astype(BF)
    buf[768:960, 0:384] = grad[0:192]
    buf[768:960, 384:768] = grad[192:384]
    for k in range(3):
        rows = pl.ds(pl.multiple_of(base + 128 * k, 128), 128)
        value = ik_ref[rows, :].astype(F32) + ir_ref[rows, :].astype(F32)
        buf[960:1088, 256 * k : 256 * (k + 1)] = value.astype(BF)
    buf[1088:PACK_ROWS, :] = jnp.zeros((PACK_ROWS - 1088, width), BF)
    out.send(768, PACK_ROWS)
    out.wait()


def final_body(turn, in_ref, sw_ref, dn_ref, mx_ref, ow_ref, ex_ref, co_ref, buf, sems):
    copies = []
    rows = PACK_ROWS // 8
    for k in range(8):
        at = rows * k
        if turn:
            at = pl.multiple_of(lax.rem(k + lax.axis_index("segment"), 8) * rows, 16)
        copies.append(pltpu.make_async_copy(in_ref.at[pl.ds(at, rows)], buf.at[rows * k : rows * (k + 1)], sems.at[k]))
    for copy in copies:
        copy.start()
    ready = 0

    def wait(upto):
        nonlocal ready
        while ready * rows < upto:
            copies[ready].wait()
            ready += 1

    for h in range(4):
        wait(192 * (h + 1))
        part = slice(192 * h, 192 * (h + 1))
        for c in range(2):
            base = 1792 * c
            sw_ref[part, c, :] = buf[part, base : base + 1024].astype(F32)
            for j in range(2):
                at = base + 1024 + 384 * j
                mx_ref[part, 2 * c + j, :] = buf[part, at : at + 384].astype(F32)
        sw_ref.send(192 * h, 192 * (h + 1))
        mx_ref.send(192 * h, 192 * (h + 1))
    wait(PACK_ROWS)
    for c in range(2):
        base = 1792 * c
        dn_ref[512 * c : 512 * c + 384, :] = buf[768:1152, base : base + 768].astype(F32)
        for k in range(3):
            part = buf[768 + 128 * k : 768 + 128 * (k + 1), base + 768 : base + 1024]
            dn_ref[512 * c + 384 : 512 * (c + 1), 256 * k : 256 * (k + 1)] = part.astype(F32)
        dn_ref.send(512 * c, 512 * (c + 1))
        base = base + 1024
        for j in range(2):
            at = base + 384 * j
            ow_ref[192 * j : 192 * (j + 1), 384 * c : 384 * (c + 1)] = buf[768:960, at : at + 384].astype(F32)
        ref = (ex_ref, co_ref)[c]
        for k in range(3):
            ref[128 * k : 128 * (k + 1), :] = buf[960:1088, base + 256 * k : base + 256 * (k + 1)].astype(F32)


class Loaded:
    def __init__(self, src, buf, sem):
        self.buf, self.shape = buf, buf.shape
        self.copy = pltpu.make_async_copy(src, buf, sem)
        self.started, self.waiting = False, True

    def start(self):
        if not self.started:
            self.copy.start()
            self.started = True

    def __getitem__(self, at):
        if self.waiting:
            self.start()
            self.copy.wait()
            self.waiting = False
        return self.buf[at]


class Stored:
    def __init__(self, dst, buf, sems):
        self.dst, self.buf, self.sems, self.shape = dst, buf, sems, buf.shape
        self.parts = []

    def __setitem__(self, at, value):
        self.buf[at] = value

    def send(self, low=None, high=None):
        k = len(self.parts)
        if low is None:
            copy = pltpu.make_async_copy(self.buf, self.dst, self.sems.at[k])
        else:
            at = slice(low, high)
            copy = pltpu.make_async_copy(self.buf.at[at], self.dst.at[at], self.sems.at[k])
        copy.start()
        self.parts.append(copy)

    def wait(self):
        for copy in self.parts:
            copy.wait()


def in_hbm(x):
    return pltpu.with_memory_space_constraint(x, pltpu.HBM)


def call(body, name, ins, specs, outs, scratch=(), deps=(), vmem=36, lazy=False):
    ins = [in_hbm(x) if spec is LOAD or spec is HBM else x for x, spec in zip(ins, specs)]
    deps = [in_hbm(x) for x in deps]
    have, extra, results, own = len(ins), len(deps), len(outs), len(scratch)
    loads = [k for k, spec in enumerate(specs) if spec is LOAD]
    stores = [k for k, out in enumerate(outs) if len(out) == 3]
    buffers = [pltpu.VMEM(ins[k].shape, ins[k].dtype) for k in loads]
    buffers += [pltpu.VMEM(outs[k][0], outs[k][1]) for k in stores]
    sems = [pltpu.SemaphoreType.DMA((max(1, len(loads)),))]
    sems += [pltpu.SemaphoreType.DMA((outs[k][2],)) for k in stores]

    def inside(*refs):
        operands, rest = list(refs[:have]), refs[have + extra :]
        written, rest = list(rest[:results]), rest[results:]
        own_refs, rest = rest[:own], rest[own:]
        bufs, (load_sems, *store_sems) = rest[: len(buffers)], rest[len(buffers) :]
        for i, k in enumerate(loads):
            operands[k] = Loaded(operands[k], bufs[i], load_sems.at[i])
            if not lazy:
                operands[k].start()
        done = []
        for i, k in enumerate(stores):
            written[k] = Stored(written[k], bufs[len(loads) + i], store_sems[i])
            done.append(written[k])
        body(*operands, *written, *own_refs)
        for one in done:
            if not one.parts:
                one.send()
        for one in done:
            one.wait()
        for k in loads:
            operands[k][0:1]

    return pl.pallas_call(
        inside,
        out_shape=[(pltpu.HBM if len(o) == 3 else jax.ShapeDtypeStruct)(o[0], o[1]) for o in outs],
        in_specs=[HBM if spec is LOAD else spec for spec in specs] + [HBM] * extra,
        out_specs=[HBM if len(o) == 3 else VMEM for o in outs],
        scratch_shapes=list(scratch) + buffers + sems,
        compiler_params=pltpu.CompilerParams(vmem_limit_bytes=vmem * 1024 * 1024),
        cost_estimate=pl.CostEstimate(flops=0, bytes_accessed=0, transcendentals=0),
        name=name,
    )(*ins, *deps)


def gate_body(*refs):
    pass


def pack_body(hb_ref, ng_ref, ro_ref, rb_ref, hg_ref, hs_ref, rw_ref, ex_ref, co_ref, small_ref, rate_ref, inner_ref):
    heads, hid, width = ex_ref.shape[0], ex_ref.shape[2], ng_ref.shape[1]
    wide = 64 * heads
    small_ref[...] = jnp.zeros(small_ref.shape, F32)
    for k in range(2):
        small_ref[1:2, width * k : width * (k + 1)] = ng_ref[k : k + 1, :]
    small_ref[3:4, 0:heads] = ro_ref[...]
    for h in range(heads):
        small_ref[0:1, hid * h : hid * (h + 1)] = hb_ref[h]
        at = slice(64 * h, 64 * (h + 1))
        small_ref[2:3, at] = rb_ref[h]
        for k in range(2):
            small_ref[2:3, wide * (k + 1) + 64 * h : wide * (k + 1) + 64 * (h + 1)] = hg_ref[h, k : k + 1, :]
        small_ref[2:3, wide * 3 + 64 * h : wide * 3 + 64 * (h + 1)] = hs_ref[h]
    rate_ref[...] = jnp.zeros(rate_ref.shape, BF)
    rate_ref[0:heads, :] = rw_ref[...]
    inner_ref[0:heads] = ex_ref[...].astype(BF)
    inner_ref[heads:] = co_ref[...].astype(BF)


def swap(value, axis):
    return lax.ppermute(value, axis, [(0, 1), (1, 0)])


def shards(
    layer_input, doc_lengths, norm_gains, mixing, rate_weight, rate_offset, expand, hidden_bias, contract,
    result_bias, head_gains, head_shift, output_proj, swiglu, down_proj, cotangent,
):
    micro, _, length, width = layer_input.shape
    heads = rate_weight.shape[2]
    hid = expand.shape[3]
    wide = heads * 64
    ff = down_proj.shape[1]
    first = lax.axis_index("segment") == 0
    dl = doc_lengths.reshape(micro, 3)
    li = layer_input.reshape(micro, length, width)
    ct = cotangent.reshape(micro, length, width)
    mix = mixing[0].reshape(width, -1)
    ow = output_proj[0]
    dn = down_proj[0]
    small, rate, inner = call(
        pack_body, "pack",
        [hidden_bias.reshape(heads, 1, hid), norm_gains[0], rate_offset, result_bias.reshape(heads, 1, 64),
         jnp.transpose(head_gains[0], (1, 0, 2)), head_shift.reshape(heads, 1, 64), rate_weight[0].T, expand[0],
         jnp.swapaxes(contract[0], 1, 2)],
        [VMEM] * 9, [((4, heads * hid), F32), ((16, width), BF), ((2 * heads, 64, hid), BF)])
    sw = swiglu[0].reshape(width, -1)

    def both(x):
        return in_hbm(x), in_hbm(swap(x, "segment"))

    small_p, mix_p, rate_p, inner_p, ow_p = both(small), both(mix), both(rate), both(inner), both(ow)
    sw = pl.pallas_call(
        gate_body, out_shape=pltpu.HBM(sw.shape, BF), in_specs=[HBM] * 6, out_specs=HBM,
        input_output_aliases={0: 0}, name="gate",
    )(sw, *[in_hbm(pair[1]) for pair in (small_p, mix_p, rate_p, inner_p, ow_p)])
    sw_p, dn_p = both(sw), both(dn)
    att_w = small_p + mix_p + rate_p + inner_p + ow_p
    tok = (length, width)
    save_shapes = [
        ((length, wide), BF, 1), ((2, 16), F32), ((length, 2 * wide), BF, 1),
        ((length, heads * hid), BF, 1), ((length, heads * hid), BF, 1), ((length, heads * hid), BF, 1),
        ((length, heads * hid), BF, 1), ((length, heads * hid), BF, 1), ((length, heads * hid), BF, 1),
        ((5, length, wide), F32, 1), ((5, length, wide), F32, 1), ((length, 16), F32, 1),
    ]
    sem = pltpu.SemaphoreType.DMA
    att_scratch = [
        pltpu.VMEM(mix.shape, BF), pltpu.VMEM(inner.shape, BF), pltpu.VMEM(small.shape, F32),
        pltpu.VMEM(rate.shape, BF), pltpu.VMEM(ow.shape, BF), sem((5,)),
    ]
    tall = (length, heads * hid)
    work = [pltpu.VMEM(tall, F32)] * 3 + [
        pltpu.VMEM((heads, length, length), BF), pltpu.VMEM((heads // 2, length, 128), BF),
        pltpu.VMEM((heads // 2, 128, 2 * hid), BF), pltpu.VMEM((length, length), F32), pltpu.VMEM((length, wide), F32),
        pltpu.VMEM((8, wide), F32),
    ]
    ffn_scratch = [pltpu.VMEM(small.shape, F32), pltpu.VMEM(sw.shape, BF), pltpu.VMEM(dn.shape, BF)]

    def ka(layer, ins):
        outs = [(tok, BF, 1), (tok, BF, 1), (tok, BF)] + save_shapes
        specs = [SMEM, LOAD] + [VMEM] * (len(ins) - 2) + [HBM] * 10
        if layer == 1:
            outs = [(tok, BF, 1)] + outs
        return call(functools.partial(ka_body, layer), f"mixer_fwd{layer}", list(ins) + list(att_w), specs, outs,
                    att_scratch + work)

    def exchange(x):
        return x, swap(x, "tensor")

    h0, x1_0, att, *save0 = ka(0, (dl, li))
    mixed0, stats0, save0 = save0[0], save0[1], save0[2:]
    ao, ar = exchange(att)
    h1_0, x2_0, hid_0, sl_0, si_0, fe = call(
        kf_body, "ffn_fwd0", [h0, ao, ar, *small_p, *sw_p, *dn_p], [LOAD] + [VMEM] * 2 + [HBM] * 6,
        [(tok, F32, 1), (tok, BF, 1)] + [((length, ff), BF, 1)] * 3 + [(tok, BF)], ffn_scratch + [sem((3,))])
    fo, fr = exchange(fe)
    lo0, hm, x1_1, att, *save1 = ka(1, (dl, h1_0, fo, fr))
    mixed1, stats1, save1 = save1[0], save1[1], save1[2:]
    ao, ar = exchange(att)
    pack_f = (length, 2 * width + ff + ff // 2)
    h1_1, fe, dxt, dfe1, keep, send = call(
        kfb_body, "ffn_both1", [dl, ct, hm, ao, ar, *small_p, *sw_p, *dn_p], [SMEM, LOAD, LOAD] + [VMEM] * 2 + [HBM] * 6,
        [(tok, F32, 1), (tok, BF), (tok, BF), (tok, BF), (pack_f, BF), (pack_f, BF)],
        ffn_scratch + [sem((3,))])

    dp = lax.axis_size("dp")
    ring = [0, 2, 4, 6, 7, 5, 3, 1] if dp == 8 else list(range(dp))

    stats = cat([stats0, stats1], 0)
    stats_in = swap(stats, "tensor")
    xo, xr = exchange(dxt)
    fo, fr = exchange(fe)
    pack_a = (length, width + 2 * wide + wide + width // 2)

    def kba(layer, xo, xr, dy, h1, x1, mixed, save, deps=()):
        return call(functools.partial(kba_body, layer, dp), f"mixer_bwd{layer}",
                    [dl, xo, xr, dy, h1, x1, mixed, stats, stats_in, *save, *att_w],
                    [SMEM] + [VMEM] * 3 + [LOAD] * 3 + [VMEM] * 2 + [LOAD] * 10 + [HBM] * 10,
                    [(tok, F32, 1), (tok, BF), (pack_a, BF), (pack_a, BF), ((2 * wide, hid), BF),
                     ((STAT_ROW + dp, hid), F32)],
                    att_scratch, deps, lazy=True)

    turn = 1 if dp == 8 else 0
    params = pltpu.CompilerParams(vmem_limit_bytes=36 * 1024 * 1024)
    pack_shape = (PACK_ROWS, ff + width)

    def grad_ffn(keep, send):
        return pl.pallas_call(
            grad_ffn_body, out_shape=pltpu.HBM(pack_shape, BF), in_specs=[VMEM] * 2, out_specs=HBM,
            scratch_shapes=[pltpu.VMEM((PACK_ROWS, ff), BF), sem((3,))], compiler_params=params, name="grad_ffn",
        )(keep, swap(send, "segment"))

    def grad_mix(pack, keep, send, ig):
        return pl.pallas_call(
            grad_mix_body, out_shape=pltpu.HBM(pack_shape, BF), in_specs=[HBM] + [VMEM] * 4, out_specs=HBM,
            scratch_shapes=[pltpu.VMEM((PACK_ROWS, width), BF), sem((3,))], compiler_params=params, name="grad_mix",
            input_output_aliases={0: 0},
        )(in_hbm(pack), keep, swap(send, "segment"), ig, swap(ig, "segment"))

    def scatter(pack, by):
        order = [ring[by:] + ring[:by]]
        return lax.psum_scatter(pack, "dp", scatter_dimension=0, axis_index_groups=order, tiled=True)

    pack1 = grad_ffn(keep, send)
    dh, dxo, keep, send, ig, misc1 = kba(1, xo, xr, dfe1, h1_1, x1_1, mixed1, save1, (pack1,))
    xo, xr = exchange(dxo)
    pack1 = grad_mix(pack1, keep, send, ig)
    part1 = scatter(pack1, turn)
    ig1, gg1, dfe0, dxt, keep, send = call(
        kbf_body, "ffn_bwd0",
        [dl, hm, dh, xo, xr, *small_p, x2_0, hid_0, sl_0, si_0, *sw_p, *dn_p],
        [SMEM, LOAD, LOAD] + [VMEM] * 2 + [HBM] * 2 + [LOAD] * 4 + [HBM] * 4,
        [(tok, F32, 1), ((1, width), F32), (tok, BF), (tok, BF), (pack_f, BF), (pack_f, BF)],
        ffn_scratch + [sem((1,)), sem((2,))], (pack1,))
    pack0 = grad_ffn(keep, send)
    xo, xr = exchange(dxt)
    after = (pack0,) if turn else (pack0, part1)
    dh, dxo, keep, send, ig, misc0 = kba(0, xo, xr, dfe0, h1_0, x1_0, mixed0, save0, after)
    xo, xr = exchange(dxo)
    pack0 = grad_mix(pack0, keep, send, ig)
    part0 = scatter(pack0, 0)
    ig0, gg0 = call(ke_body, "input_grad0", [dl, h0, dh, xo, xr, *small_p],
                    [SMEM, LOAD, LOAD] + [VMEM] * 2 + [HBM] * 2, [(tok, F32, 1), ((1, width), F32)],
                    [pltpu.VMEM(small.shape, F32), sem((1,))], (pack0,))

    left = jnp.where(first, part0, lax.ppermute(part1, "segment", [(0, 1)]))
    right = jnp.where(first, lax.ppermute(part0, "segment", [(1, 0)]), part1)
    whole = lax.all_gather(cat([left, right], 1), "dp", axis=0, axis_index_groups=[ring], tiled=True)

    def lo1_body(dl_ref, h1_ref, fo_ref, fr_ref, lo_ref):
        begin, _ = doc_places(dl_ref, length // (2 * MBT))
        low = (h1_ref[...] + (fo_ref[...].astype(F32) + fr_ref[...].astype(F32))).astype(BF)
        scatter_rows(lo_ref, block_starts(begin, length // (2 * MBT)), low)

    (lo1,) = call(lo1_body, "output1", [dl, h1_1, fo, fr], [SMEM, LOAD] + [VMEM] * 2, [(tok, BF, 1)], (), (pack0,))

    def two_rows(zero, one):
        mine, theirs = jnp.where(first, zero, one), swap(jnp.where(first, one, zero), "segment")
        return jnp.where(first, jnp.stack([mine, theirs]), jnp.stack([theirs, mine]))[None, :, None]

    layer_output = two_rows(lo0, lo1)
    input_grads = two_rows(ig0, ig1)
    total = cat([misc0, misc1, gg0.reshape(3, hid), gg1.reshape(3, hid)], 0)
    total = total + swap(total, "segment")
    for k in range(dp.bit_length() - 1):
        total = total + lax.ppermute(total, "dp", [(i, i ^ (1 << k)) for i in range(dp)])
    rows = STAT_ROW + dp
    tail = total[2 * rows :]
    misc = jnp.where(first, total[:rows], total[rows : 2 * rows])
    gain_one = jnp.where(first, tail[:3], tail[3:]).reshape(width)
    g_rate = cat([misc[RATE_ROW + heads * j : RATE_ROW + heads * (j + 1)] for j in range(3)], 1).T[None]
    g_hidden = misc[HIDDEN_ROW : HIDDEN_ROW + heads][None]
    tail = misc[HEAD_ROW : HEAD_ROW + 6].reshape(4, heads, 64)
    g_result, g_heads, g_shift = tail[0][None], tail[1:3][None], tail[3][None]
    g_offset = misc[OFFSET_ROW, :heads][None]
    g_gains = jnp.stack([gain_one, misc[GAIN_ROW : GAIN_ROW + 3].reshape(width)])[None]
    rate_stats = misc[STAT_ROW:].reshape(dp, micro, 128)[:, :, :64].reshape(dp, micro, 2, 2, 16)
    rate_stats = jnp.transpose(rate_stats[..., :heads], (1, 0, 2, 3, 4)).reshape(1, micro, dp, 2, 2 * heads)
    g_sw, g_dn, g_mix, g_out, g_expand, g_contract = call(
        functools.partial(final_body, turn), "final", [whole], [HBM],
        [((width, 2, ff), F32, 4), ((ff, width), F32, 2), ((width, 4, wide), F32, 4), ((wide, width), F32, 1),
         ((wide, hid), F32, 1), ((wide, hid), F32, 1)],
        [pltpu.VMEM(whole.shape, BF), sem((8,))], vmem=40)
    g_expand = g_expand.reshape(expand.shape)
    g_contract = jnp.swapaxes(g_contract.reshape(1, heads, 64, hid), 2, 3)
    return (
        layer_output, input_grads, g_gains, g_mix[None], g_rate, g_offset, g_expand, g_hidden, g_contract, g_result,
        g_heads, g_shift, g_out[None], g_sw[None], g_dn[None], rate_stats,
    )


def solution(mesh):
    placed = (
        P(None, "dp", None, None),
        P(None, "dp", None),
        P("segment", None, None),
        P("segment", None, None, "tensor"),
        P("segment", None, "tensor"),
        P("segment", "tensor"),
        P("segment", "tensor", None, None),
        P("segment", "tensor", None),
        P("segment", "tensor", None, None),
        P("segment", "tensor", None),
        P("segment", None, "tensor", None),
        P("segment", "tensor", None),
        P("segment", "tensor", None),
        P("segment", None, None, "tensor"),
        P("segment", "tensor", None),
        P(None, "dp", None, None),
    )
    return jax.shard_map(
        shards,
        mesh=mesh,
        in_specs=placed,
        out_specs=(
            P("segment", None, "dp", None, None),
            P("segment", None, "dp", None, None),
            P("segment", None, None),
            P("segment", None, None, "tensor"),
            P("segment", None, "tensor"),
            P("segment", "tensor"),
            P("segment", "tensor", None, None),
            P("segment", "tensor", None),
            P("segment", "tensor", None, None),
            P("segment", "tensor", None),
            P("segment", None, "tensor", None),
            P("segment", "tensor", None),
            P("segment", "tensor", None),
            P("segment", None, None, "tensor"),
            P("segment", "tensor", None),
            P("segment", None, None, None, None),
        ),
        check_vma=False,
    )
```

```python
import functools
import jax
import jax.numpy as jnp
from jax import lax
from jax.experimental import pallas as pl
from jax.experimental.pallas import tpu as pltpu
from jax.sharding import PartitionSpec as P

MBT = 16
EPS = 1e-06
RATE = 0.125
C0 = 0.7978845608028654
BF = jnp.bfloat16
F32 = jnp.float32
VMEM = pl.BlockSpec(memory_space=pltpu.VMEM)
SMEM = pl.BlockSpec(memory_space=pltpu.SMEM)
HBM = pl.BlockSpec(memory_space=pltpu.HBM)
LOAD = "load"
NRM, INV, MIS, MEANN, GZ2 = range(5)
NA, INVA, NO, INVO, GATE = range(5)
RATE_ROW, HIDDEN_ROW, HEAD_ROW, OFFSET_ROW, GAIN_ROW, STAT_ROW = 0, 18, 24, 30, 31, 40
PACK_ROWS = 1152


def dot(a, b):
    return jnp.dot(a, b, preferred_element_type=F32)


def dot_t(a, b):
    return lax.dot_general(a, b, (((1,), (1,)), ((), ())), preferred_element_type=F32)


def tdot(a, b):
    return lax.dot_general(a, b, (((0,), (0,)), ((), ())), preferred_element_type=F32)


def cat(parts, axis):
    return jnp.concatenate(parts, axis=axis)


def gelu_parts(z):
    z2 = z * z
    t = jnp.tanh(C0 * z * (1.0 + 0.044715 * z2))
    h = 0.5 * (1.0 + t)
    du = C0 * (1.0 + 0.134145 * z2)
    sech = 1.0 - t * t
    value = z * h
    slope = h + 0.5 * z * sech * du
    return value, slope, t, z2, du, sech


def gelu_two(z):
    value, slope, _, _, _, _ = gelu_parts(z)
    return value, slope


def gelu_curve(z):
    _, _, t, z2, du, sech = gelu_parts(z)
    return sech * (C0 * (1.0 + 0.26829 * z2) - z * t * du * du)


def rms_inv(values):
    return lax.rsqrt(jnp.mean(values * values, axis=-1, keepdims=True) + EPS)


class Pick:
    def __init__(self, layer, sems):
        self.own = lax.axis_index("segment") == layer
        self.sems = sems
        self.count = 0

    def start(self, own_ref, other_ref, dst):
        sem = self.sems.at[self.count]
        self.count += 1

        @pl.when(self.own)
        def _():
            pltpu.make_async_copy(own_ref, dst, sem).start()

        @pl.when(jnp.logical_not(self.own))
        def _():
            pltpu.make_async_copy(other_ref, dst, sem).start()

        return pltpu.make_async_copy(own_ref, dst, sem)


def doc_places(dl_ref, steps):
    core = lax.axis_index("segment")
    one, two = dl_ref[core, 0], dl_ref[core, 1]
    begin = jnp.where(one == steps, 0, jnp.where(two == steps, one, one + two))
    cut = jnp.where(one == steps, two, one)
    return begin, cut


def block_starts(begin, steps):
    places = []
    for s in range(steps):
        places.append(pl.multiple_of((begin + s) * MBT, MBT))
        places.append(pl.multiple_of(jnp.where(s < begin, s, s + steps) * MBT, MBT))
    return places


def gather_rows(ref, lead, places):
    return cat([ref[lead, pl.ds(p, MBT), :] for p in places], 0)


def scatter_rows(ref, places, value):
    for i, p in enumerate(places):
        ref[pl.ds(p, MBT), :] = value[i * MBT : (i + 1) * MBT, :]


def turned_mask(cut, length):
    i = lax.broadcasted_iota(jnp.int32, (length, length), 0)
    j = lax.broadcasted_iota(jnp.int32, (length, length), 1)
    si, li, sj, lj = i >> 5, (i >> 4) & 1, length // 32 - 1 - (j >> 5), (j >> 4) & 1
    di = jnp.where(li == 0, 0, jnp.where(si < cut, 1, 2))
    dj = jnp.where(lj == 0, 0, jnp.where(sj < cut, 1, 2))
    return jnp.where((di == dj) & (si < sj), 1.0 / MBT, 0.0)


def masks(cut, length):
    def parts(axis):
        i = lax.broadcasted_iota(jnp.int32, (length, length), axis)
        step, lane, t = i >> 5, (i >> 4) & 1, i & 15
        doc = jnp.where(lane == 0, 0, jnp.where(step < cut, 1, 2))
        return step, lane, t, doc

    s0, l0, t0, d0 = parts(0)
    s1, l1, t1, d1 = parts(1)
    same = d0 == d1
    block = (s0 == s1) & (l0 == l1)
    past = jnp.where(same & (s1 < s0), 1.0 / MBT, 0.0)
    past_t = jnp.where(same & (s0 < s1), 1.0 / MBT, 0.0)
    inside = jnp.where(block & (t1 <= t0), 1.0 / (t0 + 1).astype(F32), 0.0)
    inside_t = jnp.where(block & (t0 <= t1), 1.0 / (t1 + 1).astype(F32), 0.0)
    return past, past + inside, past_t, past_t + inside_t


class Halves:
    def __init__(self):
        lane = lax.broadcasted_iota(jnp.int32, (1, 128), 1)
        self.left = lane < 64
        r = lax.broadcasted_iota(jnp.int32, (256, 128), 0) & 127
        c = lax.broadcasted_iota(jnp.int32, (256, 128), 1)
        self.mean_mat = jnp.where((r < 64) == (c < 64), 1.0 / 64.0, 0.0).astype(BF)

    def mean(self, x):
        high = x.astype(BF)
        low = (x - high.astype(F32)).astype(BF)
        return dot(cat([high, low], 1), self.mean_mat)

    def split(self, x):
        zero = jnp.zeros_like(x)
        return cat([jnp.where(self.left, x, zero), jnp.where(self.left, zero, x)], 0)

    def pack(self, a, b):
        return jnp.where(self.left, a, b)

    def both(self, weights, values):
        rows = weights[0].shape[0]
        full = dot(cat(weights, 0), values)
        return self.pack(full[:rows], full[rows:])


def pair_weights(inner_ref, small_ref, heads, p, halves):
    width = inner_ref.shape[2]
    zero = jnp.zeros((64, width), BF)

    def blocks(a, b):
        return cat([cat([a, zero], 1), cat([zero, b], 1)], 0)

    def centred(index):
        w = inner_ref[heads + index].astype(F32)
        return (w - jnp.mean(w, axis=0, keepdims=True)).astype(BF)

    w1 = blocks(inner_ref[2 * p], inner_ref[2 * p + 1])
    w2 = blocks(centred(2 * p), centred(2 * p + 1))
    return w1, w2


def join(parts):
    return cat(parts, 0) if len(parts) > 1 else parts[0]


def pad_rows(parts, rows):
    have = sum(x.shape[0] for x in parts)
    if have < rows:
        parts = parts + [jnp.zeros((rows - have, parts[0].shape[1]), parts[0].dtype)]
    return cat(parts, 0) if len(parts) > 1 else parts[0]


def mixer_unrolled(refs, x_one, mix_ref, rate_ref, inner_ref, small_ref, begin_cut, x1_ready):
    (mixed_ref, stats_ref, kq_ref, x2_ref, g1_ref, y2_ref, d1_ref, ud2_ref, e1_ref, sm_ref, so_ref, sg_ref) = refs
    _, cut = begin_cut
    length = x_one.shape[0]
    heads = inner_ref.shape[0] // 2
    pairs = heads // 2
    hid = inner_ref.shape[2]
    wide = heads * 64
    steps = length // (2 * MBT)
    rows = 2 * MBT
    past, near, _, _ = masks(cut, length)
    hv = Halves()
    proj = dot(x_one, mix_ref[...])
    logits = dot_t(x_one, rate_ref[...]) + small_ref[3:4, 0:16]
    sg = jax.nn.sigmoid(logits)
    sg_ref[...] = sg
    stats_ref[...] = cat(
        [jnp.mean(sg, axis=0, keepdims=True), jnp.max(sg, axis=0, keepdims=True)], 0
    )
    rates = RATE * sg
    st = []
    for p in range(pairs):
        c = slice(128 * p, 128 * p + 128)
        h = slice(2 * hid * p, 2 * hid * (p + 1))
        q, k, v, gate = [proj[:, wide * i + 128 * p : wide * i + 128 * p + 128] for i in range(4)]
        d = dict(q=q, gate=gate, diff=v - k, c=c, h=h)
        d["w1"], d["w2"] = pair_weights(inner_ref, small_ref, heads, p, hv)
        d["b1"] = small_ref[0:1, h]
        b2 = small_ref[2:3, 128 * p : 128 * p + 128]
        d["b2"] = b2 - hv.mean(jnp.broadcast_to(b2, (8, 128)))[0:1]
        d["g"] = small_ref[2:3, wide + 128 * p : wide + 128 * p + 128]
        d["gp"] = small_ref[2:3, 2 * wide + 128 * p : 2 * wide + 128 * p + 128]
        d["be"] = small_ref[2:3, 3 * wide + 128 * p : 3 * wide + 128 * p + 128]
        d["r"] = [rates[:, 2 * p + i : 2 * p + i + 1] for i in range(2)]
        d["rp"] = hv.pack(d["r"][0], d["r"][1])
        d["kb"], d["qb"] = k.astype(BF), q.astype(BF)
        kq_ref[:, c] = d["kb"]
        kq_ref[:, wide + 128 * p : wide + 128 * p + 128] = d["qb"]
        d["base"] = dot(d["kb"], d["w1"]) + d["b1"]
        kk = dot_t(hv.split(d["kb"]), d["kb"])
        d["m1"] = [(past * (kk[i * length : (i + 1) * length] + 1.0)).astype(BF) for i in range(2)]
        for name in ("x2", "g1", "g2", "z1", "u"):
            d[name] = []
        st.append(d)
    kq_ref.send()
    sg_ref.send()
    for s in range(steps):
        sl = slice(rows * s, rows * s + rows)
        for p in range(pairs):
            d = st[p]
            c, h = d["c"], d["h"]
            z1 = d["base"][sl]
            if s:
                g1 = pad_rows(d["g1"], length)
                x2 = pad_rows(d["x2"], length)
                g2 = pad_rows(d["g2"], length)
                z1 = z1 - cat([dot(d["m1"][i][sl], g1[:, hid * i : hid * (i + 1)]) for i in range(2)], 1)
            act, slope = gelu_two(z1)
            actb = act.astype(BF)
            z2 = dot_t(actb, d["w2"]) + d["b2"]
            if s:
                far = [
                    (past[sl] * (dot_t(actb[:, hid * i : hid * (i + 1)], x2[:, hid * i : hid * (i + 1)]) + 1.0)).astype(BF)
                    for i in range(2)
                ]
                z2 = z2 - dot(cat(far, 1), hv.split(g2))
            inv = lax.rsqrt(hv.mean(z2 * z2) + EPS)
            n = z2 * inv
            mis = n * d["g"] + d["be"] - d["diff"][sl]
            misg = mis * d["g"]
            both = hv.mean(cat([misg, misg * n], 0))
            gz2 = (misg - both[:rows] - n * both[rows:]) * inv
            gz2b = gz2.astype(BF)
            u = dot(gz2b, d["w2"])
            if s:
                f = dot_t(hv.split(gz2b), g2)
                u = u - cat(
                    [
                        dot((past[sl] * f[rows * i : rows * (i + 1)]).astype(BF), x2[:, hid * i : hid * (i + 1)])
                        for i in range(2)
                    ],
                    1,
                )
            gz1 = u * slope
            r0, r1 = d["r"][0][sl], d["r"][1][sl]
            g1n = cat([gz1[:, :hid] * r0, gz1[:, hid:] * r1], 1).astype(BF)
            g2n = (gz2 * d["rp"][sl]).astype(BF)
            d["x2"].append(actb)
            d["g1"].append(g1n)
            d["g2"].append(g2n)
            d["z1"].append(z1)
            d["u"].append(u)
            x2_ref[sl, h] = actb
            g1_ref[sl, h] = g1n
            d1_ref[sl, h] = slope.astype(BF)
            sm_ref[NRM, sl, c] = n
            sm_ref[INV, sl, c] = inv
            sm_ref[MIS, sl, c] = mis
            sm_ref[MEANN, sl, c] = both[rows:]
            sm_ref[GZ2, sl, c] = gz2
    for ref in (x2_ref, g1_ref, d1_ref, sm_ref):
        ref.send()
    mixed = []
    for p in range(pairs):
        d = st[p]
        c, h = d["c"], d["h"]
        g1, x2, g2 = cat(d["g1"], 0), cat(d["x2"], 0), cat(d["g2"], 0)
        ud2_ref[:, h] = (cat(d["u"], 0) * gelu_curve(cat(d["z1"], 0))).astype(BF)
        qk = dot_t(hv.split(d["qb"]), d["kb"])
        corr = [
            dot((near * (qk[length * i : length * (i + 1)] + 1.0)).astype(BF), g1[:, hid * i : hid * (i + 1)])
            for i in range(2)
        ]
        act, slope = gelu_two(dot(d["qb"], d["w1"]) + d["b1"] - cat(corr, 1))
        actb = act.astype(BF)
        y2_ref[:, h] = actb
        e1_ref[:, h] = slope.astype(BF)
        far = [
            (near * (dot_t(actb[:, hid * i : hid * (i + 1)], x2[:, hid * i : hid * (i + 1)]) + 1.0)).astype(BF)
            for i in range(2)
        ]
        a2 = dot_t(actb, d["w2"]) + d["b2"] - dot(cat(far, 1), hv.split(g2))
        inv_a = lax.rsqrt(hv.mean(a2 * a2) + EPS)
        n_a = a2 * inv_a
        out = d["q"] + n_a * d["g"] + d["be"]
        inv_o = lax.rsqrt(hv.mean(out * out) + EPS)
        n_o = out * inv_o
        gated, _ = gelu_two(d["gate"])
        low = (gated * n_o * d["gp"]).astype(BF)
        mixed_ref[:, c] = low
        mixed.append(low)
        so_ref[NA, :, c] = n_a
        so_ref[INVA, :, c] = inv_a
        so_ref[NO, :, c] = n_o
        so_ref[INVO, :, c] = inv_o
        so_ref[GATE, :, c] = d["gate"]
    return cat(mixed, 1)


def mixer_forward(refs, x_one, mix_ref, rate_ref, inner_ref, small_ref, begin_cut, work):
    (mixed_ref, stats_ref, kq_ref, x2_ref, g1_ref, y2_ref, d1_ref, ud2_ref, e1_ref, sm_ref, so_ref, sg_ref) = refs
    base_ref, z1_ref, u_ref, m1_ref, g2_ref, w2_ref, past_ref, diff_ref, b2_ref = work
    x2_buf, g1_buf = x2_ref.buf, g1_ref.buf
    _, cut = begin_cut
    length = x_one.shape[0]
    heads = inner_ref.shape[0] // 2
    pairs = heads // 2
    hid = inner_ref.shape[2]
    wide = heads * 64
    steps = length // (2 * MBT)
    rows = 2 * MBT
    past, near, _, _ = masks(cut, length)
    past_ref[...] = past
    hv = Halves()
    proj = dot(x_one, mix_ref[...])
    logits = dot_t(x_one, rate_ref[...]) + small_ref[3:4, 0:16]
    sg = jax.nn.sigmoid(logits)
    sg_ref[...] = sg
    stats_ref[...] = cat(
        [jnp.mean(sg, axis=0, keepdims=True), jnp.max(sg, axis=0, keepdims=True)], 0
    )
    x2_buf[...] = jnp.zeros(x2_buf.shape, BF)
    g1_buf[...] = jnp.zeros(g1_buf.shape, BF)
    g2_ref[...] = jnp.zeros(g2_ref.shape, BF)

    def lanes(p):
        return slice(128 * p, 128 * p + 128), slice(2 * hid * p, 2 * hid * (p + 1))

    def row_of(k, p):
        return small_ref[2:3, wide * k + 128 * p : wide * k + 128 * p + 128]

    firsts = []
    for p in range(pairs):
        c, h = lanes(p)
        q, k, v, gate = [proj[:, wide * i + 128 * p : wide * i + 128 * p + 128] for i in range(4)]
        w1, w2_ref[p] = pair_weights(inner_ref, small_ref, heads, p, hv)
        b2 = row_of(0, p)
        b2_ref[0:1, c] = b2 - hv.mean(jnp.broadcast_to(b2, (8, 128)))[0:1]
        kb, qb = k.astype(BF), q.astype(BF)
        kq_ref[:, c] = kb
        kq_ref[:, wide + 128 * p : wide + 128 * p + 128] = qb
        diff_ref[:, c] = v - k
        so_ref[GATE, :, c] = gate
        base_ref[:, h] = dot(kb, w1) + small_ref[0:1, h]
        kk = dot_t(hv.split(kb), kb)
        for i in range(2):
            m1_ref[2 * p + i] = (past * (kk[i * length : (i + 1) * length] + 1.0)).astype(BF)
        firsts.append((q, kb, qb, w1))
    kq_ref.send()
    sg_ref.send()

    def step(s, carry, start=False):
        at = slice(s * rows, (s + 1) * rows) if isinstance(s, int) else pl.ds(pl.multiple_of(s * rows, rows), rows)
        hv = Halves()
        mask = past_ref[at, :]
        rates = RATE * sg_ref.buf[at, :]
        for p in range(pairs):
            c, h = lanes(p)

            def half(i):
                return slice(2 * hid * p + hid * i, 2 * hid * p + hid * (i + 1))

            w2, g2 = w2_ref[p], g2_ref[p]
            g = row_of(1, p)
            z1 = base_ref[at, h]
            if not start:
                z1 = z1 - cat([dot(m1_ref[2 * p + i, at, :], g1_buf[:, half(i)]) for i in range(2)], 1)
            act, slope = gelu_two(z1)
            actb = act.astype(BF)
            z2 = dot_t(actb, w2) + b2_ref[0:1, c]
            if not start:
                far = [
                    (mask * (dot_t(actb[:, hid * i : hid * (i + 1)], x2_buf[:, half(i)]) + 1.0)).astype(BF)
                    for i in range(2)
                ]
                z2 = z2 - hv.both(far, g2)
            inv = lax.rsqrt(hv.mean(z2 * z2) + EPS)
            n = z2 * inv
            mis = n * g + row_of(3, p) - diff_ref[at, c]
            misg = mis * g
            both = hv.mean(cat([misg, misg * n], 0))
            gz2 = (misg - both[:rows] - n * both[rows:]) * inv
            gz2b = gz2.astype(BF)
            u = dot(gz2b, w2)
            if not start:
                f = dot_t(hv.split(gz2b), g2)
                u = u - cat(
                    [dot((mask * f[rows * i : rows * (i + 1)]).astype(BF), x2_buf[:, half(i)]) for i in range(2)], 1
                )
            gz1 = u * slope
            r0, r1 = rates[:, 2 * p : 2 * p + 1], rates[:, 2 * p + 1 : 2 * p + 2]
            x2_buf[at, h] = actb
            g1_buf[at, h] = cat([gz1[:, :hid] * r0, gz1[:, hid:] * r1], 1).astype(BF)
            g2_ref[p, at, :] = (gz2 * hv.pack(r0, r1)).astype(BF)
            z1_ref[at, h] = z1
            u_ref[at, h] = u
            d1_ref[at, h] = slope.astype(BF)
            sm_ref[NRM, at, c] = n
            sm_ref[INV, at, c] = inv
            sm_ref[MIS, at, c] = mis
            sm_ref[MEANN, at, c] = both[rows:]
            sm_ref[GZ2, at, c] = gz2
        return carry

    step(0, 0, True)
    step(1, 0)
    lax.fori_loop(2, steps, step, 0)
    for ref in (x2_ref, g1_ref, d1_ref, sm_ref):
        ref.send()
    mixed = []
    for p in range(pairs):
        c, h = lanes(p)
        q, kb, qb, w1 = firsts[p]
        g1, x2, g2, w2 = g1_buf[:, h], x2_buf[:, h], g2_ref[p], w2_ref[p]
        ud2_ref[:, h] = (u_ref[:, h] * gelu_curve(z1_ref[:, h])).astype(BF)
        qk = dot_t(hv.split(qb), kb)
        corr = [
            dot((near * (qk[length * i : length * (i + 1)] + 1.0)).astype(BF), g1[:, hid * i : hid * (i + 1)])
            for i in range(2)
        ]
        act, slope = gelu_two(dot(qb, w1) + small_ref[0:1, h] - cat(corr, 1))
        actb = act.astype(BF)
        y2_ref[:, h] = actb
        e1_ref[:, h] = slope.astype(BF)
        far = [
            (near * (dot_t(actb[:, hid * i : hid * (i + 1)], x2[:, hid * i : hid * (i + 1)]) + 1.0)).astype(BF)
            for i in range(2)
        ]
        a2 = dot_t(actb, w2) + b2_ref[0:1, c] - hv.both(far, g2)
        inv_a = lax.rsqrt(hv.mean(a2 * a2) + EPS)
        n_a = a2 * inv_a
        out = q + n_a * row_of(1, p) + row_of(3, p)
        inv_o = lax.rsqrt(hv.mean(out * out) + EPS)
        n_o = out * inv_o
        gated, _ = gelu_two(so_ref.buf[GATE, :, c])
        low = (gated * n_o * row_of(2, p)).astype(BF)
        mixed_ref[:, c] = low
        mixed.append(low)
        so_ref[NA, :, c] = n_a
        so_ref[INVA, :, c] = inv_a
        so_ref[NO, :, c] = n_o
        so_ref[INVO, :, c] = inv_o
    return cat(mixed, 1)


def mixer_backward(dmixed, mixed_refs, inner_ref, small_ref, begin_cut, ig_ref, ms_ref):
    (kq_ref, x2_ref, g1_ref, y2_ref, d1_ref, ud2_ref, e1_ref, sm_ref, so_ref, sg_ref) = mixed_refs
    _, cut = begin_cut
    length = dmixed.shape[0]
    heads = inner_ref.shape[0] // 2
    pairs = heads // 2
    hid = inner_ref.shape[2]
    wide = heads * 64
    steps = length // (2 * MBT)
    rows = 2 * MBT
    past, near, past_t, near_t = masks(cut, length)
    hv = Halves()

    def turned(x):
        return cat([x[rows * k : rows * (k + 1)] for k in reversed(range(steps))], 0)

    past_b = turned_mask(cut, length)
    sg = sg_ref[...]
    rates = RATE * sg

    def by_head(fn):
        return [fn(slice(hid * i, hid * (i + 1)), i) for i in range(2)]

    st = []
    for p in range(pairs):
        c = slice(128 * p, 128 * p + 128)
        h = slice(2 * hid * p, 2 * hid * (p + 1))
        d = dict(c=c, h=h)
        d["w1"], d["w2"] = pair_weights(inner_ref, small_ref, heads, p, hv)
        g = small_ref[2:3, wide + 128 * p : wide + 128 * p + 128]
        gp = small_ref[2:3, 2 * wide + 128 * p : 2 * wide + 128 * p + 128]
        d["g"] = g
        d["r"] = [rates[:, 2 * p + i : 2 * p + i + 1] for i in range(2)]
        d["rp"] = hv.pack(d["r"][0], d["r"][1])
        kb = kq_ref[:, c]
        qb = kq_ref[:, wide + 128 * p : wide + 128 * p + 128]
        x2, g1, y2 = x2_ref[:, h], g1_ref[:, h], y2_ref[:, h]
        gz2 = sm_ref[GZ2, :, c]
        gz2b = gz2.astype(BF)
        g2b = (gz2 * d["rp"]).astype(BF)
        dm = dmixed[:, c]
        gate = so_ref[GATE, :, c]
        n_o, inv_o = so_ref[NO, :, c], so_ref[INVO, :, c]
        n_a, inv_a = so_ref[NA, :, c], so_ref[INVA, :, c]
        gated, gate_slope = gelu_two(gate)
        d["dgate"] = dm * n_o * gp * gate_slope
        drm = dm * gated
        d["dgp"] = jnp.sum(drm * n_o, axis=0, keepdims=True)
        dpg = drm * gp
        do = (dpg - n_o * hv.mean(dpg * n_o)) * inv_o
        dn = do * g
        both = hv.mean(cat([dn, dn * n_a], 0))
        da2 = (dn - both[:length] - n_a * both[length:]) * inv_a
        d["dg"] = jnp.sum(do * n_a, axis=0, keepdims=True)
        d["dbe"] = jnp.sum(do, axis=0, keepdims=True)
        d["db2"] = jnp.sum(da2, axis=0, keepdims=True)
        da2b = da2.astype(BF)
        da2m, g2m = hv.split(da2b), hv.split(g2b)
        km = hv.split(kb)

        def weigh(mask, full, i):
            return (mask * full[length * i : length * (i + 1)]).astype(BF)

        p2 = dot_t(da2m, g2b)
        p2t = dot_t(g2m, da2b)
        dy2 = dot(da2b, d["w2"]) - cat(by_head(lambda e, i: dot(weigh(near, p2, i), x2[:, e])), 1)
        d["bx2"] = cat(by_head(lambda e, i: dot(weigh(near_t, p2t, i), y2[:, e])), 1)
        syt = by_head(lambda e, i: (near_t * (dot_t(x2[:, e], y2[:, e]) + 1.0)).astype(BF))
        d["bg2"] = -hv.both(syt, da2b)
        da1 = dy2 * e1_ref[:, h].astype(F32)
        da1b = da1.astype(BF)
        d["db1"] = jnp.sum(da1, axis=0, keepdims=True)
        p1 = by_head(lambda e, i: (near * dot_t(da1b[:, e], g1[:, e])).astype(BF))
        p1t = by_head(lambda e, i: (near_t * dot_t(g1[:, e], da1b[:, e])).astype(BF))
        d["dq"] = do + dot_t(da1b, d["w1"]) - hv.both(p1, kb)
        d["dk"] = -hv.both(p1t, qb)
        kq = dot_t(km, qb) + 1.0
        kk = dot_t(km, turned(kb)) + 1.0
        d["bg1"] = cat(by_head(lambda e, i: dot(weigh(near_t, kq, i), da1b[:, e])), 1)
        x2r, gz2r = turned(x2), turned(gz2b)
        d["m1t"] = [weigh(past_b, kk, i) for i in range(2)]
        d["rx"] = by_head(lambda e, i: (past_b * (dot_t(x2[:, e], x2r[:, e]) + 1.0)).astype(BF))
        ft = dot_t(g2m, gz2r)
        d["ft"] = [weigh(past_b, ft, i) for i in range(2)]
        d.update(x2=x2, y2=y2, g1=g1, g2b=g2b, gz2=gz2, gz2b=gz2b, x2r=x2r, gz2r=gz2r)
        d.update(kb=kb, qb=qb, da1b=da1b, da2b=da2b)
        for name in ("z1", "z2", "u", "rg1", "rg2", "t"):
            d[name] = [None] * steps
        st.append(d)
    for s in reversed(range(steps)):
        sl = slice(rows * s, rows * s + rows)
        later = length - rows * (s + 1)
        mask = past_b[sl, :later]
        for p in range(pairs):
            d = st[p]
            c, h = d["c"], d["h"]
            x2, x2e, g2e = d["x2"], d["x2"][: rows * s], d["g2b"][: rows * s]
            bg1, bg2, bx2 = -d["bg1"][sl], d["bg2"][sl], -d["bx2"][sl]
            if s < steps - 1:

                def full(parts):
                    return join(parts[: s : -1])

                z1l, z2l, ul = full(d["z1"]), full(d["z2"]), full(d["u"])
                x2l = d["x2r"][:later]
                bg1 = bg1 - cat(by_head(lambda e, i: dot(d["m1t"][i][sl, :later], z1l[:, e])), 1)
                xu = by_head(lambda e, i: (mask * dot_t(x2[sl, e], ul[:, e])).astype(BF))
                bg2 = bg2 - hv.both([d["rx"][i][sl, :later] for i in range(2)], z2l) - hv.both(xu, d["gz2r"][:later])
                gz = dot_t(hv.split(d["g2b"][sl]), z2l)
                bx2 = bx2 - cat(
                    by_head(
                        lambda e, i: dot((mask * gz[rows * i : rows * (i + 1)]).astype(BF), x2l[:, e])
                        + dot(d["ft"][i][sl, :later], ul[:, e])
                    ),
                    1,
                )
            r0, r1 = d["r"][0][sl], d["r"][1][sl]
            dgz1 = cat([bg1[:, :hid] * r0, bg1[:, hid:] * r1], 1)
            slope = d1_ref[sl, h].astype(F32)
            du = dgz1 * slope
            dub = du.astype(BF)
            dz1 = dgz1 * ud2_ref[sl, h].astype(F32)
            dgz2 = bg2 * d["rp"][sl] + dot_t(dub, d["w2"])
            if s:
                hm = by_head(lambda e, i: (past[sl, : rows * s] * dot_t(dub[:, e], x2e[:, e])).astype(BF))
                dgz2 = dgz2 - hv.both(hm, g2e)
            n, inv = sm_ref[NRM, sl, c], sm_ref[INV, sl, c]
            mis, mn = sm_ref[MIS, sl, c], sm_ref[MEANN, sl, c]
            g = d["g"]
            e = dgz2 * inv
            three = hv.mean(cat([e, e * n, dgz2 * d["gz2"][sl]], 0))
            dmis = e - three[:rows] - n * three[rows : 2 * rows]
            t = dmis * g
            dn = t * g - e * mn - mis * g * three[rows : 2 * rows]
            two = hv.mean(cat([dn, dn * n], 0))
            dz2 = inv * (dn - two[:rows] - n * (two[rows:] + three[2 * rows :]))
            d["dg"] = d["dg"] + jnp.sum(t * n + dmis * mis, axis=0, keepdims=True)
            d["dbe"] = d["dbe"] + jnp.sum(t, axis=0, keepdims=True)
            d["db2"] = d["db2"] + jnp.sum(dz2, axis=0, keepdims=True)
            dz2b = dz2.astype(BF)
            dx2 = bx2 + dot(dz2b, d["w2"])
            if s:
                j = dot_t(hv.split(dz2b), g2e)
                dx2 = dx2 - cat(
                    by_head(
                        lambda e, i: dot((past[sl, : rows * s] * j[rows * i : rows * (i + 1)]).astype(BF), x2e[:, e])
                    ),
                    1,
                )
            dz1 = dz1 + dx2 * slope
            d["db1"] = d["db1"] + jnp.sum(dz1, axis=0, keepdims=True)
            d["z1"][s], d["z2"][s], d["u"][s] = dz1.astype(BF), dz2b, dub
            d["rg1"][s], d["rg2"][s], d["t"][s] = bg1, bg2, t
    parts = [[], [], [], []]
    rate_cols = []
    for p in range(pairs):
        d = st[p]
        z1, z2, u = cat(d["z1"], 0), cat(d["z2"], 0), cat(d["u"], 0)
        t = cat(d["t"], 0)
        g1 = d["g1"]
        both = by_head(
            lambda e, i: (past * dot_t(z1[:, e], g1[:, e]) + past_t * dot_t(g1[:, e], z1[:, e])).astype(BF)
        )
        dk = d["dk"] + t + dot_t(z1, d["w1"]) - hv.both(both, d["kb"])
        for i, value in enumerate((d["dq"], dk, -t, d["dgate"])):
            parts[i].append(value.astype(BF))
        dw1 = tdot(cat([d["kb"], d["qb"]], 0), cat([z1, d["da1b"]], 0))
        dw2 = tdot(cat([z2, d["da2b"], d["gz2b"]], 0), cat([d["x2"], d["y2"], u], 0))
        for i in range(2):
            row = 64 * (2 * p + i)
            ig_ref[row : row + 64, :] = dw1[64 * i : 64 * i + 64, hid * i : hid * (i + 1)].astype(BF)
            row = row + 64 * heads
            ig_ref[row : row + 64, :] = dw2[64 * i : 64 * i + 64, hid * i : hid * (i + 1)].astype(BF)
            row = HIDDEN_ROW + 2 * p + i
            ms_ref[row : row + 1, :] = d["db1"][:, hid * i : hid * (i + 1)]
        one = cat(d["rg1"], 0) * g1.astype(F32)
        two = cat(d["rg2"], 0) * d["g2b"].astype(F32)
        two = cat([jnp.where(hv.left, two, 0.0), jnp.where(hv.left, 0.0, two)], 1)
        for i in range(2):
            whole = one[:, hid * i : hid * i + 128] + one[:, hid * i + 128 : hid * (i + 1)]
            whole = whole + two[:, 128 * i : 128 * (i + 1)]
            rate_cols.append(jnp.sum(whole, axis=-1, keepdims=True))
        for j, name in enumerate(("db2", "dg", "dgp", "dbe")):
            piece = 3 * j + p
            row = HEAD_ROW + piece // 2
            ms_ref[row : row + 1, 128 * (piece % 2) : 128 * (piece % 2) + 128] = d[name]
    lane = lax.broadcasted_iota(jnp.int32, (1, 16), 1)
    dlog = jnp.zeros((length, 16), F32)
    for i, col in enumerate(rate_cols):
        dlog = dlog + jnp.where(lane == i, col, 0.0)
    dlog = dlog * (1.0 - sg)
    ms_ref[OFFSET_ROW : OFFSET_ROW + 1, 0:16] = jnp.sum(dlog, axis=0, keepdims=True)
    dmix = [cat(x, 1) for x in parts]
    return dmix, dlog.astype(BF)


def ka_body(layer, *args):
    if layer == 0:
        dl_ref, li_ref = args[:2]
        rest = args[2:]
    else:
        dl_ref, h1_ref, fo_ref, fr_ref = args[:4]
        rest = args[4:]
    wrefs, rest = rest[:10], rest[10:]
    if layer == 1:
        lo_ref, rest = rest[0], rest[1:]
    hb_ref, x1_ref, att_ref = rest[:3]
    saves, scratch = rest[3:15], rest[15:]
    mix_v, inner_v, small_v, rate_v, out_v, sems = scratch[:6]
    pick = Pick(layer, sems)
    c_small = pick.start(wrefs[0], wrefs[1], small_v)
    c_mix = pick.start(wrefs[2], wrefs[3], mix_v)
    c_rate = pick.start(wrefs[4], wrefs[5], rate_v)
    c_inner = pick.start(wrefs[6], wrefs[7], inner_v)
    c_out = pick.start(wrefs[8], wrefs[9], out_v)
    length = hb_ref.shape[0]
    steps = length // (2 * MBT)
    begin, cut = doc_places(dl_ref, steps)
    places = block_starts(begin, steps)
    if layer == 0:
        low = gather_rows(li_ref, lax.axis_index("segment"), places)
    else:
        low = (h1_ref[...] + (fo_ref[...].astype(F32) + fr_ref[...].astype(F32))).astype(BF)
        scatter_rows(lo_ref, places, low)
        lo_ref.send()
    hb_ref[...] = low
    hb_ref.send()
    h = low.astype(F32)
    inv = rms_inv(h)
    c_small.wait()
    x_one = (h * inv * small_v[1:2, 0 : h.shape[1]]).astype(BF)
    x1_ref[...] = x_one
    x1_ref.send()
    c_mix.wait()
    c_rate.wait()
    c_inner.wait()
    forward = mixer_unrolled if layer else mixer_forward
    mixed = forward(saves, x_one, mix_v, rate_v, inner_v, small_v, (begin, cut), scratch[6:])
    c_out.wait()
    att_ref[...] = dot(mixed, out_v[...]).astype(BF)


def ffn_forward(h1, small_v, sw_v, dn_v, copies):
    width = h1.shape[1]
    inv = rms_inv(h1)
    x2 = (h1 * inv * small_v[1:2, width : 2 * width]).astype(BF)
    copies[0].wait()
    up_at = sw_v.shape[1] // 2
    gate = dot(x2, sw_v[:, :up_at])
    up = dot(x2, sw_v[:, up_at:])
    sgm = 1.0 / (1.0 + jnp.exp(-gate))
    silu = gate * sgm
    slope = up * (sgm * (1.0 + gate * (1.0 - sgm)))
    hidden = (silu * up).astype(BF)
    copies[1].wait()
    feed = dot(hidden, dn_v[...]).astype(BF)
    return x2, hidden, slope, silu, feed


def ffn_backward(dfe, slope, silu, sw_v, dn_v):
    up_at = sw_v.shape[1] // 2
    dh = dot_t(dfe, dn_v[...])
    dg, du = (dh * slope).astype(BF), (dh * silu).astype(BF)
    dx = dot_t(dg, sw_v[:, :up_at]) + dot_t(du, sw_v[:, up_at:])
    return dg, du, dx.astype(BF)


def pack_ffn(keep_ref, send_ref, x2, dg, du, hidden, dfe):
    first = lax.axis_index("segment") == 0
    width, wide = x2.shape[1], dg.shape[1]
    half = wide // 2

    def put(ref, grad, hid):
        ref[:, 0:width] = x2
        ref[:, width : width + wide] = grad
        ref[:, width + wide : width + wide + half] = hid
        ref[:, width + wide + half :] = dfe

    @pl.when(first)
    def _():
        put(keep_ref, dg, hidden[:, :half])
        put(send_ref, du, hidden[:, half:])

    @pl.when(jnp.logical_not(first))
    def _():
        put(keep_ref, du, hidden[:, half:])
        put(send_ref, dg, hidden[:, :half])


def kf_body(hb_ref, ao_ref, ar_ref, s_own, s_oth, w_own, w_oth, d_own, d_oth,
            h1_ref, x2_ref, hid_ref, sl_ref, si_ref, fe_ref, small_v, sw_v, dn_v, sems):
    pick = Pick(0, sems)
    c_small = pick.start(s_own, s_oth, small_v)
    copies = [pick.start(w_own, w_oth, sw_v), pick.start(d_own, d_oth, dn_v)]
    h1 = hb_ref[...].astype(F32) + (ao_ref[...].astype(F32) + ar_ref[...].astype(F32))
    h1_ref[...] = h1
    h1_ref.send()
    c_small.wait()
    x2, hidden, slope, silu, feed = ffn_forward(h1, small_v, sw_v, dn_v, copies)
    x2_ref[...] = x2
    hid_ref[...] = hidden
    sl_ref[...] = slope.astype(BF)
    si_ref[...] = silu.astype(BF)
    fe_ref[...] = feed


def kfb_body(dl_ref, ct_ref, hb_ref, ao_ref, ar_ref, s_own, s_oth, w_own, w_oth, d_own, d_oth,
             h1_ref, fe_ref, dxt_ref, dfe_ref, keep_ref, send_ref, small_v, sw_v, dn_v, sems):
    pick = Pick(1, sems)
    c_small = pick.start(s_own, s_oth, small_v)
    copies = [pick.start(w_own, w_oth, sw_v), pick.start(d_own, d_oth, dn_v)]
    length = hb_ref.shape[0]
    steps = length // (2 * MBT)
    begin, _ = doc_places(dl_ref, steps)
    dfe = gather_rows(ct_ref, lax.axis_index("segment"), block_starts(begin, steps))
    dfe_ref[...] = dfe
    h1 = hb_ref[...].astype(F32) + (ao_ref[...].astype(F32) + ar_ref[...].astype(F32))
    h1_ref[...] = h1
    h1_ref.send()
    c_small.wait()
    x2, hidden, slope, silu, feed = ffn_forward(h1, small_v, sw_v, dn_v, copies)
    fe_ref[...] = feed
    dg, du, dx = ffn_backward(dfe, slope, silu, sw_v, dn_v)
    dxt_ref[...] = dx
    pack_ffn(keep_ref, send_ref, x2, dg, du, hidden, dfe)


def norm_back(dx, x, gain, base):
    inv = rms_inv(x)
    e = dx * gain
    grad = base + e * inv - x * (jnp.mean(e * x, axis=-1, keepdims=True) * inv * inv * inv)
    gain_grad = jnp.sum(dx * x * inv, axis=0, keepdims=True)
    return grad, gain_grad


def kbf_body(dl_ref, hb_ref, dh_ref, xo_ref, xr_ref, t_own, t_oth, x2_ref, hid_ref, sl_ref, si_ref,
             w_own, w_oth, d_own, d_oth,
             ig_ref, gg_ref, dfe_ref, dxt_ref, keep_ref, send_ref, small_v, sw_v, dn_v, sems, sems_two):
    above = Pick(1, sems)
    c_small = above.start(t_own, t_oth, small_v)
    pick = Pick(0, sems_two)
    copies = [pick.start(d_own, d_oth, dn_v), pick.start(w_own, w_oth, sw_v)]
    length, width = hb_ref.shape
    steps = length // (2 * MBT)
    begin, _ = doc_places(dl_ref, steps)
    dx = xo_ref[...].astype(F32) + xr_ref[...].astype(F32)
    c_small.wait()
    grad, gain = norm_back(dx, hb_ref[...].astype(F32), small_v[1:2, 0:width], dh_ref[...])
    scatter_rows(ig_ref, block_starts(begin, steps), grad)
    ig_ref.send()
    gg_ref[...] = gain
    dfe = grad.astype(BF)
    dfe_ref[...] = dfe
    for c in copies:
        c.wait()
    dg, du, dxt = ffn_backward(dfe, sl_ref[...].astype(F32), si_ref[...].astype(F32), sw_v, dn_v)
    dxt_ref[...] = dxt
    pack_ffn(keep_ref, send_ref, x2_ref[...], dg, du, hid_ref[...], dfe)


def stat_rows(own, other, dp):
    zero = lax.axis_index("tensor") == 0
    low, high = jnp.where(zero, own, other), jnp.where(zero, other, own)
    line = cat([low[0:1], high[0:1], low[1:2], high[1:2], jnp.zeros((1, 64), F32)], 1)
    core = lax.axis_index("segment")
    line = cat([jnp.where(core == 0, line, 0.0), jnp.where(core == 0, 0.0, line)], 1)
    row = lax.broadcasted_iota(jnp.int32, (dp, 256), 0)
    return jnp.where(row == lax.axis_index("dp"), line, 0.0)


def kba_body(layer, dp, dl_ref, xo_ref, xr_ref, dy_ref, h1_ref, x1_ref, mixed_ref, so_ref, sr_ref, *rest):
    saves, rest = rest[:10], rest[10:]
    wrefs, rest = rest[:10], rest[10:]
    dh_ref, dxo_ref, keep_ref, send_ref, ig_ref, ms_ref, mix_v, inner_v, small_v, rate_v, out_v, sems = rest
    pick = Pick(layer, sems)
    kq, x2, g1, y2, d1, ud2, e1, sm, so, sg = saves
    c_small = pick.start(wrefs[0], wrefs[1], small_v)
    h1_ref.start()
    c_out = pick.start(wrefs[8], wrefs[9], out_v)
    c_inner = pick.start(wrefs[6], wrefs[7], inner_v)
    for ref in (so, sg, sm, kq, x2, g1, y2, e1, d1, ud2, x1_ref, mixed_ref):
        ref.start()
    c_mix = pick.start(wrefs[2], wrefs[3], mix_v)
    c_rate = pick.start(wrefs[4], wrefs[5], rate_v)
    length, width = h1_ref.shape
    steps = length // (2 * MBT)
    place = doc_places(dl_ref, steps)
    dx = xo_ref[...].astype(F32) + xr_ref[...].astype(F32)
    c_small.wait()
    dh, gain = norm_back(dx, h1_ref[...], small_v[1:2, width : 2 * width], dy_ref[...].astype(F32))
    dh_ref[...] = dh
    dh_ref.send()
    ms_ref[...] = jnp.zeros(ms_ref.shape, F32)
    at = slice(2 * layer, 2 * layer + 2)
    ms_ref[STAT_ROW : STAT_ROW + dp, :] = stat_rows(so_ref[at, :], sr_ref[at, :], dp)
    for j in range(3):
        ms_ref[GAIN_ROW + j : GAIN_ROW + j + 1, :] = gain[:, 256 * j : 256 * j + 256]
    da = dh.astype(BF)
    c_out.wait()
    c_inner.wait()
    dmixed = dot_t(da, out_v[...])
    dmix, dlog = mixer_backward(dmixed, saves, inner_v, small_v, place, ig_ref, ms_ref)
    x1 = x1_ref[...]
    drate = tdot(dlog, x1)
    heads = inner_v.shape[0] // 2
    for j in range(3):
        row = RATE_ROW + heads * j
        ms_ref[row : row + heads, :] = drate[:heads, 256 * j : 256 * j + 256]
    c_mix.wait()
    c_rate.wait()
    dxo_ref[...] = (dot_t(cat(dmix, 1), mix_v[...]) + dot(dlog, rate_v[...])).astype(BF)
    first = lax.axis_index("segment") == 0
    half = width // 2
    wide = 2 * dmix[0].shape[1]
    mixed = mixed_ref[...]

    def put(ref, one, two, att):
        ref[:, 0:width] = x1
        ref[:, width : width + wide // 2] = one
        ref[:, width + wide // 2 : width + wide] = two
        ref[:, width + wide : width + wide + mixed.shape[1]] = mixed
        ref[:, width + wide + mixed.shape[1] :] = att

    @pl.when(first)
    def _():
        put(keep_ref, dmix[0], dmix[1], da[:, :half])
        put(send_ref, dmix[2], dmix[3], da[:, half:])

    @pl.when(jnp.logical_not(first))
    def _():
        put(keep_ref, dmix[2], dmix[3], da[:, half:])
        put(send_ref, dmix[0], dmix[1], da[:, :half])


def ke_body(dl_ref, hb_ref, dh_ref, xo_ref, xr_ref, s_own, s_oth, ig_ref, gg_ref, small_v, sems):
    pick = Pick(0, sems)
    c_small = pick.start(s_own, s_oth, small_v)
    length, width = hb_ref.shape
    steps = length // (2 * MBT)
    begin, _ = doc_places(dl_ref, steps)
    dx = xo_ref[...].astype(F32) + xr_ref[...].astype(F32)
    c_small.wait()
    grad, gain = norm_back(dx, hb_ref[...].astype(F32), small_v[1:2, 0:width], dh_ref[...])
    scatter_rows(ig_ref, block_starts(begin, steps), grad)
    gg_ref[...] = gain


def beside(one, two, low, high):
    return cat([one[:, low:high], two[:, low:high]], 0)


class Columns:
    def __init__(self, dst, buf, at, sems):
        self.dst, self.buf, self.at, self.sems, self.copies = dst, buf, at, sems, []

    def send(self, low, high):
        copy = pltpu.make_async_copy(
            self.buf.at[low:high], self.dst.at[low:high, self.at : self.at + self.buf.shape[1]],
            self.sems.at[len(self.copies)],
        )
        copy.start()
        self.copies.append(copy)

    def wait(self):
        for copy in self.copies:
            copy.wait()


def grad_ffn_body(kf_ref, rf_ref, out_ref, buf, sems):
    width, wide = 768, 1024
    half = wide // 2
    out = Columns(out_ref, buf, 0, sems)
    for k in range(2):
        rows = slice(384 * k, 384 * (k + 1))
        x = beside(kf_ref, rf_ref, 384 * k, 384 * (k + 1))
        buf[rows, :] = tdot(x, beside(kf_ref, rf_ref, width, width + wide)).astype(BF)
        out.send(384 * k, 384 * (k + 1))
    down = tdot(beside(kf_ref, rf_ref, width + wide, width + wide + half),
                beside(kf_ref, rf_ref, width + wide + half, 2 * width + wide + half)).astype(BF)
    buf[768:1152, 0:width] = down[0:384]
    for k in range(3):
        buf[768 + 128 * k : 768 + 128 * (k + 1), width:wide] = down[384:512, 256 * k : 256 * (k + 1)]
    out.send(768, PACK_ROWS)
    out.wait()


def grad_mix_body(pack_ref, ka_ref, ra_ref, ik_ref, ir_ref, out_ref, buf, sems):
    width = 768
    out = Columns(out_ref, buf, 1024, sems)
    base = lax.axis_index("segment") * 384
    for k in range(2):
        rows = slice(384 * k, 384 * (k + 1))
        x = beside(ka_ref, ra_ref, 384 * k, 384 * (k + 1))
        buf[rows, :] = tdot(x, beside(ka_ref, ra_ref, width, 2 * width)).astype(BF)
        out.send(384 * k, 384 * (k + 1))
    grad = tdot(beside(ka_ref, ra_ref, 1536, 1920), beside(ka_ref, ra_ref, 1920, 2304)).astype(BF)
    buf[768:960, 0:384] = grad[0:192]
    buf[768:960, 384:768] = grad[192:384]
    for k in range(3):
        rows = pl.ds(pl.multiple_of(base + 128 * k, 128), 128)
        value = ik_ref[rows, :].astype(F32) + ir_ref[rows, :].astype(F32)
        buf[960:1088, 256 * k : 256 * (k + 1)] = value.astype(BF)
    buf[1088:PACK_ROWS, :] = jnp.zeros((PACK_ROWS - 1088, width), BF)
    out.send(768, PACK_ROWS)
    out.wait()


def final_body(turn, in_ref, sw_ref, dn_ref, mx_ref, ow_ref, ex_ref, co_ref, buf, sems):
    copies = []
    rows = PACK_ROWS // 8
    for k in range(8):
        at = rows * k
        if turn:
            at = pl.multiple_of(lax.rem(k + lax.axis_index("segment"), 8) * rows, 16)
        copies.append(pltpu.make_async_copy(in_ref.at[pl.ds(at, rows)], buf.at[rows * k : rows * (k + 1)], sems.at[k]))
    for copy in copies:
        copy.start()
    ready = 0

    def wait(upto):
        nonlocal ready
        while ready * rows < upto:
            copies[ready].wait()
            ready += 1

    for h in range(4):
        wait(192 * (h + 1))
        part = slice(192 * h, 192 * (h + 1))
        for c in range(2):
            base = 1792 * c
            sw_ref[part, c, :] = buf[part, base : base + 1024].astype(F32)
            for j in range(2):
                at = base + 1024 + 384 * j
                mx_ref[part, 2 * c + j, :] = buf[part, at : at + 384].astype(F32)
        sw_ref.send(192 * h, 192 * (h + 1))
        mx_ref.send(192 * h, 192 * (h + 1))
    wait(PACK_ROWS)
    for c in range(2):
        base = 1792 * c
        dn_ref[512 * c : 512 * c + 384, :] = buf[768:1152, base : base + 768].astype(F32)
        for k in range(3):
            part = buf[768 + 128 * k : 768 + 128 * (k + 1), base + 768 : base + 1024]
            dn_ref[512 * c + 384 : 512 * (c + 1), 256 * k : 256 * (k + 1)] = part.astype(F32)
        dn_ref.send(512 * c, 512 * (c + 1))
        base = base + 1024
        for j in range(2):
            at = base + 384 * j
            ow_ref[192 * j : 192 * (j + 1), 384 * c : 384 * (c + 1)] = buf[768:960, at : at + 384].astype(F32)
        ref = (ex_ref, co_ref)[c]
        for k in range(3):
            ref[128 * k : 128 * (k + 1), :] = buf[960:1088, base + 256 * k : base + 256 * (k + 1)].astype(F32)


class Loaded:
    def __init__(self, src, buf, sem):
        self.buf, self.shape = buf, buf.shape
        self.copy = pltpu.make_async_copy(src, buf, sem)
        self.started, self.waiting = False, True

    def start(self):
        if not self.started:
            self.copy.start()
            self.started = True

    def __getitem__(self, at):
        if self.waiting:
            self.start()
            self.copy.wait()
            self.waiting = False
        return self.buf[at]


class Stored:
    def __init__(self, dst, buf, sems):
        self.dst, self.buf, self.sems, self.shape = dst, buf, sems, buf.shape
        self.parts = []

    def __setitem__(self, at, value):
        self.buf[at] = value

    def send(self, low=None, high=None):
        k = len(self.parts)
        if low is None:
            copy = pltpu.make_async_copy(self.buf, self.dst, self.sems.at[k])
        else:
            at = slice(low, high)
            copy = pltpu.make_async_copy(self.buf.at[at], self.dst.at[at], self.sems.at[k])
        copy.start()
        self.parts.append(copy)

    def wait(self):
        for copy in self.parts:
            copy.wait()


def in_hbm(x):
    return pltpu.with_memory_space_constraint(x, pltpu.HBM)


def call(body, name, ins, specs, outs, scratch=(), deps=(), vmem=36, lazy=False):
    ins = [in_hbm(x) if spec is LOAD or spec is HBM else x for x, spec in zip(ins, specs)]
    deps = [in_hbm(x) for x in deps]
    have, extra, results, own = len(ins), len(deps), len(outs), len(scratch)
    loads = [k for k, spec in enumerate(specs) if spec is LOAD]
    stores = [k for k, out in enumerate(outs) if len(out) == 3]
    buffers = [pltpu.VMEM(ins[k].shape, ins[k].dtype) for k in loads]
    buffers += [pltpu.VMEM(outs[k][0], outs[k][1]) for k in stores]
    sems = [pltpu.SemaphoreType.DMA((max(1, len(loads)),))]
    sems += [pltpu.SemaphoreType.DMA((outs[k][2],)) for k in stores]

    def inside(*refs):
        operands, rest = list(refs[:have]), refs[have + extra :]
        written, rest = list(rest[:results]), rest[results:]
        own_refs, rest = rest[:own], rest[own:]
        bufs, (load_sems, *store_sems) = rest[: len(buffers)], rest[len(buffers) :]
        for i, k in enumerate(loads):
            operands[k] = Loaded(operands[k], bufs[i], load_sems.at[i])
            if not lazy:
                operands[k].start()
        done = []
        for i, k in enumerate(stores):
            written[k] = Stored(written[k], bufs[len(loads) + i], store_sems[i])
            done.append(written[k])
        body(*operands, *written, *own_refs)
        for one in done:
            if not one.parts:
                one.send()
        for one in done:
            one.wait()
        for k in loads:
            operands[k][0:1]

    return pl.pallas_call(
        inside,
        out_shape=[(pltpu.HBM if len(o) == 3 else jax.ShapeDtypeStruct)(o[0], o[1]) for o in outs],
        in_specs=[HBM if spec is LOAD else spec for spec in specs] + [HBM] * extra,
        out_specs=[HBM if len(o) == 3 else VMEM for o in outs],
        scratch_shapes=list(scratch) + buffers + sems,
        compiler_params=pltpu.CompilerParams(vmem_limit_bytes=vmem * 1024 * 1024),
        cost_estimate=pl.CostEstimate(flops=0, bytes_accessed=0, transcendentals=0),
        name=name,
    )(*ins, *deps)


def gate_body(*refs):
    pass


def pack_body(hb_ref, ng_ref, ro_ref, rb_ref, hg_ref, hs_ref, rw_ref, ex_ref, co_ref, small_ref, rate_ref, inner_ref):
    heads, hid, width = ex_ref.shape[0], ex_ref.shape[2], ng_ref.shape[1]
    wide = 64 * heads
    small_ref[...] = jnp.zeros(small_ref.shape, F32)
    for k in range(2):
        small_ref[1:2, width * k : width * (k + 1)] = ng_ref[k : k + 1, :]
    small_ref[3:4, 0:heads] = ro_ref[...]
    for h in range(heads):
        small_ref[0:1, hid * h : hid * (h + 1)] = hb_ref[h]
        at = slice(64 * h, 64 * (h + 1))
        small_ref[2:3, at] = rb_ref[h]
        for k in range(2):
            small_ref[2:3, wide * (k + 1) + 64 * h : wide * (k + 1) + 64 * (h + 1)] = hg_ref[h, k : k + 1, :]
        small_ref[2:3, wide * 3 + 64 * h : wide * 3 + 64 * (h + 1)] = hs_ref[h]
    rate_ref[...] = jnp.zeros(rate_ref.shape, BF)
    rate_ref[0:heads, :] = rw_ref[...]
    inner_ref[0:heads] = ex_ref[...].astype(BF)
    inner_ref[heads:] = co_ref[...].astype(BF)


def swap(value, axis):
    return lax.ppermute(value, axis, [(0, 1), (1, 0)])


def shards(
    layer_input, doc_lengths, norm_gains, mixing, rate_weight, rate_offset, expand, hidden_bias, contract,
    result_bias, head_gains, head_shift, output_proj, swiglu, down_proj, cotangent,
):
    micro, _, length, width = layer_input.shape
    heads = rate_weight.shape[2]
    hid = expand.shape[3]
    wide = heads * 64
    ff = down_proj.shape[1]
    first = lax.axis_index("segment") == 0
    dl = doc_lengths.reshape(micro, 3)
    li = layer_input.reshape(micro, length, width)
    ct = cotangent.reshape(micro, length, width)
    mix = mixing[0].reshape(width, -1)
    ow = output_proj[0]
    dn = down_proj[0]
    small, rate, inner = call(
        pack_body, "pack",
        [hidden_bias.reshape(heads, 1, hid), norm_gains[0], rate_offset, result_bias.reshape(heads, 1, 64),
         jnp.transpose(head_gains[0], (1, 0, 2)), head_shift.reshape(heads, 1, 64), rate_weight[0].T, expand[0],
         jnp.swapaxes(contract[0], 1, 2)],
        [VMEM] * 9, [((4, heads * hid), F32), ((16, width), BF), ((2 * heads, 64, hid), BF)])
    sw = swiglu[0].reshape(width, -1)

    def both(x):
        return in_hbm(x), in_hbm(swap(x, "segment"))

    small_p, mix_p, rate_p, inner_p, ow_p = both(small), both(mix), both(rate), both(inner), both(ow)
    sw = pl.pallas_call(
        gate_body, out_shape=pltpu.HBM(sw.shape, BF), in_specs=[HBM] * 6, out_specs=HBM,
        input_output_aliases={0: 0}, name="gate",
    )(sw, *[in_hbm(pair[1]) for pair in (small_p, mix_p, rate_p, inner_p, ow_p)])
    sw_p, dn_p = both(sw), both(dn)
    att_w = small_p + mix_p + rate_p + inner_p + ow_p
    tok = (length, width)
    save_shapes = [
        ((length, wide), BF, 1), ((2, 16), F32), ((length, 2 * wide), BF, 1),
        ((length, heads * hid), BF, 1), ((length, heads * hid), BF, 1), ((length, heads * hid), BF, 1),
        ((length, heads * hid), BF, 1), ((length, heads * hid), BF, 1), ((length, heads * hid), BF, 1),
        ((5, length, wide), F32, 1), ((5, length, wide), F32, 1), ((length, 16), F32, 1),
    ]
    sem = pltpu.SemaphoreType.DMA
    att_scratch = [
        pltpu.VMEM(mix.shape, BF), pltpu.VMEM(inner.shape, BF), pltpu.VMEM(small.shape, F32),
        pltpu.VMEM(rate.shape, BF), pltpu.VMEM(ow.shape, BF), sem((5,)),
    ]
    tall = (length, heads * hid)
    work = [pltpu.VMEM(tall, F32)] * 3 + [
        pltpu.VMEM((heads, length, length), BF), pltpu.VMEM((heads // 2, length, 128), BF),
        pltpu.VMEM((heads // 2, 128, 2 * hid), BF), pltpu.VMEM((length, length), F32), pltpu.VMEM((length, wide), F32),
        pltpu.VMEM((8, wide), F32),
    ]
    ffn_scratch = [pltpu.VMEM(small.shape, F32), pltpu.VMEM(sw.shape, BF), pltpu.VMEM(dn.shape, BF)]

    def ka(layer, ins):
        outs = [(tok, BF, 1), (tok, BF, 1), (tok, BF)] + save_shapes
        specs = [SMEM, LOAD] + [VMEM] * (len(ins) - 2) + [HBM] * 10
        if layer == 1:
            outs = [(tok, BF, 1)] + outs
        return call(functools.partial(ka_body, layer), f"mixer_fwd{layer}", list(ins) + list(att_w), specs, outs,
                    att_scratch + work)

    def exchange(x):
        return x, swap(x, "tensor")

    h0, x1_0, att, *save0 = ka(0, (dl, li))
    mixed0, stats0, save0 = save0[0], save0[1], save0[2:]
    ao, ar = exchange(att)
    h1_0, x2_0, hid_0, sl_0, si_0, fe = call(
        kf_body, "ffn_fwd0", [h0, ao, ar, *small_p, *sw_p, *dn_p], [LOAD] + [VMEM] * 2 + [HBM] * 6,
        [(tok, F32, 1), (tok, BF, 1)] + [((length, ff), BF, 1)] * 3 + [(tok, BF)], ffn_scratch + [sem((3,))])
    fo, fr = exchange(fe)
    lo0, hm, x1_1, att, *save1 = ka(1, (dl, h1_0, fo, fr))
    mixed1, stats1, save1 = save1[0], save1[1], save1[2:]
    ao, ar = exchange(att)
    pack_f = (length, 2 * width + ff + ff // 2)
    h1_1, fe, dxt, dfe1, keep, send = call(
        kfb_body, "ffn_both1", [dl, ct, hm, ao, ar, *small_p, *sw_p, *dn_p], [SMEM, LOAD, LOAD] + [VMEM] * 2 + [HBM] * 6,
        [(tok, F32, 1), (tok, BF), (tok, BF), (tok, BF), (pack_f, BF), (pack_f, BF)],
        ffn_scratch + [sem((3,))])

    dp = lax.axis_size("dp")
    ring = [0, 2, 4, 6, 7, 5, 3, 1] if dp == 8 else list(range(dp))

    stats = cat([stats0, stats1], 0)
    stats_in = swap(stats, "tensor")
    xo, xr = exchange(dxt)
    fo, fr = exchange(fe)
    pack_a = (length, width + 2 * wide + wide + width // 2)

    def kba(layer, xo, xr, dy, h1, x1, mixed, save, deps=()):
        return call(functools.partial(kba_body, layer, dp), f"mixer_bwd{layer}",
                    [dl, xo, xr, dy, h1, x1, mixed, stats, stats_in, *save, *att_w],
                    [SMEM] + [VMEM] * 3 + [LOAD] * 3 + [VMEM] * 2 + [LOAD] * 10 + [HBM] * 10,
                    [(tok, F32, 1), (tok, BF), (pack_a, BF), (pack_a, BF), ((2 * wide, hid), BF),
                     ((STAT_ROW + dp, hid), F32)],
                    att_scratch, deps, lazy=True)

    turn = 1 if dp == 8 else 0
    params = pltpu.CompilerParams(vmem_limit_bytes=36 * 1024 * 1024)
    pack_shape = (PACK_ROWS, ff + width)

    def grad_ffn(keep, send):
        return pl.pallas_call(
            grad_ffn_body, out_shape=pltpu.HBM(pack_shape, BF), in_specs=[VMEM] * 2, out_specs=HBM,
            scratch_shapes=[pltpu.VMEM((PACK_ROWS, ff), BF), sem((3,))], compiler_params=params, name="grad_ffn",
        )(keep, swap(send, "segment"))

    def grad_mix(pack, keep, send, ig):
        return pl.pallas_call(
            grad_mix_body, out_shape=pltpu.HBM(pack_shape, BF), in_specs=[HBM] + [VMEM] * 4, out_specs=HBM,
            scratch_shapes=[pltpu.VMEM((PACK_ROWS, width), BF), sem((3,))], compiler_params=params, name="grad_mix",
            input_output_aliases={0: 0},
        )(in_hbm(pack), keep, swap(send, "segment"), ig, swap(ig, "segment"))

    def scatter(pack, by):
        order = [ring[by:] + ring[:by]]
        return lax.psum_scatter(pack, "dp", scatter_dimension=0, axis_index_groups=order, tiled=True)

    pack1 = grad_ffn(keep, send)
    dh, dxo, keep, send, ig, misc1 = kba(1, xo, xr, dfe1, h1_1, x1_1, mixed1, save1, (pack1,))
    xo, xr = exchange(dxo)
    pack1 = grad_mix(pack1, keep, send, ig)
    part1 = scatter(pack1, turn)
    ig1, gg1, dfe0, dxt, keep, send = call(
        kbf_body, "ffn_bwd0",
        [dl, hm, dh, xo, xr, *small_p, x2_0, hid_0, sl_0, si_0, *sw_p, *dn_p],
        [SMEM, LOAD, LOAD] + [VMEM] * 2 + [HBM] * 2 + [LOAD] * 4 + [HBM] * 4,
        [(tok, F32, 1), ((1, width), F32), (tok, BF), (tok, BF), (pack_f, BF), (pack_f, BF)],
        ffn_scratch + [sem((1,)), sem((2,))], (pack1,))
    pack0 = grad_ffn(keep, send)
    xo, xr = exchange(dxt)
    after = (pack0,) if turn else (pack0, part1)
    dh, dxo, keep, send, ig, misc0 = kba(0, xo, xr, dfe0, h1_0, x1_0, mixed0, save0, after)
    xo, xr = exchange(dxo)
    pack0 = grad_mix(pack0, keep, send, ig)
    part0 = scatter(pack0, 0)
    ig0, gg0 = call(ke_body, "input_grad0", [dl, h0, dh, xo, xr, *small_p],
                    [SMEM, LOAD, LOAD] + [VMEM] * 2 + [HBM] * 2, [(tok, F32, 1), ((1, width), F32)],
                    [pltpu.VMEM(small.shape, F32), sem((1,))], (pack0,))

    left = jnp.where(first, part0, lax.ppermute(part1, "segment", [(0, 1)]))
    right = jnp.where(first, lax.ppermute(part0, "segment", [(1, 0)]), part1)
    whole = lax.all_gather(cat([left, right], 1), "dp", axis=0, axis_index_groups=[ring], tiled=True)

    def lo1_body(dl_ref, h1_ref, fo_ref, fr_ref, lo_ref):
        begin, _ = doc_places(dl_ref, length // (2 * MBT))
        low = (h1_ref[...] + (fo_ref[...].astype(F32) + fr_ref[...].astype(F32))).astype(BF)
        scatter_rows(lo_ref, block_starts(begin, length // (2 * MBT)), low)

    (lo1,) = call(lo1_body, "output1", [dl, h1_1, fo, fr], [SMEM, LOAD] + [VMEM] * 2, [(tok, BF, 1)], (), (pack0,))

    def two_rows(zero, one):
        mine, theirs = jnp.where(first, zero, one), swap(jnp.where(first, one, zero), "segment")
        return jnp.where(first, jnp.stack([mine, theirs]), jnp.stack([theirs, mine]))[None, :, None]

    layer_output = two_rows(lo0, lo1)
    input_grads = two_rows(ig0, ig1)
    total = cat([misc0, misc1, gg0.reshape(3, hid), gg1.reshape(3, hid)], 0)
    total = total + swap(total, "segment")
    for k in range(dp.bit_length() - 1):
        total = total + lax.ppermute(total, "dp", [(i, i ^ (1 << k)) for i in range(dp)])
    rows = STAT_ROW + dp
    tail = total[2 * rows :]
    misc = jnp.where(first, total[:rows], total[rows : 2 * rows])
    gain_one = jnp.where(first, tail[:3], tail[3:]).reshape(width)
    g_rate = cat([misc[RATE_ROW + heads * j : RATE_ROW + heads * (j + 1)] for j in range(3)], 1).T[None]
    g_hidden = misc[HIDDEN_ROW : HIDDEN_ROW + heads][None]
    tail = misc[HEAD_ROW : HEAD_ROW + 6].reshape(4, heads, 64)
    g_result, g_heads, g_shift = tail[0][None], tail[1:3][None], tail[3][None]
    g_offset = misc[OFFSET_ROW, :heads][None]
    g_gains = jnp.stack([gain_one, misc[GAIN_ROW : GAIN_ROW + 3].reshape(width)])[None]
    rate_stats = misc[STAT_ROW:].reshape(dp, micro, 128)[:, :, :64].reshape(dp, micro, 2, 2, 16)
    rate_stats = jnp.transpose(rate_stats[..., :heads], (1, 0, 2, 3, 4)).reshape(1, micro, dp, 2, 2 * heads)
    g_sw, g_dn, g_mix, g_out, g_expand, g_contract = call(
        functools.partial(final_body, turn), "final", [whole], [HBM],
        [((width, 2, ff), F32, 4), ((ff, width), F32, 2), ((width, 4, wide), F32, 4), ((wide, width), F32, 1),
         ((wide, hid), F32, 1), ((wide, hid), F32, 1)],
        [pltpu.VMEM(whole.shape, BF), sem((8,))], vmem=40)
    g_expand = g_expand.reshape(expand.shape)
    g_contract = jnp.swapaxes(g_contract.reshape(1, heads, 64, hid), 2, 3)
    return (
        layer_output, input_grads, g_gains, g_mix[None], g_rate, g_offset, g_expand, g_hidden, g_contract, g_result,
        g_heads, g_shift, g_out[None], g_sw[None], g_dn[None], rate_stats,
    )


def solution(mesh):
    placed = (
        P(None, "dp", None, None),
        P(None, "dp", None),
        P("segment", None, None),
        P("segment", None, None, "tensor"),
        P("segment", None, "tensor"),
        P("segment", "tensor"),
        P("segment", "tensor", None, None),
        P("segment", "tensor", None),
        P("segment", "tensor", None, None),
        P("segment", "tensor", None),
        P("segment", None, "tensor", None),
        P("segment", "tensor", None),
        P("segment", "tensor", None),
        P("segment", None, None, "tensor"),
        P("segment", "tensor", None),
        P(None, "dp", None, None),
    )
    return jax.shard_map(
        shards,
        mesh=mesh,
        in_specs=placed,
        out_specs=(
            P("segment", None, "dp", None, None),
            P("segment", None, "dp", None, None),
            P("segment", None, None),
            P("segment", None, None, "tensor"),
            P("segment", None, "tensor"),
            P("segment", "tensor"),
            P("segment", "tensor", None, None),
            P("segment", "tensor", None),
            P("segment", "tensor", None, None),
            P("segment", "tensor", None),
            P("segment", None, "tensor", None),
            P("segment", "tensor", None),
            P("segment", "tensor", None),
            P("segment", None, None, "tensor"),
            P("segment", "tensor", None),
            P("segment", None, None, None, None),
        ),
        check_vma=False,
    )
```
